256 devices in a mesh: expert: 32 (over x, z), tensor: 4 (over y), dp: 2 (over core).
Axes of the slice: x: 4, y: 4, z: 8, core: 2. Of those that a mesh axis runs over, the one named last changes fastest.
Arguments:
- tokens: bfloat16 [32768, 5120], P(('dp', 'expert', 'tensor')), parts along dimension 0, may hold values from -6 to 6
- out_grad: bfloat16 [32768, 5120], P(('dp', 'expert', 'tensor')), parts along dimension 0, may hold values from -1.5 to 1.5
- gate: float32 [32768], P(('dp', 'expert', 'tensor')), parts along dimension 0, may hold values from 0.25 to 2
- route: int32 [32768, 1], P(('dp', 'expert', 'tensor')), parts along dimension 0, may hold values from 0 to 32; in each aligned block of 128 rows (0 to 127, 128 to 255, ...) at most 6 rows name the same one
- gate_weight: bfloat16 [32, 5120, 1024], P('expert', None, 'tensor'), may hold values from -0.078125 to 0.078125
- up_weight: bfloat16 [32, 5120, 1024], P('expert', None, 'tensor'), may hold values from -0.078125 to 0.078125
- down_weight: bfloat16 [32, 1024, 5120], P('expert', 'tensor'), may hold values from -0.1875 to 0.1875
Outputs:
- token_grad: bfloat16 [32768, 5120], P(('dp', 'expert', 'tensor')), parts along dimension 0
- gate_grad: bfloat16 [32768], P(('dp', 'expert', 'tensor')), parts along dimension 0
The draws below stay inside these ranges and needn't reach their ends.
There are 2 independent parts, one for each index of `dp`. The reference program is written for one: setup_inputs(seed, part) draws one part's arguments, and reference() takes and returns one part's arrays. A program takes and returns all parts, laid end to end along the dimension named above; an argument that names none is the same for every part. Nothing has to cross between parts.
Inputs may be any that keep to these rules, and one draw needn't show every extreme that they name: `route`: id 32 is the no-op expert. Among the 128 rows of one device (aligned blocks), no id is named by more than 6 rows, a bound that some block reaches.
All inputs are finite; a program needn't handle non-finite values.
Results may differ from the reference program's by a relative error of at most 0.019.
Values may be sent and summed in bfloat16 or wider, within the bound.
No kernel may reach another device: no remote copies, remote signals or barrier semaphores. Data moves between devices by JAX's collectives and lax.ppermute only.
A program may use at most 128 MiB of HBM per device.

```python
import math
import jax
import jax.numpy as jnp
import numpy as np
from jax import lax

D = 5120
FF = 1024
TOK_DEV = 128
EXPERTS = 32
CAP = 6
TOKENS = 16384
N_EXPERT = 32
N_TENSOR = 4


def block_levels(rng, shape, split, smallest, top_value):
    loudness = 1.0
    for dim, blocks in split:
        steps = jax.random.uniform(jax.random.fold_in(jax.random.fold_in(rng, 6), dim), (blocks,), jnp.float32, smallest / len(split), top_value / len(split))
        loudness = loudness * jnp.repeat(jnp.exp(steps), shape[dim] // blocks).reshape((-1,) + (1,) * (len(shape) - 1 - dim))
    return loudness


def assign_block(stream_key, own, number, rows, count, top, limit, skew):
    sequence = jax.random.permutation(stream_key, count)
    crowded, usual = portions_of(count, rows * top, limit, skew, True), portions_of(count, rows * top, limit, skew, False)
    places = jnp.arange(count)

    def named(lengths, turn):
        used = int((lengths > 0).sum())
        fixed = max(1, used // 4)
        moved = fixed + (places - fixed + turn * (used - fixed)) % max(1, count - fixed)
        return jnp.zeros((count,), jnp.int32).at[sequence[jnp.where(places < fixed, places, moved)]].set(jnp.asarray(lengths, jnp.int32))

    lengths = jnp.where(number % 4 == 0, named(crowded, number // 4), named(usual, number - number // 4 - 1))
    mixed = jax.random.permutation(jax.random.fold_in(own, 3), count)
    donor, taker = mixed[0:count // 2 * 2:2], mixed[1:count // 2 * 2:2]
    room = jnp.minimum(lengths[donor] - 1, limit - lengths[taker]) // 2
    room = jnp.where((donor == sequence[0]) | (taker == sequence[0]) | (lengths[taker] == 0), 0, jnp.maximum(room, 0))
    moved = jax.random.randint(jax.random.fold_in(own, 4), (count // 2,), 0, 1 << 20) % (room + 1)
    lengths = lengths.at[donor].add(-moved).at[taker].add(moved)
    labels = jnp.searchsorted(jnp.cumsum(lengths), jnp.arange(rows * top), side="right").astype(jnp.int32)
    grid = labels.reshape(top, rows).T
    grid = grid[jax.random.permutation(jax.random.fold_in(own, 1), rows)]
    turn = jax.random.randint(jax.random.fold_in(own, 2), (rows, 1), 0, top)
    return jnp.take_along_axis(grid, (jnp.arange(top)[None, :] + turn) % top, axis=1)


def portions_of(amount, total, bound, skew, full):
    weights = [(1 << 20) // math.isqrt(rank ** skew) + 1 for rank in range(1, amount + 1)]
    largest = bound if full else min(bound, max(-(-total // amount), total * weights[0] // sum(weights)))
    least = 1 if total - largest >= amount - 1 else 0
    given, rest = [largest] + [least] * (amount - 1), total - largest - least * (amount - 1)
    while rest > 0:
        free = [i for i in range(1, amount) if given[i] < largest] or [i for i in range(1, amount) if given[i] < bound]
        pool, remaining = sum([weights[i] for i in free]), rest
        for i in free:
            extra = min(bound - given[i], max(1, remaining * weights[i] // pool), rest)
            given[i] = given[i] + extra
            rest = rest - extra
    return np.array(given)


def gaussian(key, extent, scale, most, pieces=(), kind=jnp.bfloat16):
    entries = jax.random.normal(key, extent, jnp.float32) * scale
    if len(pieces) > 0:
        entries = block_levels(key, extent, pieces, -0.22, 0.18) * entries
    return jnp.clip(entries, min=-most, max=most).astype(kind)


def setup_inputs(seed: int = 0, part: int = 0) -> dict:
    arg_keys = jax.random.split(jax.random.key(seed), 8)
    part_keys = jax.random.split(jax.random.fold_in(arg_keys[7], part), 8)
    tokens = gaussian(part_keys[0], (TOKENS, D), 1.0, 6.0, ((0, 128),))
    out_grad = gaussian(part_keys[1], (TOKENS, D), 0.25, 1.5, ((0, 128),))
    gate = jnp.clip(jnp.exp(math.log(2.0) - 2.0794415 * jax.random.uniform(part_keys[2], (TOKENS,), jnp.float32) ** block_levels(part_keys[2], (TOKENS,), ((0, 128),), -0.2, 0.2)), 0.25, 2.0)
    route_keys = jax.random.split(jax.random.fold_in(part_keys[3], 1), TOKENS // TOK_DEV)
    route_turns = jax.random.permutation(jax.random.fold_in(part_keys[3], 3), TOKENS // TOK_DEV)
    route = jax.vmap(lambda own, number: assign_block(jax.random.fold_in(part_keys[3], 2), own, number, TOK_DEV, EXPERTS + 1, 1, CAP, 2))(route_keys, route_turns).reshape((TOKENS, 1))
    gate_weight = gaussian(arg_keys[4], (EXPERTS, D, FF), D ** -0.5, 0.078125, ((0, 32), (2, 4)))
    up_weight = gaussian(arg_keys[5], (EXPERTS, D, FF), D ** -0.5, 0.078125, ((0, 32), (2, 4)))
    down_weight = gaussian(arg_keys[6], (EXPERTS, FF, D), FF ** -0.5, 0.1875, ((0, 32), (1, 4)))
    return {"tokens": tokens, "out_grad": out_grad, "gate": gate, "route": route, "gate_weight": gate_weight, "up_weight": up_weight, "down_weight": down_weight}


def silu_parts(value):
    sigmoid_value = jax.nn.sigmoid(value)
    return value * sigmoid_value, sigmoid_value * (1.0 + value * (1.0 - sigmoid_value))


def expert_grads(rows_x, rows_dy, w_gate, w_up, w_down):
    pre_gate = jnp.dot(rows_x, w_gate, preferred_element_type=jnp.float32)
    pre_up = jnp.dot(rows_x, w_up, preferred_element_type=jnp.float32)
    back_hidden = lax.dot_general(rows_dy, w_down, (((1,), (1,)), ((), ())), preferred_element_type=jnp.float32)
    activated, slope = silu_parts(pre_gate)
    gate_term = jnp.sum(activated * pre_up * back_hidden, axis=-1)
    grad_gate = (back_hidden * pre_up * slope).astype(jnp.bfloat16)
    grad_up = (back_hidden * activated).astype(jnp.bfloat16)
    grad_rows = lax.dot_general(grad_gate, w_gate, (((1,), (1,)), ((), ())), preferred_element_type=jnp.float32)
    grad_rows = grad_rows + lax.dot_general(grad_up, w_up, (((1,), (1,)), ((), ())), preferred_element_type=jnp.float32)
    return grad_rows, gate_term


def blocked_grads(rows_x, rows_dy, w_gate, w_up, w_down, blocks):
    span = w_gate.shape[1] // blocks
    total_rows = jnp.zeros((rows_x.shape[0], rows_x.shape[1]), jnp.float32)
    total_terms = jnp.zeros((rows_x.shape[0],), jnp.float32)
    for block in range(blocks):
        low = block * span
        rows, terms = expert_grads(rows_x, rows_dy, w_gate[:, low:low + span], w_up[:, low:low + span], w_down[low:low + span, :])
        total_rows = total_rows + rows.astype(jnp.bfloat16).astype(jnp.float32)
        total_terms = total_terms + terms.astype(jnp.bfloat16).astype(jnp.float32)
    return total_rows, total_terms


def reference(tokens, out_grad, gate, route, gate_weight, up_weight, down_weight):
    total, width = tokens.shape
    experts = gate_weight.shape[0]
    expert_id = route[:, 0].astype(jnp.int32)
    row_limit = N_EXPERT * N_TENSOR * CAP
    padded_tokens = jnp.concatenate([tokens, jnp.zeros((1, width), jnp.bfloat16)], 0)
    padded_grads = jnp.concatenate([out_grad, jnp.zeros((1, width), jnp.bfloat16)], 0)

    def visit(carry, expert):
        rows_acc, term_acc = carry
        index = jnp.nonzero(expert_id == expert, size=row_limit, fill_value=total)[0].astype(jnp.int32)
        rows, terms = blocked_grads(padded_tokens[index], padded_grads[index], gate_weight[expert], up_weight[expert], down_weight[expert], N_TENSOR)
        rows_acc = rows_acc.at[index].set(rows.astype(jnp.bfloat16))
        term_acc = term_acc.at[index].set(terms.astype(jnp.bfloat16))
        return (rows_acc, term_acc), None

    start = (jnp.zeros((total + 1, width), jnp.bfloat16), jnp.zeros((total + 1,), jnp.bfloat16))
    (rows_acc, term_acc), _ = lax.scan(visit, start, jnp.arange(experts, dtype=jnp.int32))
    routed = expert_id < experts
    own_term = jnp.sum(out_grad.astype(jnp.float32) * tokens.astype(jnp.float32), axis=1)
    token_grad = jnp.where(routed[:, None], gate[:, None] * rows_acc[:total].astype(jnp.float32), gate[:, None] * out_grad.astype(jnp.float32)).astype(jnp.bfloat16)
    gate_grad = jnp.where(routed, term_acc[:total].astype(jnp.float32), own_term).astype(jnp.bfloat16)
    return token_grad, gate_grad
```

```python
import jax
import jax.numpy as jnp
from jax import lax
from jax.experimental import pallas as pl
from jax.experimental.pallas import tpu as pltpu
from jax.sharding import PartitionSpec as P

BF = jnp.bfloat16
F32 = jnp.float32
CAP = 6
ROWS = 8
TERM_LANES = 128
VMEM_LIMIT = 56 * 1024 * 1024


def dot(a, b):
    return jnp.dot(a, b, preferred_element_type=F32)


def dot_t(a, b):
    return lax.dot_general(a, b, (((1,), (1,)), ((), ())), preferred_element_type=F32)


def eye(n):
    return lax.broadcasted_iota(jnp.int32, (n, n), 0) == lax.broadcasted_iota(jnp.int32, (n, n), 1)


def to_column(row):
    n = row.shape[1]
    return jnp.sum(jnp.where(eye(n), jnp.broadcast_to(row, (n, n)), 0), axis=1, keepdims=True)


def to_row(column):
    n = column.shape[0]
    return jnp.sum(jnp.where(eye(n), jnp.broadcast_to(column, (n, n)), 0), axis=0, keepdims=True)


def places(route_row):
    n = route_row.shape[1]
    across = jnp.broadcast_to(route_row, (n, n))
    down = jnp.broadcast_to(to_column(route_row), (n, n))
    earlier = lax.broadcasted_iota(jnp.int32, (n, n), 0) < lax.broadcasted_iota(jnp.int32, (n, n), 1)
    slot = jnp.sum(jnp.where((across == down) & earlier, 1, 0), axis=0, keepdims=True)
    second = jnp.where(slot >= 3, 1, 0)
    base = route_row * ROWS
    return base + slot, base + CAP + second, slot - 3 * second


def pack_kernel(route_ref, rows_ref, out_ref):
    n, width = rows_ref.shape
    total = out_ref.shape[0]
    part = width // 4
    main, tail, block = places(route_ref[...])
    row = lax.broadcasted_iota(jnp.int32, (total, n), 0)
    select = jnp.where(row == main, 1.0, 0.0).astype(BF)
    last = rows_ref[:, 3 * part :]
    for j in range(3):
        tail_select = jnp.where((row == tail) & (block == j), 1.0, 0.0).astype(BF)
        cols = pl.ds(j * part, part)
        out_ref[:, cols] = (dot(select, rows_ref[:, cols]) + dot(tail_select, last)).astype(BF)


def pack(route_row, rows, experts):
    n, width = rows.shape
    return pl.pallas_call(
        pack_kernel,
        out_shape=jax.ShapeDtypeStruct((experts * ROWS, width // 4 * 3), BF),
        compiler_params=pltpu.CompilerParams(vmem_limit_bytes=VMEM_LIMIT),
        cost_estimate=pl.CostEstimate(
            flops=2 * experts * ROWS * n * width * 3 // 2,
            bytes_accessed=2 * width * (n + experts * CAP),
            transcendentals=0,
        ),
        name="pack",
    )(route_row, rows)


def slot_matrix(slots, packed, slot_dim, tail):
    shape = (slots, packed) if slot_dim == 0 else (packed, slots)
    slot = lax.broadcasted_iota(jnp.int32, shape, slot_dim)
    row = lax.broadcasted_iota(jnp.int32, shape, 1 - slot_dim)
    group, place = row >> 3, row & 7
    if tail is None:
        hit = (slot == group * CAP + place) & (place < CAP)
    else:
        hit = (slot == group * CAP + (place - CAP) * 3 + tail) & (place >= CAP)
    return jnp.where(hit, 1.0, 0.0).astype(BF)


def expert_kernel(
    xo_hbm, xt_hbm, dyo_hbm, dyt_hbm, wgu_hbm, wdn_hbm,
    own_ref, other_ref,
    x_raw, dy_raw, x, dy, wgu, wdn, grads, term, sems,
):
    packed, main_width = x_raw.shape[1:]
    blocks, width, both = wgu.shape
    hidden = both // 2
    slots = x.shape[0] // 2
    part = width // 4
    x_copies = [
        pltpu.make_async_copy(src, x_raw.at[i], sems.at[i]) for i, src in enumerate((xo_hbm, xt_hbm))
    ]
    dy_copies = [
        pltpu.make_async_copy(src, dy_raw.at[i], sems.at[2 + i]) for i, src in enumerate((dyo_hbm, dyt_hbm))
    ]
    wgu_copies = [
        pltpu.make_async_copy(wgu_hbm.at[i], wgu.at[i], sems.at[4 + i]) for i in range(blocks)
    ]
    wdn_copy = pltpu.make_async_copy(wdn_hbm, wdn, sems.at[4 + blocks])
    for copy in x_copies + dy_copies + [wdn_copy] + wgu_copies:
        copy.start()
    spread = slot_matrix(slots, packed, 0, None)
    spread_tail = [slot_matrix(slots, packed, 0, j) for j in range(3)]

    def unpack(raw, copies, full):
        for i in range(2):
            copies[i].wait()
            low = i * slots
            for j in range(3):
                full[low : low + slots, j * part : (j + 1) * part] = dot(
                    spread, raw[i, :, j * part : (j + 1) * part]
                ).astype(BF)
            last = dot(spread_tail[0], raw[i, :, :part])
            last += dot(spread_tail[1], raw[i, :, part : 2 * part])
            last += dot(spread_tail[2], raw[i, :, 2 * part :])
            full[low : low + slots, 3 * part :] = last.astype(BF)

    unpack(x_raw, x_copies, x)
    unpack(dy_raw, dy_copies, dy)
    wdn_copy.wait()
    for copy in wgu_copies:
        copy.wait()
    term[...] = jnp.zeros_like(term)

    def forward(b, _):
        pre = dot(x[...], wgu[b])
        back = dot_t(dy[...], wdn[pl.ds(pl.multiple_of(b * hidden, hidden), hidden), :])
        pre_gate, pre_up = pre[:, :hidden], pre[:, hidden:]
        s = jax.nn.sigmoid(pre_gate)
        activated = pre_gate * s
        slope = s * (1.0 + pre_gate * (1.0 - s))
        term[...] += activated * pre_up * back
        grads[b, :, :hidden] = (back * pre_up * slope).astype(BF)
        grads[b, :, hidden:] = (back * activated).astype(BF)
        return 0

    lax.fori_loop(0, blocks, forward, 0)
    terms = jnp.broadcast_to(jnp.sum(term[...], axis=1, keepdims=True), (2 * slots, TERM_LANES)).astype(BF)

    gather = slot_matrix(slots, packed, 1, None)
    gather_tail = [slot_matrix(slots, packed, 1, j) for j in range(3)]
    outs = (own_ref, other_ref)
    for i in range(2):
        outs[i][:, main_width:] = dot(gather, terms[i * slots : (i + 1) * slots]).astype(BF)

    def backward(low):
        total = dot_t(grads[0], wgu[0, low : low + part, :])
        for b in range(1, blocks):
            total += dot_t(grads[b], wgu[b, low : low + part, :])
        return total.astype(BF)

    last = backward(3 * part)
    for j in range(3):
        rows = backward(j * part)
        for i in range(2):
            span = slice(i * slots, (i + 1) * slots)
            outs[i][:, j * part : (j + 1) * part] = (
                dot(gather, rows[span]) + dot(gather_tail[j], last[span])
            ).astype(BF)


def expert_part(xo, xt, dyo, dyt, wgu, wdn):
    packed, main_width = xo.shape
    blocks, width, both = wgu.shape
    slots = packed // ROWS * CAP
    out = jax.ShapeDtypeStruct((packed, main_width + TERM_LANES), BF)
    return pl.pallas_call(
        expert_kernel,
        out_shape=(out, out),
        in_specs=[pl.BlockSpec(memory_space=pl.ANY)] * 6,
        scratch_shapes=[
            pltpu.VMEM((2, packed, main_width), BF),
            pltpu.VMEM((2, packed, main_width), BF),
            pltpu.VMEM((2 * slots, width), BF),
            pltpu.VMEM((2 * slots, width), BF),
            pltpu.VMEM(wgu.shape, BF),
            pltpu.VMEM(wdn.shape, BF),
            pltpu.VMEM((blocks, 2 * slots, both), BF),
            pltpu.VMEM((2 * slots, both // 2), F32),
            pltpu.SemaphoreType.DMA((5 + blocks,)),
        ],
        compiler_params=pltpu.CompilerParams(vmem_limit_bytes=VMEM_LIMIT),
        cost_estimate=pl.CostEstimate(
            flops=2 * 2 * slots * width * both // 2 * blocks * 5,
            bytes_accessed=2 * (wgu.size + wdn.size + 6 * xo.size),
            transcendentals=2 * slots * both // 2 * blocks,
        ),
        name="expert",
    )(xo, xt, dyo, dyt, wgu, wdn)


def combine_kernel(route_ref, gate_ref, own_term_ref, out_grad_ref, ret_ref, token_grad_ref, gate_grad_ref):
    n, width = out_grad_ref.shape
    packed = ret_ref.shape[0]
    part = width // 4
    experts = packed // ROWS
    route_row = route_ref[...]
    main, tail, block = (to_column(v) for v in places(route_row))
    routed = to_column(route_row) < experts
    gate = to_column(gate_ref[...])
    row = lax.broadcasted_iota(jnp.int32, (n, packed), 1)
    select = jnp.where(row == main, 1.0, 0.0).astype(BF)
    last = jnp.zeros((n, part), F32)
    for j in range(4):
        cols = pl.ds(j * part, part)
        if j < 3:
            tail_select = jnp.where((row == tail) & (block == j), 1.0, 0.0).astype(BF)
            piece = ret_ref[:, cols]
            rows = dot(select, piece)
            last += dot(tail_select, piece)
        else:
            rows = last
        rows = jnp.where(routed, rows, out_grad_ref[:, cols].astype(F32))
        token_grad_ref[:, cols] = (gate * rows).astype(BF)
    terms = dot(select, ret_ref[:, 3 * part :])[:, :1]
    gate_grad_ref[...] = jnp.where(route_row < experts, to_row(terms), own_term_ref[...]).astype(BF)


def combine(route_row, gate_row, own_term, out_grad, ret):
    n, width = out_grad.shape
    return pl.pallas_call(
        combine_kernel,
        out_shape=(jax.ShapeDtypeStruct((n, width), BF), jax.ShapeDtypeStruct((1, n), BF)),
        compiler_params=pltpu.CompilerParams(vmem_limit_bytes=VMEM_LIMIT),
        cost_estimate=pl.CostEstimate(
            flops=2 * ret.shape[0] * n * width * 3 // 2,
            bytes_accessed=2 * (2 * out_grad.size + ret.size),
            transcendentals=0,
        ),
        name="combine",
    )(route_row, gate_row, own_term, out_grad, ret)


def per_device(tokens, out_grad, gate, route, gate_weight, up_weight, down_weight):
    experts = lax.axis_size("expert")
    n, width = tokens.shape
    hidden = gate_weight.shape[2] // 2
    core = lax.axis_index("dp")
    swap = [(0, 1), (1, 0)]
    route_row = route.reshape(1, n)

    halves = [lax.dynamic_slice(w[0], (0, core * hidden), (width, hidden)) for w in (gate_weight, up_weight)]
    wgu = lax.all_gather(jnp.concatenate(halves, axis=1), "tensor", axis=0, tiled=False)
    wdn = lax.all_gather(
        lax.dynamic_slice(down_weight[0], (core * hidden, 0), (hidden, width)), "tensor", axis=0, tiled=True
    )

    def send(rows):
        packed = pack(route_row, rows, experts).reshape(experts, ROWS, -1)
        got = lax.all_to_all(packed, "expert", split_axis=0, concat_axis=0, tiled=True)
        got = got.reshape(experts * ROWS, -1)
        return got, lax.ppermute(got, "dp", swap)

    xo, xt = send(tokens)
    dyo, dyt = send(out_grad)
    own, other = expert_part(xo, xt, dyo, dyt, wgu, wdn)
    from_other = lax.ppermute(other, "dp", swap)
    total = (own.astype(F32) + from_other.astype(F32)).astype(BF).reshape(experts, ROWS, -1)
    ret = lax.all_to_all(total, "expert", split_axis=0, concat_axis=0, tiled=True)
    own_term = jnp.sum(out_grad.astype(F32) * tokens.astype(F32), axis=1)
    token_grad, gate_grad = combine(
        route_row, gate.reshape(1, n), own_term.reshape(1, n), out_grad, ret.reshape(experts * ROWS, -1)
    )
    return token_grad, gate_grad.reshape(n)


def solution(mesh):
    rows = P(("dp", "expert", "tensor"), None)
    return jax.shard_map(
        per_device,
        mesh=mesh,
        in_specs=(
            rows,
            rows,
            P(("dp", "expert", "tensor")),
            rows,
            P("expert", None, "tensor"),
            P("expert", None, "tensor"),
            P("expert", "tensor", None),
        ),
        out_specs=(rows, P(("dp", "expert", "tensor"))),
        check_vma=False,
    )
```

```python
import jax
import jax.numpy as jnp
from jax import lax
from jax.experimental import pallas as pl
from jax.experimental.pallas import tpu as pltpu
from jax.sharding import PartitionSpec as P

BF = jnp.bfloat16
F32 = jnp.float32
CAP = 6
ROWS = 8
TERM_LANES = 128
FIRST_COST = 1000
UNITS = 10
VMEM_LIMIT = 56 * 1024 * 1024


def dot(a, b):
    return jnp.dot(a, b, preferred_element_type=F32)


def dot_t(a, b):
    return lax.dot_general(a, b, (((1,), (1,)), ((), ())), preferred_element_type=F32)


def eye(n):
    return lax.broadcasted_iota(jnp.int32, (n, n), 0) == lax.broadcasted_iota(jnp.int32, (n, n), 1)


def to_column(row):
    n = row.shape[1]
    return jnp.sum(jnp.where(eye(n), jnp.broadcast_to(row, (n, n)), 0), axis=1, keepdims=True)


def to_row(column):
    n = column.shape[0]
    return jnp.sum(jnp.where(eye(n), jnp.broadcast_to(column, (n, n)), 0), axis=0, keepdims=True)


def places(route_row):
    n = route_row.shape[1]
    across = jnp.broadcast_to(route_row, (n, n))
    down = jnp.broadcast_to(to_column(route_row), (n, n))
    earlier = lax.broadcasted_iota(jnp.int32, (n, n), 0) < lax.broadcasted_iota(jnp.int32, (n, n), 1)
    slot = jnp.sum(jnp.where((across == down) & earlier, 1, 0), axis=0, keepdims=True)
    second = jnp.where(slot >= 3, 1, 0)
    base = route_row * ROWS
    return base + slot, base + CAP + second, slot - 3 * second


def pack_kernel(route_ref, rows_ref, out_ref):
    n, width = rows_ref.shape
    total = out_ref.shape[0]
    part = width // 4
    main, tail, block = places(route_ref[...])
    row = lax.broadcasted_iota(jnp.int32, (total, n), 0)
    select = jnp.where(row == main, 1.0, 0.0).astype(BF)
    last = rows_ref[:, 3 * part :]
    for j in range(3):
        tail_select = jnp.where((row == tail) & (block == j), 1.0, 0.0).astype(BF)
        cols = pl.ds(j * part, part)
        out_ref[:, cols] = (dot(select, rows_ref[:, cols]) + dot(tail_select, last)).astype(BF)


def pack(route_row, rows, experts):
    n, width = rows.shape
    return pl.pallas_call(
        pack_kernel,
        out_shape=jax.ShapeDtypeStruct((experts * ROWS, width // 4 * 3), BF),
        compiler_params=pltpu.CompilerParams(vmem_limit_bytes=VMEM_LIMIT),
        cost_estimate=pl.CostEstimate(
            flops=2 * experts * ROWS * n * width * 3 // 2,
            bytes_accessed=2 * width * (n + experts * CAP),
            transcendentals=0,
        ),
        name="pack",
    )(route_row, rows)


def weight_pieces(core, gate_weight, up_weight, down_weight, units, pieces):
    width, hidden = gate_weight.shape[0], gate_weight.shape[1] // 2
    rows = width // UNITS
    first, stride, steps = units

    def unit(i):
        return first + stride * i

    def kernel(core_ref, gate_ref, up_ref, down_ref, *outs):
        here = unit(pl.program_id(0))
        block = jnp.concatenate([gate_ref[...], up_ref[...], down_ref[...].T], axis=1)
        for (low, high), out in zip(pieces, outs):

            @pl.when((here >= low) & (here < high))
            def _(out=out):
                out[...] = block

    def place(low, high):
        return pl.BlockSpec((rows, 3 * hidden), lambda i, c: (jnp.clip(unit(i), low, high - 1) - low, 0))

    return pl.pallas_call(
        kernel,
        grid_spec=pltpu.PrefetchScalarGridSpec(
            num_scalar_prefetch=1,
            grid=(steps,),
            in_specs=[pl.BlockSpec((rows, hidden), lambda i, c: (unit(i), c[0]))] * 2
            + [pl.BlockSpec((hidden, rows), lambda i, c: (c[0], unit(i)))],
            out_specs=[place(*piece) for piece in pieces],
        ),
        out_shape=[jax.ShapeDtypeStruct(((high - low) * rows, 3 * hidden), BF) for low, high in pieces],
        compiler_params=pltpu.CompilerParams(vmem_limit_bytes=VMEM_LIMIT),
        cost_estimate=pl.CostEstimate(
            flops=0, bytes_accessed=2 * 3 * 3 * steps * rows * hidden, transcendentals=0
        ),
        name="weights",
    )(core, gate_weight, up_weight, down_weight)


def copy_pieces(pieces, full, sems):
    copies, low = [], 0
    for piece in pieces:
        rows = piece.shape[0]
        copies.append(pltpu.make_async_copy(piece, full.at[pl.ds(low, rows)], sems.at[len(copies)]))
        low += rows
    return copies


def slot_matrix(slots, packed, slot_dim, tail):
    shape = (slots, packed) if slot_dim == 0 else (packed, slots)
    slot = lax.broadcasted_iota(jnp.int32, shape, slot_dim)
    row = lax.broadcasted_iota(jnp.int32, shape, 1 - slot_dim)
    group, place = row >> 3, row & 7
    if tail is None:
        hit = (slot == group * CAP + place) & (place < CAP)
    else:
        hit = (slot == group * CAP + (place - CAP) * 3 + tail) & (place >= CAP)
    return jnp.where(hit, 1.0, 0.0).astype(BF)


def block_forward(x, dy, w, grads):
    both = grads.shape[1]
    hidden = both // 2
    pre = dot(x[...], w[:, :both])
    back = dot(dy[...], w[:, both:])
    pre_gate, pre_up = pre[:, :hidden], pre[:, hidden:]
    s = jax.nn.sigmoid(pre_gate)
    activated = pre_gate * s
    slope = s * (1.0 + pre_gate * (1.0 - s))
    grads[:, :hidden] = (back * pre_up * slope).astype(BF)
    grads[:, hidden:] = (back * activated).astype(BF)
    return activated * pre_up * back


def first_kernel(
    x_own, x_other, dy_own, dy_other, o0, o1, o2, u0, u1, u2, d0, d1, d2,
    x_hbm, dy_hbm, sum_hbm, term_ref,
    raw, x, dy, w, grads, total, sems,
):
    packed = raw.shape[1]
    blocks, width, triple = w.shape
    both = triple // 3 * 2
    slots = x.shape[0] // 2
    part = width // 4
    raw_copies = [
        pltpu.make_async_copy(src, raw.at[i], sems.at[i])
        for i, src in enumerate((x_own, x_other, dy_own, dy_other))
    ]
    w_copies = []
    for i, pieces in enumerate(((o0, o1, o2), (u0, u1, u2), (d0, d1, d2))):
        w_copies += copy_pieces(pieces, w.at[i], sems.at[pl.ds(7 + 3 * i, 3)])
    for copy in raw_copies + w_copies:
        copy.start()
    spread = slot_matrix(slots, packed, 0, None)
    spread_tail = [slot_matrix(slots, packed, 0, j) for j in range(3)]
    for i, copy in enumerate(raw_copies):
        copy.wait()
        full = (x, dy)[i // 2]
        rows = slice(i % 2 * slots, (i % 2 + 1) * slots)
        pieces = [slice(j * part, (j + 1) * part) for j in range(3)]
        for j in range(3):
            full[rows, pieces[j]] = dot(spread, raw[i, :, pieces[j]]).astype(BF)
        last = dot(spread_tail[0], raw[i, :, pieces[0]])
        last += dot(spread_tail[1], raw[i, :, pieces[1]])
        last += dot(spread_tail[2], raw[i, :, pieces[2]])
        full[rows, 3 * part :] = last.astype(BF)
    x_out = pltpu.make_async_copy(x, x_hbm, sems.at[4])
    dy_out = pltpu.make_async_copy(dy, dy_hbm, sems.at[5])
    x_out.start()
    dy_out.start()
    for copy in w_copies:
        copy.wait()
    term_ref[...] = jnp.zeros_like(term_ref)

    def forward(b, _):
        term_ref[...] += block_forward(x, dy, w.at[b], grads.at[b])
        return 0

    lax.fori_loop(0, blocks, forward, 0)
    for j in range(4):
        cols = slice(j * part, (j + 1) * part)
        piece = dot_t(grads[0], w[0, cols, :both])
        for b in range(1, blocks):
            piece += dot_t(grads[b], w[b, cols, :both])
        total[:, cols] = piece.astype(BF)
    out = pltpu.make_async_copy(total, sum_hbm, sems.at[6])
    out.start()
    x_out.wait()
    dy_out.wait()
    out.wait()


def first_blocks(rows, weights):
    packed = rows[0].shape[0]
    slots = packed // ROWS * CAP
    triple = weights[0].shape[1]
    width = sum(w.shape[0] for w in weights[:3])
    hidden = triple // 3
    full = jax.ShapeDtypeStruct((2 * slots, width), BF)
    return pl.pallas_call(
        first_kernel,
        out_shape=(full, full, full, jax.ShapeDtypeStruct((2 * slots, hidden), F32)),
        in_specs=[pl.BlockSpec(memory_space=pl.ANY)] * 13,
        out_specs=(pl.BlockSpec(memory_space=pl.ANY),) * 3 + (pl.BlockSpec(memory_space=pltpu.VMEM),),
        scratch_shapes=[
            pltpu.VMEM((4,) + rows[0].shape, BF),
            pltpu.VMEM((2 * slots, width), BF),
            pltpu.VMEM((2 * slots, width), BF),
            pltpu.VMEM((3, width, triple), BF),
            pltpu.VMEM((3, 2 * slots, 2 * hidden), BF),
            pltpu.VMEM((2 * slots, width), BF),
            pltpu.SemaphoreType.DMA((16,)),
        ],
        compiler_params=pltpu.CompilerParams(vmem_limit_bytes=VMEM_LIMIT),
        cost_estimate=pl.CostEstimate(flops=FIRST_COST, bytes_accessed=FIRST_COST, transcendentals=0),
        name="first",
    )(*rows, *weights)


def last_kernel(
    x_hbm, dy_hbm, w0, w1, w2, w3, w4, w5, sum_hbm, term_ref,
    own_ref, other_ref,
    x, dy, w, total, grads, sems,
):
    packed = own_ref.shape[0]
    slots = x.shape[0] // 2
    part = x.shape[1] // 4
    both = grads.shape[1]
    copies = [
        pltpu.make_async_copy(src, dst, sems.at[i])
        for i, (src, dst) in enumerate(((x_hbm, x), (dy_hbm, dy), (sum_hbm, total)))
    ]
    copies = copies[:2] + copy_pieces((w0, w1, w2, w3, w4, w5), w, sems.at[pl.ds(3, 6)]) + copies[2:]
    for copy in copies:
        copy.start()
    gather = slot_matrix(slots, packed, 1, None)
    gather_tail = [slot_matrix(slots, packed, 1, j) for j in range(3)]
    for copy in copies[:-1]:
        copy.wait()
    term = term_ref[...] + block_forward(x, dy, w, grads)
    terms = jnp.broadcast_to(jnp.sum(term, axis=1, keepdims=True), (2 * slots, TERM_LANES)).astype(BF)
    copies[-1].wait()

    def backward(j):
        cols = slice(j * part, (j + 1) * part)
        piece = dot_t(grads[...], w[cols, :both])
        return (total[:, cols].astype(F32) + piece).astype(BF)

    outs = (own_ref, other_ref)
    spans = [slice(i * slots, (i + 1) * slots) for i in range(2)]
    for i in range(2):
        outs[i][:, 3 * part :] = dot(gather, terms[spans[i]]).astype(BF)
    last = backward(3)
    for j in range(3):
        rows = backward(j)
        for i in range(2):
            outs[i][:, j * part : (j + 1) * part] = (
                dot(gather, rows[spans[i]]) + dot(gather_tail[j], last[spans[i]])
            ).astype(BF)


def last_block(x, dy, weights, total, term, packed):
    rows, width = x.shape
    triple = weights[0].shape[1]
    hidden = triple // 3
    out = jax.ShapeDtypeStruct((packed, width // 4 * 3 + TERM_LANES), BF)
    return pl.pallas_call(
        last_kernel,
        out_shape=(out, out),
        in_specs=[pl.BlockSpec(memory_space=pl.ANY)] * 9 + [pl.BlockSpec(memory_space=pltpu.VMEM)],
        scratch_shapes=[
            pltpu.VMEM((rows, width), BF),
            pltpu.VMEM((rows, width), BF),
            pltpu.VMEM((width, triple), BF),
            pltpu.VMEM((rows, width), BF),
            pltpu.VMEM((rows, 2 * hidden), BF),
            pltpu.SemaphoreType.DMA((9,)),
        ],
        compiler_params=pltpu.CompilerParams(vmem_limit_bytes=VMEM_LIMIT),
        cost_estimate=pl.CostEstimate(
            flops=2 * rows * width * hidden * 5,
            bytes_accessed=2 * (width * triple + 5 * rows * width),
            transcendentals=rows * hidden,
        ),
        name="last",
    )(x, dy, *weights, total, term)


def add_kernel(a_ref, b_ref, out_ref):
    out_ref[...] = (a_ref[...].astype(F32) + b_ref[...].astype(F32)).astype(BF)


def add(a, b):
    rows, cols = a.shape
    spec = pl.BlockSpec((rows // 4, cols), lambda i: (i, 0))
    return pl.pallas_call(
        add_kernel,
        grid=(4,),
        out_shape=jax.ShapeDtypeStruct((rows, cols), BF),
        in_specs=[spec, spec],
        out_specs=spec,
        compiler_params=pltpu.CompilerParams(vmem_limit_bytes=VMEM_LIMIT),
        cost_estimate=pl.CostEstimate(flops=rows * cols, bytes_accessed=6 * rows * cols, transcendentals=0),
        name="add",
    )(a, b)


def combine_kernel(route_ref, gate_ref, own_term_ref, out_grad_ref, ret_ref, token_grad_ref, gate_grad_ref):
    n, width = out_grad_ref.shape
    packed = ret_ref.shape[0]
    part = width // 4
    experts = packed // ROWS
    route_row = route_ref[...]
    main, tail, block = (to_column(v) for v in places(route_row))
    routed = to_column(route_row) < experts
    gate = to_column(gate_ref[...])
    row = lax.broadcasted_iota(jnp.int32, (n, packed), 1)
    select = jnp.where(row == main, 1.0, 0.0).astype(BF)
    last = jnp.zeros((n, part), F32)
    for j in range(4):
        cols = pl.ds(j * part, part)
        if j < 3:
            tail_select = jnp.where((row == tail) & (block == j), 1.0, 0.0).astype(BF)
            piece = ret_ref[:, cols]
            rows = dot(select, piece)
            last += dot(tail_select, piece)
        else:
            rows = last
        rows = jnp.where(routed, rows, out_grad_ref[:, cols].astype(F32))
        token_grad_ref[:, cols] = (gate * rows).astype(BF)
    terms = dot(select, ret_ref[:, 3 * part :])[:, :1]
    gate_grad_ref[...] = jnp.where(route_row < experts, to_row(terms), own_term_ref[...]).astype(BF)


def combine(route_row, gate_row, own_term, out_grad, ret):
    n, width = out_grad.shape
    return pl.pallas_call(
        combine_kernel,
        out_shape=(jax.ShapeDtypeStruct((n, width), BF), jax.ShapeDtypeStruct((1, n), BF)),
        compiler_params=pltpu.CompilerParams(vmem_limit_bytes=VMEM_LIMIT),
        cost_estimate=pl.CostEstimate(
            flops=2 * ret.shape[0] * n * width * 3 // 2,
            bytes_accessed=2 * (2 * out_grad.size + ret.size),
            transcendentals=0,
        ),
        name="combine",
    )(route_row, gate_row, own_term, out_grad, ret)


def per_device(tokens, out_grad, gate, route, gate_weight, up_weight, down_weight):
    experts = lax.axis_size("expert")
    groups = lax.axis_size("tensor")
    n, width = tokens.shape
    core = lax.axis_index("dp")
    swap = [(0, 1), (1, 0)]
    up = [(i, (i + 1) % groups) for i in range(groups)]
    down = [(i, (i - 1) % groups) for i in range(groups)]
    route_row = route.reshape(1, n)

    weights = (gate_weight[0], up_weight[0], down_weight[0])
    core_id = core.reshape(1)
    first_part, last_part = weight_pieces(core_id, *weights, (0, UNITS - 1, 2), ((0, 1), (9, 10)))
    up_0 = lax.ppermute(first_part, "tensor", up)
    down_0 = lax.ppermute(last_part, "tensor", down)
    core_id, first_part, last_part = lax.optimization_barrier((core_id, first_part, last_part))
    pieces = weight_pieces(core_id, *weights, (0, 1, UNITS), ((1, 6), (6, 10), (4, 9), (0, 4)))
    route_row, up_next, up_rest, down_next, down_rest = lax.optimization_barrier((route_row, *pieces))
    unit = width // UNITS

    def exchange(rows):
        got = lax.all_to_all(
            rows.reshape(experts, ROWS, -1), "expert", split_axis=0, concat_axis=0, tiled=True
        )
        return got.reshape(experts * ROWS, -1)

    x_packed = pack(route_row, tokens, experts)
    x_packed, up_0, down_0 = lax.optimization_barrier((x_packed, up_0, down_0))
    x_own = exchange(x_packed)
    up_1 = lax.ppermute(up_next, "tensor", up)
    down_1 = lax.ppermute(down_next, "tensor", down)
    x_other = lax.ppermute(x_own, "dp", swap)

    dy_packed = pack(route_row, out_grad, experts)
    dy_packed, up_1, down_1 = lax.optimization_barrier((dy_packed, up_1, down_1))
    dy_own = exchange(dy_packed)
    up_2 = lax.ppermute(up_rest, "tensor", up)
    down_2 = lax.ppermute(down_rest, "tensor", down)
    far = {
        0: lax.ppermute(up_0, "tensor", up),
        9: lax.ppermute(down_0, "tensor", down),
        1: lax.ppermute(up_1[:unit], "tensor", up),
        8: lax.ppermute(down_1[4 * unit :], "tensor", down),
    }
    dy_own, up_2, down_2, far[0], far[1], far[8], far[9] = lax.optimization_barrier(
        (dy_own, up_2, down_2, far[0], far[1], far[8], far[9])
    )
    far[2] = lax.ppermute(up_1[unit : 4 * unit], "tensor", up)
    far[5] = lax.ppermute(down_1[unit : 4 * unit], "tensor", down)
    dy_other = lax.ppermute(dy_own, "dp", swap)

    x, dy, total, term = first_blocks(
        (x_own, x_other, dy_own, dy_other),
        (down_rest, down_next, last_part, up_0, up_1, up_2, down_2, down_1, down_0),
    )
    own, other = last_block(x, dy, [far[i] for i in (0, 1, 2, 5, 8, 9)], total, term, experts * ROWS)
    back = add(own, lax.ppermute(other, "dp", swap)).reshape(experts, ROWS, -1)
    ret = lax.all_to_all(back, "expert", split_axis=0, concat_axis=0, tiled=True)
    own_term = jnp.sum(out_grad.astype(F32) * tokens.astype(F32), axis=1)
    token_grad, gate_grad = combine(
        route_row, gate.reshape(1, n), own_term.reshape(1, n), out_grad, ret.reshape(experts * ROWS, -1)
    )
    return token_grad, gate_grad.reshape(n)


def solution(mesh):
    rows = P(("dp", "expert", "tensor"), None)
    return jax.shard_map(
        per_device,
        mesh=mesh,
        in_specs=(
            rows,
            rows,
            P(("dp", "expert", "tensor")),
            rows,
            P("expert", None, "tensor"),
            P("expert", None, "tensor"),
            P("expert", "tensor", None),
        ),
        out_specs=(rows, P(("dp", "expert", "tensor"))),
        check_vma=False,
    )
```

```python
import jax
import jax.numpy as jnp
from jax import lax
from jax.experimental import pallas as pl
from jax.experimental.pallas import tpu as pltpu
from jax.sharding import PartitionSpec as P

BF = jnp.bfloat16
F32 = jnp.float32
CAP = 6
ROWS = 8
TERM_LANES = 128
HALF_STEPS = 2
VMEM_ALL = 56 * 1024 * 1024
SMALL_VMEM = 20 * 1024 * 1024


def dot(a, b):
    return jnp.dot(a, b, preferred_element_type=F32)


def dot_t(a, b):
    return lax.dot_general(a, b, (((1,), (1,)), ((), ())), preferred_element_type=F32)


def eye(n):
    return lax.broadcasted_iota(jnp.int32, (n, n), 0) == lax.broadcasted_iota(jnp.int32, (n, n), 1)


def to_column(row):
    n = row.shape[1]
    return jnp.sum(jnp.where(eye(n), jnp.broadcast_to(row, (n, n)), 0), axis=1, keepdims=True)


def to_row(column):
    n = column.shape[0]
    return jnp.sum(jnp.where(eye(n), jnp.broadcast_to(column, (n, n)), 0), axis=0, keepdims=True)


def places(route_row):
    n = route_row.shape[1]
    across = jnp.broadcast_to(route_row, (n, n))
    down = jnp.broadcast_to(to_column(route_row), (n, n))
    earlier = lax.broadcasted_iota(jnp.int32, (n, n), 0) < lax.broadcasted_iota(jnp.int32, (n, n), 1)
    slot = jnp.sum(jnp.where((across == down) & earlier, 1, 0), axis=0, keepdims=True)
    second = jnp.where(slot >= 3, 1, 0)
    base = route_row * ROWS
    return base + slot, base + CAP + second, slot - 3 * second


def pack_kernel(route_ref, x_ref, dy_ref, out_ref):
    n, width = x_ref.shape
    total = out_ref.shape[0]
    part = width // 4
    main, tail, block = places(route_ref[...])
    row = lax.broadcasted_iota(jnp.int32, (total, n), 0)
    select = jnp.where(row == main, 1.0, 0.0).astype(BF)
    for j in range(3):
        tail_select = jnp.where((row == tail) & (block == j), 1.0, 0.0).astype(BF)
        cols = pl.ds(j * part, part)
        for i, rows_ref in enumerate((x_ref, dy_ref)):
            last = rows_ref[:, 3 * part :]
            out_ref[:, pl.ds((3 * i + j) * part, part)] = (
                dot(select, rows_ref[:, cols]) + dot(tail_select, last)
            ).astype(BF)


def pack(route_row, x, dy, experts):
    n, width = x.shape
    return pl.pallas_call(
        pack_kernel,
        out_shape=jax.ShapeDtypeStruct((experts * ROWS, width // 4 * 6), BF),
        compiler_params=pltpu.CompilerParams(vmem_limit_bytes=VMEM_ALL),
        cost_estimate=pl.CostEstimate(
            flops=2 * experts * ROWS * n * width * 3,
            bytes_accessed=4 * width * (n + experts * CAP),
            transcendentals=0,
        ),
        name="pack",
    )(route_row, x, dy)


def weights_kernel(core_ref, gate_ref, up_ref, down_ref, out_ref):
    rows, span = out_ref.shape
    hidden = down_ref.shape[0]
    i = pl.program_id(0)
    for part, ref in enumerate((gate_ref, up_ref)):

        @pl.when(i // HALF_STEPS == part)
        def _(ref=ref):
            out_ref[...] = ref[...]

    @pl.when(i // HALF_STEPS == 2)
    def _():
        for k in range(rows // hidden):
            out_ref[k * hidden : (k + 1) * hidden, :] = down_ref[:, k * span : (k + 1) * span]


def weight_stack(core, gate_weight, up_weight, down_weight):
    width, span = gate_weight.shape
    rows = width // 2 // HALF_STEPS

    def up_place(part):
        return lambda i, c: (c[0] * HALF_STEPS + jnp.clip(i - part * HALF_STEPS, 0, HALF_STEPS - 1), 0)

    return pl.pallas_call(
        weights_kernel,
        grid_spec=pltpu.PrefetchScalarGridSpec(
            num_scalar_prefetch=1,
            grid=(3 * HALF_STEPS,),
            in_specs=[
                pl.BlockSpec((rows, span), up_place(0)),
                pl.BlockSpec((rows, span), up_place(1)),
                pl.BlockSpec((span // 2, width // HALF_STEPS), lambda i, c: (c[0], jnp.maximum(i - 2 * HALF_STEPS, 0))),
            ],
            out_specs=pl.BlockSpec((rows, span), lambda i, c: (i, 0)),
        ),
        out_shape=jax.ShapeDtypeStruct((width * 3 // 2, span), BF),
        compiler_params=pltpu.CompilerParams(vmem_limit_bytes=VMEM_ALL),
        cost_estimate=pl.CostEstimate(
            flops=0, bytes_accessed=2 * 3 * width * span, transcendentals=0
        ),
        name="weights",
    )(core, gate_weight, up_weight, down_weight)


def slot_matrix(slots, packed, slot_dim, tail):
    shape = (slots, packed) if slot_dim == 0 else (packed, slots)
    slot = lax.broadcasted_iota(jnp.int32, shape, slot_dim)
    row = lax.broadcasted_iota(jnp.int32, shape, 1 - slot_dim)
    group, place = row >> 3, row & 7
    if tail is None:
        hit = (slot == group * CAP + place) & (place < CAP)
    else:
        hit = (slot == group * CAP + (place - CAP) * 3 + tail) & (place >= CAP)
    return jnp.where(hit, 1.0, 0.0).astype(BF)


def hidden_grads(pre_gate, pre_up, back):
    s = jax.nn.sigmoid(pre_gate)
    activated = pre_gate * s
    slope = s * (1.0 + pre_gate * (1.0 - s))
    return (back * pre_up * slope).astype(BF), (back * activated).astype(BF), activated * pre_up * back


def first_kernel(
    rows_hbm, gate_hbm, up_hbm, down_hbm,
    x_hbm, dy_hbm, sum_hbm, term_ref,
    raw, x, dy, gate, up, down, total, sems,
):
    packed = raw.shape[0]
    slots, part = x.shape[0], x.shape[1] // 4
    copies = [
        pltpu.make_async_copy(src, dst, sems.at[i])
        for i, (src, dst) in enumerate(((rows_hbm, raw), (gate_hbm, gate), (up_hbm, up), (down_hbm, down)))
    ]
    for copy in copies:
        copy.start()
    spread = slot_matrix(slots, packed, 0, None)
    spread_tail = [slot_matrix(slots, packed, 0, j) for j in range(3)]
    copies[0].wait()
    for k, full in enumerate((x, dy)):
        pieces = [slice((3 * k + j) * part, (3 * k + j + 1) * part) for j in range(3)]
        for j in range(3):
            full[:, j * part : (j + 1) * part] = dot(spread, raw[:, pieces[j]]).astype(BF)
        last = dot(spread_tail[0], raw[:, pieces[0]])
        last += dot(spread_tail[1], raw[:, pieces[1]])
        last += dot(spread_tail[2], raw[:, pieces[2]])
        full[:, 3 * part :] = last.astype(BF)
    outs = [
        pltpu.make_async_copy(src, dst, sems.at[4 + i])
        for i, (src, dst) in enumerate(((x, x_hbm), (dy, dy_hbm), (total, sum_hbm)))
    ]
    outs[0].start()
    outs[1].start()
    copies[1].wait()
    pre_gate = dot(x[...], gate[...])
    copies[2].wait()
    pre_up = dot(x[...], up[...])
    copies[3].wait()
    grad_gate, grad_up, term_ref[...] = hidden_grads(pre_gate, pre_up, dot_t(dy[...], down[...]))
    for j in range(4):
        cols = slice(j * part, (j + 1) * part)
        total[:, cols] = (dot_t(grad_gate, gate[cols, :]) + dot_t(grad_up, up[cols, :])).astype(BF)
    outs[2].start()
    for copy in outs:
        copy.wait()


def first_block(rows, gate_weight, up_weight, down_weight):
    packed = rows.shape[0]
    slots = packed // ROWS * CAP
    width, span = gate_weight.shape
    full = jax.ShapeDtypeStruct((slots, width), BF)
    any_spec = pl.BlockSpec(memory_space=pl.ANY)
    return pl.pallas_call(
        first_kernel,
        out_shape=(full, full, full, jax.ShapeDtypeStruct((slots, span), F32)),
        in_specs=[any_spec] * 4,
        out_specs=(any_spec,) * 3 + (pl.BlockSpec(memory_space=pltpu.VMEM),),
        scratch_shapes=[
            pltpu.VMEM(rows.shape, BF),
            pltpu.VMEM((slots, width), BF),
            pltpu.VMEM((slots, width), BF),
            pltpu.VMEM((width, span), BF),
            pltpu.VMEM((width, span), BF),
            pltpu.VMEM((span, width), BF),
            pltpu.VMEM((slots, width), BF),
            pltpu.SemaphoreType.DMA((7,)),
        ],
        compiler_params=pltpu.CompilerParams(vmem_limit_bytes=VMEM_ALL),
        cost_estimate=pl.CostEstimate(
            flops=2 * slots * width * span * 5,
            bytes_accessed=2 * (3 * width * span + rows.size + 3 * slots * width),
            transcendentals=slots * span,
        ),
        name="first",
    )(rows, gate_weight, up_weight, down_weight)


def rest_kernel(
    index_ref, x_hbm, dy_hbm, stack, stack_blocks, sum_hbm, term_ref,
    out_ref,
    x, dy, gu, down, total, grads, sems,
):
    packed = out_ref.shape[0]
    slots, width = x.shape
    part = width // 4
    span = stack.shape[3]
    half = width // 2
    hidden = span // 2
    groups = stack.shape[0]
    blocks = groups - 1
    x_copy = pltpu.make_async_copy(x_hbm, x, sems.at[0])
    dy_copy = pltpu.make_async_copy(dy_hbm, dy, sems.at[1])
    sum_copy = pltpu.make_async_copy(sum_hbm, total, sems.at[2])
    gu_copies, down_copies = [], []
    for b in range(blocks):
        index = lax.rem(index_ref[0] + 1 + b, groups)
        low = 3 + 6 * b
        gu_copies.append(
            [
                pltpu.make_async_copy(
                    stack.at[index, c, pl.ds(part_id * half, half)],
                    gu.at[pl.ds(c * half, half), pl.ds((2 * b + part_id) * span, span)],
                    sems.at[low + 2 * c + part_id],
                )
                for c in range(2)
                for part_id in range(2)
            ]
        )
        down_copies.append(
            [
                pltpu.make_async_copy(
                    stack_blocks.at[index, c, pl.ds(width // hidden, width // span)],
                    down.at[:, pl.ds((2 * b + c) * hidden, hidden)],
                    sems.at[low + 4 + c],
                )
                for c in range(2)
            ]
        )
    x_copy.start()
    for copy in gu_copies[0]:
        copy.start()
    dy_copy.start()
    for copies in gu_copies[1:] + down_copies:
        for copy in copies:
            copy.start()
    sum_copy.start()
    gather = slot_matrix(slots, packed, 1, None)
    gather_tail = [slot_matrix(slots, packed, 1, j) for j in range(3)]
    x_copy.wait()
    pres = []
    for b in range(blocks):
        for copy in gu_copies[b]:
            copy.wait()
        pres.append(dot(x[...], gu[:, 2 * b * span : 2 * (b + 1) * span]))
    dy_copy.wait()
    for copies in down_copies:
        for copy in copies:
            copy.wait()
    back = dot_t(dy[:, :span], down[0])
    for k in range(1, width // span):
        back += dot_t(dy[:, k * span : (k + 1) * span], down[k])
    term = term_ref[...]
    for b in range(blocks):
        low = 2 * b * span
        grad_gate, grad_up, more = hidden_grads(
            pres[b][:, :span], pres[b][:, span:], back[:, b * span : (b + 1) * span]
        )
        grads[:, low : low + span] = grad_gate
        grads[:, low + span : low + 2 * span] = grad_up
        term += more
    terms = jnp.broadcast_to(jnp.sum(term, axis=1, keepdims=True), (slots, TERM_LANES)).astype(BF)
    out_ref[:, 3 * part :] = dot(gather, terms).astype(BF)
    sum_copy.wait()

    def backward(j):
        cols = slice(j * part, (j + 1) * part)
        return (total[:, cols].astype(F32) + dot_t(grads[...], gu[cols, :])).astype(BF)

    last = backward(3)
    for j in range(3):
        out_ref[:, j * part : (j + 1) * part] = (dot(gather, backward(j)) + dot(gather_tail[j], last)).astype(BF)


def rest_blocks(index, x, dy, stacks, total, term, packed):
    slots, width = x.shape
    groups, cores, rows, span = stacks.shape
    blocks, hidden = groups - 1, span // 2
    any_spec = pl.BlockSpec(memory_space=pl.ANY)
    vmem_spec = pl.BlockSpec(memory_space=pltpu.VMEM)
    return pl.pallas_call(
        rest_kernel,
        out_shape=jax.ShapeDtypeStruct((packed, width // 4 * 3 + TERM_LANES), BF),
        in_specs=[pl.BlockSpec(memory_space=pltpu.SMEM)] + [any_spec] * 5 + [vmem_spec],
        out_specs=vmem_spec,
        scratch_shapes=[
            pltpu.VMEM((slots, width), BF),
            pltpu.VMEM((slots, width), BF),
            pltpu.VMEM((width, 2 * blocks * span), BF),
            pltpu.VMEM((width // span, blocks * span, span), BF),
            pltpu.VMEM((slots, width), BF),
            pltpu.VMEM((slots, 2 * blocks * span), BF),
            pltpu.SemaphoreType.DMA((3 + 6 * blocks,)),
        ],
        compiler_params=pltpu.CompilerParams(vmem_limit_bytes=VMEM_ALL),
        cost_estimate=pl.CostEstimate(
            flops=2 * slots * width * span * 5 * blocks,
            bytes_accessed=2 * (blocks * width * span * 3 + 4 * slots * width),
            transcendentals=slots * span * blocks,
        ),
        name="rest",
    )(index, x, dy, stacks, stacks.reshape(groups, cores, -1, hidden, span), total, term)


def combine_kernel(route_ref, gate_ref, own_term_ref, out_grad_ref, ret_ref, token_grad_ref, gate_grad_ref):
    n, width = out_grad_ref.shape
    packed = ret_ref.shape[0]
    part = width // 4
    experts = packed // ROWS
    route_row = route_ref[...]
    main, tail, block = (to_column(v) for v in places(route_row))
    routed = to_column(route_row) < experts
    gate = to_column(gate_ref[...])
    row = lax.broadcasted_iota(jnp.int32, (n, packed), 1)
    select = jnp.where(row == main, 1.0, 0.0).astype(BF)
    last = jnp.zeros((n, part), F32)
    for j in range(4):
        cols = pl.ds(j * part, part)
        if j < 3:
            tail_select = jnp.where((row == tail) & (block == j), 1.0, 0.0).astype(BF)
            piece = ret_ref[:, cols]
            rows = dot(select, piece)
            last += dot(tail_select, piece)
        else:
            rows = last
        rows = jnp.where(routed, rows, out_grad_ref[:, cols].astype(F32))
        token_grad_ref[:, cols] = (gate * rows).astype(BF)
    terms = dot(select, ret_ref[:, 3 * part :])[:, :1]
    gate_grad_ref[...] = jnp.where(route_row < experts, to_row(terms), own_term_ref[...]).astype(BF)


def combine(route_row, gate_row, own_term, out_grad, ret):
    n, width = out_grad.shape
    return pl.pallas_call(
        combine_kernel,
        out_shape=(jax.ShapeDtypeStruct((n, width), BF), jax.ShapeDtypeStruct((1, n), BF)),
        compiler_params=pltpu.CompilerParams(vmem_limit_bytes=SMALL_VMEM),
        cost_estimate=pl.CostEstimate(
            flops=2 * ret.shape[0] * n * width * 3 // 2,
            bytes_accessed=2 * (2 * out_grad.size + ret.size),
            transcendentals=0,
        ),
        name="combine",
    )(route_row, gate_row, own_term, out_grad, ret)


def per_device(tokens, out_grad, gate, route, gate_weight, up_weight, down_weight):
    experts = lax.axis_size("expert")
    n, width = tokens.shape
    core = lax.axis_index("dp")
    route_row = route.reshape(1, n)
    weights = (gate_weight[0], up_weight[0], down_weight[0])

    stack = weight_stack(core.reshape(1), *weights)
    stacks = lax.all_gather(stack, ("tensor", "dp"), axis=0, tiled=False)
    stacks = stacks.reshape(-1, 2, *stack.shape)

    pack_route, stack = lax.optimization_barrier((route_row, stack))
    packed = pack(pack_route, tokens, out_grad, experts).reshape(experts, ROWS, -1)
    got = lax.all_to_all(packed, "expert", split_axis=0, concat_axis=0, tiled=True)
    x, dy, total, term = first_block(got.reshape(experts * ROWS, -1), *weights)
    back = rest_blocks(
        lax.axis_index("tensor").reshape(1), x, dy, stacks, total, term, experts * ROWS
    ).reshape(experts, ROWS, -1)
    ret = lax.all_to_all(back, "expert", split_axis=0, concat_axis=0, tiled=True)
    own_term = jnp.sum(out_grad.astype(F32) * tokens.astype(F32), axis=1)
    token_grad, gate_grad = combine(
        route_row, gate.reshape(1, n), own_term.reshape(1, n), out_grad, ret.reshape(experts * ROWS, -1)
    )
    return token_grad, gate_grad.reshape(n)


def solution(mesh):
    rows = P(("dp", "expert", "tensor"), None)
    return jax.shard_map(
        per_device,
        mesh=mesh,
        in_specs=(
            rows,
            rows,
            P(("dp", "expert", "tensor")),
            rows,
            P("expert", None, "tensor"),
            P("expert", None, "tensor"),
            P("expert", "tensor", None),
        ),
        out_specs=(rows, P(("dp", "expert", "tensor"))),
        check_vma=False,
    )
```

```python
import functools

import jax
import jax.numpy as jnp
from jax import lax
from jax.experimental import pallas as pl
from jax.experimental.pallas import tpu as pltpu
from jax.sharding import PartitionSpec as P

BF = jnp.bfloat16
F32 = jnp.float32
CAP = 6
ROWS = 8
TERM_LANES = 128
PARTS = 60
UP_PARTS = 40
HEAD = 6
HALF = 30
VMEM_ALL = 56 * 1024 * 1024
SMALL_VMEM = 20 * 1024 * 1024


def dot(a, b):
    return jnp.dot(a, b, preferred_element_type=F32)


def dot_t(a, b):
    return lax.dot_general(a, b, (((1,), (1,)), ((), ())), preferred_element_type=F32)


def eye(n):
    return lax.broadcasted_iota(jnp.int32, (n, n), 0) == lax.broadcasted_iota(jnp.int32, (n, n), 1)


def to_column(row):
    n = row.shape[1]
    return jnp.sum(jnp.where(eye(n), jnp.broadcast_to(row, (n, n)), 0), axis=1, keepdims=True)


def to_row(column):
    n = column.shape[0]
    return jnp.sum(jnp.where(eye(n), jnp.broadcast_to(column, (n, n)), 0), axis=0, keepdims=True)


def places(route_row):
    n = route_row.shape[1]
    across = jnp.broadcast_to(route_row, (n, n))
    down = jnp.broadcast_to(to_column(route_row), (n, n))
    earlier = lax.broadcasted_iota(jnp.int32, (n, n), 0) < lax.broadcasted_iota(jnp.int32, (n, n), 1)
    slot = jnp.sum(jnp.where((across == down) & earlier, 1, 0), axis=0, keepdims=True)
    second = jnp.where(slot >= 3, 1, 0)
    base = route_row * ROWS
    return base + slot, base + CAP + second, slot - 3 * second


def pack_kernel(route_ref, x_ref, dy_ref, out_ref):
    n, width = x_ref.shape
    total = out_ref.shape[0]
    part = width // 4
    main, tail, block = places(route_ref[...])
    row = lax.broadcasted_iota(jnp.int32, (total, n), 0)
    select = jnp.where(row == main, 1.0, 0.0).astype(BF)
    for j in range(3):
        tail_select = jnp.where((row == tail) & (block == j), 1.0, 0.0).astype(BF)
        cols = pl.ds(j * part, part)
        for i, rows_ref in enumerate((x_ref, dy_ref)):
            last = rows_ref[:, 3 * part :]
            out_ref[:, pl.ds((3 * i + j) * part, part)] = (
                dot(select, rows_ref[:, cols]) + dot(tail_select, last)
            ).astype(BF)


def pack(route_row, x, dy, experts):
    n, width = x.shape
    return pl.pallas_call(
        pack_kernel,
        out_shape=jax.ShapeDtypeStruct((experts * ROWS, width // 4 * 6), BF),
        compiler_params=pltpu.CompilerParams(vmem_limit_bytes=VMEM_ALL),
        cost_estimate=pl.CostEstimate(
            flops=2 * experts * ROWS * n * width * 3,
            bytes_accessed=4 * width * (n + experts * CAP),
            transcendentals=0,
        ),
        name="pack",
    )(route_row, x, dy)


def part_copies(weights, core, low, high, out, sems):
    gate, up, down = weights
    hidden, span = out.shape[0] // (high - low), out.shape[1]
    columns = pl.ds(pl.multiple_of(core * hidden, hidden), hidden)
    last_up = min(high, UP_PARTS)
    copies = []
    if low < last_up:
        rows = slice(low * hidden, last_up * hidden)
        for i, ref in enumerate((gate, up)):
            dst = out.at[0 : (last_up - low) * hidden, i * hidden : (i + 1) * hidden]
            copies.append(pltpu.make_async_copy(ref.at[rows, columns], dst, sems.at[len(copies)]))
    for k in range(max(low, UP_PARTS), high):
        src = down.at[columns, (k - UP_PARTS) * span : (k - UP_PARTS + 1) * span]
        dst = out.at[(k - low) * hidden : (k - low + 1) * hidden, :]
        copies.append(pltpu.make_async_copy(src, dst, sems.at[len(copies)]))
    return copies


def weights_kernel(read, write, core_ref, gate, up, down, *refs):
    outs, held, sems = refs[: len(write)], refs[len(write) : -1], refs[-1]
    hidden = held[0].shape[1] // 2
    copies = []
    for (low, high), buffer in zip(read, held):
        copies += part_copies((gate, up, down), core_ref[0], low, high, buffer, sems.at[pl.ds(len(copies), PARTS)])
    for copy in copies:
        copy.start()
    for copy in copies:
        copy.wait()
    copies = []
    for i, ((low, high), out) in enumerate(zip(write, outs)):
        for (first, last), buffer in zip(read, held):
            if first <= low and high <= last:
                src = buffer.at[(low - first) * hidden : (high - first) * hidden, :]
                copies.append(pltpu.make_async_copy(src, out, sems.at[i]))
    for copy in copies:
        copy.start()
    for copy in copies:
        copy.wait()


def weight_parts(core, weights, read, write):
    width, span = weights[0].shape
    hidden = span // 2
    any_spec = pl.BlockSpec(memory_space=pl.ANY)
    size = lambda parts: ((parts[1] - parts[0]) * hidden, span)
    return pl.pallas_call(
        functools.partial(weights_kernel, read, write),
        out_shape=[jax.ShapeDtypeStruct(size(parts), BF) for parts in write],
        in_specs=[pl.BlockSpec(memory_space=pltpu.SMEM)] + [any_spec] * 3,
        out_specs=[any_spec] * len(write),
        scratch_shapes=[pltpu.VMEM(size(parts), BF) for parts in read]
        + [pltpu.SemaphoreType.DMA((2 * PARTS,))],
        compiler_params=pltpu.CompilerParams(vmem_limit_bytes=VMEM_ALL),
        cost_estimate=pl.CostEstimate(
            flops=0, bytes_accessed=4 * span * hidden * sum(b - a for a, b in read + write), transcendentals=0
        ),
        name="weights",
    )(core, *weights)


def block_copies(pieces, ranges, gu, down, place, sems):
    hidden, span = pieces[0].shape[1:]
    up_copies, down_copies = [], []
    for i, (piece, (low, high)) in enumerate(zip(pieces, ranges)):
        middle = min(max(low, UP_PARTS), high)
        if low < middle:
            up_copies.append(
                pltpu.make_async_copy(
                    piece.at[pl.ds(0, middle - low)],
                    gu.at[pl.ds(low, middle - low), :, pl.ds(place * span, span)],
                    sems.at[2 * i],
                )
            )
        if middle < high:
            down_copies.append(
                pltpu.make_async_copy(
                    piece.at[pl.ds(middle - low, high - middle)],
                    down.at[pl.ds(middle - UP_PARTS, high - middle), pl.ds(place * hidden, hidden)],
                    sems.at[2 * i + 1],
                )
            )
    return up_copies, down_copies


def slot_matrix(slots, packed, slot_dim, tail):
    shape = (slots, packed) if slot_dim == 0 else (packed, slots)
    slot = lax.broadcasted_iota(jnp.int32, shape, slot_dim)
    row = lax.broadcasted_iota(jnp.int32, shape, 1 - slot_dim)
    group, place = row >> 3, row & 7
    if tail is None:
        hit = (slot == group * CAP + place) & (place < CAP)
    else:
        hit = (slot == group * CAP + (place - CAP) * 3 + tail) & (place >= CAP)
    return jnp.where(hit, 1.0, 0.0).astype(BF)


def hidden_grads(x, dy, gu, down, grads, up_copies, down_copies):
    spans, total, span = down.shape
    blocks = len(up_copies)
    hidden = total // blocks
    width = x.shape[1]
    pres = []
    for b in range(blocks):
        for copy in up_copies[b]:
            copy.wait()
        pres.append(dot(x[...], gu[:, :, b * span : (b + 1) * span].reshape(width, span)))
    for copies in down_copies:
        for copy in copies:
            copy.wait()
    back = dot_t(dy[:, :span], down[0])
    for k in range(1, spans):
        back += dot_t(dy[:, k * span : (k + 1) * span], down[k])
    terms = None
    for b in range(blocks):
        pre_gate, pre_up = pres[b][:, :hidden], pres[b][:, hidden:]
        here = back[:, b * hidden : (b + 1) * hidden]
        s = jax.nn.sigmoid(pre_gate)
        activated = pre_gate * s
        slope = s * (1.0 + pre_gate * (1.0 - s))
        low = b * span
        grads[:, low : low + hidden] = (here * pre_up * slope).astype(BF)
        grads[:, low + hidden : low + span] = (here * activated).astype(BF)
        term = activated * pre_up * here
        terms = term if terms is None else terms + term
    return terms


def row_grads(grads, gu, j):
    parts, hidden, columns = gu.shape
    rows = slice(j * parts // 4, (j + 1) * parts // 4)
    return dot_t(grads[...], gu[rows].reshape(parts // 4 * hidden, columns))


def first_kernel(ranges, *refs):
    own_hbm, other_hbm = refs[:2]
    pieces, refs = refs[2 : 2 + sum(map(len, ranges))], refs[2 + sum(map(len, ranges)) :]
    x_hbm, dy_hbm, sum_hbm, term_ref, raw, x, dy, gu, down, grads, total, sems = refs
    packed = raw.shape[1]
    slots, part = x.shape[0] // 2, x.shape[1] // 4
    raw_copies = [pltpu.make_async_copy(src, raw.at[i], sems.at[i]) for i, src in enumerate((own_hbm, other_hbm))]
    up_copies, down_copies, used = [], [], 0
    for b, block in enumerate(ranges):
        here = pieces[used : used + len(block)]
        ups, downs = block_copies(here, block, gu, down, b, sems.at[pl.ds(5 + 2 * used, 2 * len(block))])
        used += len(block)
        up_copies.append(ups)
        down_copies.append(downs)
    for copies in [raw_copies] + up_copies + down_copies:
        for copy in copies:
            copy.start()
    spread = slot_matrix(slots, packed, 0, None)
    spread_tail = [slot_matrix(slots, packed, 0, j) for j in range(3)]
    for i in range(2):
        raw_copies[i].wait()
        rows = slice(i * slots, (i + 1) * slots)
        for k, full in enumerate((x, dy)):
            cols = [slice((3 * k + j) * part, (3 * k + j + 1) * part) for j in range(3)]
            for j in range(3):
                full[rows, j * part : (j + 1) * part] = dot(spread, raw[i, :, cols[j]]).astype(BF)
            last = dot(spread_tail[0], raw[i, :, cols[0]])
            last += dot(spread_tail[1], raw[i, :, cols[1]])
            last += dot(spread_tail[2], raw[i, :, cols[2]])
            full[rows, 3 * part :] = last.astype(BF)
    outs = [
        pltpu.make_async_copy(src, dst, sems.at[2 + i])
        for i, (src, dst) in enumerate(((x, x_hbm), (dy, dy_hbm), (total, sum_hbm)))
    ]
    outs[0].start()
    outs[1].start()
    term_ref[...] = hidden_grads(x, dy, gu, down, grads, up_copies, down_copies)
    for j in range(4):
        total[:, j * part : (j + 1) * part] = row_grads(grads, gu, j).astype(BF)
    outs[2].start()
    for copy in outs:
        copy.wait()


def first_blocks(own, other, blocks, ranges, width):
    packed = own.shape[0]
    slots = packed // ROWS * CAP
    hidden, span = blocks[0][0].shape[1:]
    count = len(blocks)
    pieces = [piece for block in blocks for piece in block]
    full = jax.ShapeDtypeStruct((2 * slots, width), BF)
    any_spec = pl.BlockSpec(memory_space=pl.ANY)
    return pl.pallas_call(
        functools.partial(first_kernel, ranges),
        out_shape=(full, full, full, jax.ShapeDtypeStruct((2 * slots, hidden), F32)),
        in_specs=[any_spec] * (2 + len(pieces)),
        out_specs=(any_spec,) * 3 + (pl.BlockSpec(memory_space=pltpu.VMEM),),
        scratch_shapes=[
            pltpu.VMEM((2,) + own.shape, BF),
            pltpu.VMEM((2 * slots, width), BF),
            pltpu.VMEM((2 * slots, width), BF),
            pltpu.VMEM((UP_PARTS, hidden, count * span), BF),
            pltpu.VMEM((PARTS - UP_PARTS, count * hidden, span), BF),
            pltpu.VMEM((2 * slots, count * span), BF),
            pltpu.VMEM((2 * slots, width), BF),
            pltpu.SemaphoreType.DMA((5 + 2 * len(pieces),)),
        ],
        compiler_params=pltpu.CompilerParams(vmem_limit_bytes=VMEM_ALL),
        cost_estimate=pl.CostEstimate(
            flops=2 * 2 * slots * width * hidden * count * 5,
            bytes_accessed=2 * (count * 3 * width * hidden + 2 * own.size + 6 * slots * width),
            transcendentals=2 * slots * hidden * count,
        ),
        name="first",
    )(own, other, *pieces)


def last_kernel(ranges, *refs):
    pieces, refs = refs[: len(ranges)], refs[len(ranges) :]
    x_hbm, dy_hbm, sum_hbm, term_ref, own_ref, other_ref, x, dy, gu, down, total, grads, sems = refs
    packed = own_ref.shape[0]
    slots, part = x.shape[0] // 2, x.shape[1] // 4
    x_copy = pltpu.make_async_copy(x_hbm, x, sems.at[0])
    dy_copy = pltpu.make_async_copy(dy_hbm, dy, sems.at[1])
    sum_copy = pltpu.make_async_copy(sum_hbm, total, sems.at[2])
    up_copies, down_copies = block_copies(pieces, ranges, gu, down, 0, sems.at[pl.ds(3, 2 * len(ranges))])
    for copy in [x_copy] + up_copies + [dy_copy] + down_copies + [sum_copy]:
        copy.start()
    gather = slot_matrix(slots, packed, 1, None)
    gather_tail = [slot_matrix(slots, packed, 1, j) for j in range(3)]
    x_copy.wait()
    terms = hidden_grads(x, dy, gu, down, grads, [up_copies], [down_copies + [dy_copy]]) + term_ref[...]
    terms = jnp.broadcast_to(jnp.sum(terms, axis=1, keepdims=True), (2 * slots, TERM_LANES)).astype(BF)
    sum_copy.wait()

    def backward(j):
        return (total[:, j * part : (j + 1) * part].astype(F32) + row_grads(grads, gu, j)).astype(BF)

    outs = (own_ref, other_ref)
    spans = [slice(i * slots, (i + 1) * slots) for i in range(2)]
    for i in range(2):
        outs[i][:, 3 * part :] = dot(gather, terms[spans[i]]).astype(BF)
    last = backward(3)
    for j in range(3):
        rows = backward(j)
        for i in range(2):
            outs[i][:, j * part : (j + 1) * part] = (
                dot(gather, rows[spans[i]]) + dot(gather_tail[j], last[spans[i]])
            ).astype(BF)


def last_block(pieces, ranges, x, dy, total, term, packed):
    rows, width = x.shape
    hidden, span = pieces[0].shape[1:]
    out = jax.ShapeDtypeStruct((packed, width // 4 * 3 + TERM_LANES), BF)
    any_spec = pl.BlockSpec(memory_space=pl.ANY)
    vmem_spec = pl.BlockSpec(memory_space=pltpu.VMEM)
    return pl.pallas_call(
        functools.partial(last_kernel, ranges),
        out_shape=(out, out),
        in_specs=[any_spec] * (len(pieces) + 3) + [vmem_spec],
        out_specs=(vmem_spec, vmem_spec),
        scratch_shapes=[
            pltpu.VMEM((rows, width), BF),
            pltpu.VMEM((rows, width), BF),
            pltpu.VMEM((UP_PARTS, hidden, span), BF),
            pltpu.VMEM((PARTS - UP_PARTS, hidden, span), BF),
            pltpu.VMEM((rows, width), BF),
            pltpu.VMEM((rows, span), BF),
            pltpu.SemaphoreType.DMA((3 + 2 * len(pieces),)),
        ],
        compiler_params=pltpu.CompilerParams(vmem_limit_bytes=VMEM_ALL),
        cost_estimate=pl.CostEstimate(
            flops=2 * rows * width * hidden * 5,
            bytes_accessed=2 * (3 * width * hidden + 5 * rows * width),
            transcendentals=rows * hidden,
        ),
        name="last",
    )(*pieces, x, dy, total, term)


def combine_kernel(route_ref, gate_ref, own_term_ref, out_grad_ref, ret_ref, token_grad_ref, gate_grad_ref):
    n, width = out_grad_ref.shape
    packed = ret_ref.shape[0]
    part = width // 4
    experts = packed // ROWS
    route_row = route_ref[...]
    main, tail, block = (to_column(v) for v in places(route_row))
    routed = to_column(route_row) < experts
    gate = to_column(gate_ref[...])
    row = lax.broadcasted_iota(jnp.int32, (n, packed), 1)
    select = jnp.where(row == main, 1.0, 0.0).astype(BF)
    last = jnp.zeros((n, part), F32)
    for j in range(4):
        cols = pl.ds(j * part, part)
        if j < 3:
            tail_select = jnp.where((row == tail) & (block == j), 1.0, 0.0).astype(BF)
            piece = ret_ref[:, cols]
            rows = dot(select, piece)
            last += dot(tail_select, piece)
        else:
            rows = last
        rows = jnp.where(routed, rows, out_grad_ref[:, cols].astype(F32))
        token_grad_ref[:, cols] = (gate * rows).astype(BF)
    terms = dot(select, ret_ref[:, 3 * part :])[:, :1]
    gate_grad_ref[...] = jnp.where(route_row < experts, to_row(terms), own_term_ref[...]).astype(BF)


def combine(route_row, gate_row, own_term, out_grad, ret):
    n, width = out_grad.shape
    return pl.pallas_call(
        combine_kernel,
        out_shape=(jax.ShapeDtypeStruct((n, width), BF), jax.ShapeDtypeStruct((1, n), BF)),
        compiler_params=pltpu.CompilerParams(vmem_limit_bytes=SMALL_VMEM),
        cost_estimate=pl.CostEstimate(
            flops=2 * ret.shape[0] * n * width * 3 // 2,
            bytes_accessed=2 * (2 * out_grad.size + ret.size),
            transcendentals=0,
        ),
        name="combine",
    )(route_row, gate_row, own_term, out_grad, ret)


def per_device(tokens, out_grad, gate, route, gate_weight, up_weight, down_weight):
    experts = lax.axis_size("expert")
    groups = lax.axis_size("tensor")
    n, width = tokens.shape
    swap = [(0, 1), (1, 0)]
    up = [(i, (i + 1) % groups) for i in range(groups)]
    down = [(i, (i - 1) % groups) for i in range(groups)]
    route_row = route.reshape(1, n)

    core = lax.axis_index("dp").reshape(1)
    weights = (gate_weight[0], up_weight[0], down_weight[0])
    ends = ((0, HEAD), (PARTS - HEAD, PARTS))
    rests = ((HEAD, PARTS), (0, PARTS - HEAD))
    head, tail = weight_parts(core, weights, ends, ends)
    up_head = lax.ppermute(head, "tensor", up)
    down_tail = lax.ppermute(tail, "tensor", down)
    core, head, tail = lax.optimization_barrier((core, head, tail))
    up_rest, down_rest = weight_parts(core, weights, ((0, PARTS),), rests)

    route_row, up_rest, down_rest = lax.optimization_barrier((route_row, up_rest, down_rest))
    packed = pack(route_row, tokens, out_grad, experts)
    packed, up_head, down_tail = lax.optimization_barrier((packed, up_head, down_tail))
    got = lax.all_to_all(
        packed.reshape(experts, ROWS, -1), "expert", split_axis=0, concat_axis=0, tiled=True
    ).reshape(experts * ROWS, -1)

    from_up = lax.ppermute(up_rest, "tensor", up)
    from_down = lax.ppermute(down_rest, "tensor", down)
    far_head = lax.ppermute(up_head, "tensor", up)
    far_tail = lax.ppermute(down_tail, "tensor", down)
    got, from_up, from_down, far_head, far_tail = lax.optimization_barrier(
        (got, from_up, from_down, far_head, far_tail)
    )
    part = width // UP_PARTS
    far_up = lax.ppermute(from_up[: (HALF - HEAD) * part], "tensor", up)
    far_down = lax.ppermute(from_down[HALF * part :], "tensor", down)
    got_other = lax.ppermute(got, "dp", swap)

    squares = lambda piece: piece.reshape(-1, part, 2 * part)
    blocks = ((head, up_rest), (up_head, from_up), (from_down, down_tail))
    ranges = ((ends[0], rests[0]),) * 2 + ((rests[1], ends[1]),)
    x, dy, total, term = first_blocks(got, got_other, [list(map(squares, b)) for b in blocks], ranges, width)
    far = (far_head, far_up, far_down, far_tail)
    far_ranges = (ends[0], (HEAD, HALF), (HALF, PARTS - HEAD), ends[1])
    own, other = last_block(list(map(squares, far)), far_ranges, x, dy, total, term, experts * ROWS)
    from_other = lax.ppermute(other, "dp", swap)
    back = (own.astype(F32) + from_other.astype(F32)).astype(BF).reshape(experts, ROWS, -1)
    ret = lax.all_to_all(back, "expert", split_axis=0, concat_axis=0, tiled=True)
    own_term = jnp.sum(out_grad.astype(F32) * tokens.astype(F32), axis=1)
    token_grad, gate_grad = combine(
        route_row, gate.reshape(1, n), own_term.reshape(1, n), out_grad, ret.reshape(experts * ROWS, -1)
    )
    return token_grad, gate_grad.reshape(n)


def solution(mesh):
    rows = P(("dp", "expert", "tensor"), None)
    return jax.shard_map(
        per_device,
        mesh=mesh,
        in_specs=(
            rows,
            rows,
            P(("dp", "expert", "tensor")),
            rows,
            P("expert", None, "tensor"),
            P("expert", None, "tensor"),
            P("expert", "tensor", None),
        ),
        out_specs=(rows, P(("dp", "expert", "tensor"))),
        check_vma=False,
    )
```

```python
import functools

import jax
import jax.numpy as jnp
from jax import lax
from jax.experimental import pallas as pl
from jax.experimental.pallas import tpu as pltpu
from jax.sharding import PartitionSpec as P

BF = jnp.bfloat16
F32 = jnp.float32
CAP = 6
ROWS = 8
TERM_LANES = 128
PARTS = 60
UP_PARTS = 40
HALF = 30
HEAD = 16
ENDS = ((0, HEAD), (PARTS - HEAD, PARTS))
RESTS = ((HEAD, PARTS), (0, PARTS - HEAD))
WEIGHT_CHUNKS = (ENDS[0], ENDS[1], (HEAD, PARTS - HEAD))
FAR_FLOPS = 62000000000
FIRST_FLOPS = 1000
VMEM_ALL = 56 * 1024 * 1024
SMALL_VMEM = 20 * 1024 * 1024
FIRST_VMEM = 38 * 1024 * 1024
LAST_VMEM = 34 * 1024 * 1024
COLUMN_PIECES = 1


def dot(a, b):
    return jnp.dot(a, b, preferred_element_type=F32)


def dot_t(a, b):
    return lax.dot_general(a, b, (((1,), (1,)), ((), ())), preferred_element_type=F32)


def eye(n):
    return lax.broadcasted_iota(jnp.int32, (n, n), 0) == lax.broadcasted_iota(jnp.int32, (n, n), 1)


def to_column(row):
    n = row.shape[1]
    return jnp.sum(jnp.where(eye(n), jnp.broadcast_to(row, (n, n)), 0), axis=1, keepdims=True)


def to_row(column):
    n = column.shape[0]
    return jnp.sum(jnp.where(eye(n), jnp.broadcast_to(column, (n, n)), 0), axis=0, keepdims=True)


def places(route_row):
    n = route_row.shape[1]
    across = jnp.broadcast_to(route_row, (n, n))
    down = jnp.broadcast_to(to_column(route_row), (n, n))
    earlier = lax.broadcasted_iota(jnp.int32, (n, n), 0) < lax.broadcasted_iota(jnp.int32, (n, n), 1)
    slot = jnp.sum(jnp.where((across == down) & earlier, 1, 0), axis=0, keepdims=True)
    second = jnp.where(slot >= 3, 1, 0)
    base = route_row * ROWS
    return base + slot, base + CAP + second, slot - 3 * second


def pack_kernel(route_ref, x_ref, dy_ref, out_ref):
    n, width = x_ref.shape
    total = out_ref.shape[0]
    part = width // 4
    main, tail, block = places(route_ref[...])
    row = lax.broadcasted_iota(jnp.int32, (total, n), 0)
    select = jnp.where(row == main, 1.0, 0.0).astype(BF)
    for j in range(3):
        tail_select = jnp.where((row == tail) & (block == j), 1.0, 0.0).astype(BF)
        cols = pl.ds(j * part, part)
        for i, rows_ref in enumerate((x_ref, dy_ref)):
            last = rows_ref[:, 3 * part :]
            out_ref[:, pl.ds((3 * i + j) * part, part)] = (
                dot(select, rows_ref[:, cols]) + dot(tail_select, last)
            ).astype(BF)


def pack(route_row, x, dy, experts):
    n, width = x.shape
    return pl.pallas_call(
        pack_kernel,
        out_shape=jax.ShapeDtypeStruct((experts * ROWS, width // 4 * 6), BF),
        compiler_params=pltpu.CompilerParams(vmem_limit_bytes=VMEM_ALL),
        cost_estimate=pl.CostEstimate(
            flops=2 * experts * ROWS * n * width * 3,
            bytes_accessed=4 * width * (n + experts * CAP),
            transcendentals=0,
        ),
        name="pack",
    )(route_row, x, dy)


def part_copies(weights, core, low, high, out, sems):
    gate, up, down = weights
    hidden, span = out.shape[0] // (high - low), out.shape[1]
    columns = pl.ds(pl.multiple_of(core * hidden, hidden), hidden)
    last_up = min(high, UP_PARTS)
    copies = []
    if low < last_up:
        rows = slice(low * hidden, last_up * hidden)
        for i, ref in enumerate((gate, up)):
            dst = out.at[0 : (last_up - low) * hidden, i * hidden : (i + 1) * hidden]
            copies.append(pltpu.make_async_copy(ref.at[rows, columns], dst, sems.at[len(copies)]))
    for k in range(max(low, UP_PARTS), high):
        src = down.at[columns, (k - UP_PARTS) * span : (k - UP_PARTS + 1) * span]
        dst = out.at[(k - low) * hidden : (k - low + 1) * hidden, :]
        copies.append(pltpu.make_async_copy(src, dst, sems.at[len(copies)]))
    return copies


def weights_kernel(core_ref, gate, up, down, head, up_rest, down_rest, tail, held, read_sems, write_sems):
    hidden = held.shape[1] // 2
    reads = []
    for low, high in WEIGHT_CHUNKS:
        rows = held.at[pl.ds(low * hidden, (high - low) * hidden)]
        sems = read_sems.at[pl.ds(2 * low, 2 * (high - low))]
        reads.append(part_copies((gate, up, down), core_ref[0], low, high, rows, sems))
    writes = [
        pltpu.make_async_copy(held.at[pl.ds(low * hidden, (high - low) * hidden)], out, write_sems.at[i])
        for i, (out, (low, high)) in enumerate(
            ((head, ENDS[0]), (tail, ENDS[1]), (up_rest, RESTS[0]), (down_rest, RESTS[1]))
        )
    ]
    for copies in reads:
        for copy in copies:
            copy.start()
    for copies, write in zip(reads, writes):
        for copy in copies:
            copy.wait()
        write.start()
    writes[3].start()
    for write in writes:
        write.wait()


def weight_parts(core, weights):
    width, span = weights[0].shape
    hidden = span // 2
    any_spec = pl.BlockSpec(memory_space=pl.ANY)
    size = lambda parts: jax.ShapeDtypeStruct(((parts[1] - parts[0]) * hidden, span), BF)
    return pl.pallas_call(
        weights_kernel,
        out_shape=[size(parts) for parts in (ENDS[0],) + RESTS + (ENDS[1],)],
        in_specs=[pl.BlockSpec(memory_space=pltpu.SMEM)] + [any_spec] * 3,
        out_specs=[any_spec] * 4,
        scratch_shapes=[
            pltpu.VMEM((PARTS * hidden, span), BF),
            pltpu.SemaphoreType.DMA((2 * PARTS,)),
            pltpu.SemaphoreType.DMA((4,)),
        ],
        compiler_params=pltpu.CompilerParams(vmem_limit_bytes=VMEM_ALL),
        cost_estimate=pl.CostEstimate(flops=0, bytes_accessed=6 * PARTS * hidden * span, transcendentals=0),
        name="weights",
    )(core, *weights)


def far_kernel(ranges, up_hbm, down_hbm, *refs):
    sems = refs[-1]
    copies = []
    for i, (out, (side, low, high)) in enumerate(zip(refs[:-1], ranges)):
        hidden = out.shape[0] // (high - low)
        src = (up_hbm, down_hbm)[side].at[low * hidden : high * hidden, :]
        copies.append(pltpu.make_async_copy(src, out, sems.at[i]))
    for copy in copies:
        copy.start()
    for copy in copies:
        copy.wait()


def far_parts(from_up, from_down, ranges):
    rows, span = from_up.shape
    hidden = span // 2
    any_spec = pl.BlockSpec(memory_space=pl.ANY)
    return pl.pallas_call(
        functools.partial(far_kernel, ranges),
        out_shape=[jax.ShapeDtypeStruct(((high - low) * hidden, span), BF) for _, low, high in ranges],
        in_specs=[any_spec] * 2,
        out_specs=[any_spec] * len(ranges),
        scratch_shapes=[pltpu.SemaphoreType.DMA((len(ranges),))],
        compiler_params=pltpu.CompilerParams(vmem_limit_bytes=VMEM_ALL),
        cost_estimate=pl.CostEstimate(flops=FAR_FLOPS, bytes_accessed=0, transcendentals=0),
        name="far",
    )(from_up, from_down)


def block_copies(pieces, ranges, gu, down, place, sems):
    hidden, span = pieces[0].shape[1:]
    up_copies, down_copies = [], []
    for i, (piece, (low, high)) in enumerate(zip(pieces, ranges)):
        middle = min(max(low, UP_PARTS), high)
        if low < middle:
            up_copies.append(
                pltpu.make_async_copy(
                    piece.at[pl.ds(0, middle - low)],
                    gu.at[pl.ds(low, middle - low), :, pl.ds(place * span, span)],
                    sems.at[2 * i],
                )
            )
        if middle < high:
            down_copies.append(
                pltpu.make_async_copy(
                    piece.at[pl.ds(middle - low, high - middle)],
                    down.at[pl.ds(middle - UP_PARTS, high - middle), pl.ds(place * hidden, hidden)],
                    sems.at[2 * i + 1],
                )
            )
    return up_copies, down_copies


def slot_matrix(slots, packed, slot_dim, tail):
    shape = (slots, packed) if slot_dim == 0 else (packed, slots)
    slot = lax.broadcasted_iota(jnp.int32, shape, slot_dim)
    row = lax.broadcasted_iota(jnp.int32, shape, 1 - slot_dim)
    group, place = row >> 3, row & 7
    if tail is None:
        hit = (slot == group * CAP + place) & (place < CAP)
    else:
        hit = (slot == group * CAP + (place - CAP) * 3 + tail) & (place >= CAP)
    return jnp.where(hit, 1.0, 0.0).astype(BF)


def hidden_grads(x, dy, gu, down, grads, up_copies, down_copies):
    spans, total, span = down.shape
    blocks = len(up_copies)
    hidden = total // blocks
    width = x.shape[1]
    pres = []
    for b in range(blocks):
        for copy in up_copies[b]:
            copy.wait()
        pres.append(dot(x[...], gu[:, :, b * span : (b + 1) * span].reshape(width, span)))
    for copies in down_copies:
        for copy in copies:
            copy.wait()
    back = dot_t(dy[:, :span], down[0])
    for k in range(1, spans):
        back += dot_t(dy[:, k * span : (k + 1) * span], down[k])
    terms = None
    for b in range(blocks):
        pre_gate, pre_up = pres[b][:, :hidden], pres[b][:, hidden:]
        here = back[:, b * hidden : (b + 1) * hidden]
        s = jax.nn.sigmoid(pre_gate)
        activated = pre_gate * s
        slope = s * (1.0 + pre_gate * (1.0 - s))
        low = b * span
        grads[:, low : low + hidden] = (here * pre_up * slope).astype(BF)
        grads[:, low + hidden : low + span] = (here * activated).astype(BF)
        term = activated * pre_up * here
        terms = term if terms is None else terms + term
    return terms


def row_grads(grads, gu, j):
    parts, hidden, columns = gu.shape
    rows = slice(j * parts // 4, (j + 1) * parts // 4)
    return dot_t(grads[...], gu[rows].reshape(parts // 4 * hidden, columns))


def unpack_kernel(rows_ref, *outs):
    packed = rows_ref.shape[0]
    slots, width = outs[0].shape[0], rows_ref.shape[1] // 6 * 4
    part = width // 4
    per = len(outs) // 2
    spread = slot_matrix(slots, packed, 0, None)
    spread_tail = [slot_matrix(slots, packed, 0, j) for j in range(3)]
    for k in range(2):
        cols = [slice((3 * k + j) * part, (3 * k + j + 1) * part) for j in range(3)]
        pieces = [dot(spread, rows_ref[:, cols[j]]) for j in range(3)]
        last = dot(spread_tail[0], rows_ref[:, cols[0]])
        last += dot(spread_tail[1], rows_ref[:, cols[1]])
        last += dot(spread_tail[2], rows_ref[:, cols[2]])
        wide = width // per
        for j, piece in enumerate(pieces + [last]):
            low = j * part % wide
            outs[k * per + j * part // wide][:, low : low + part] = piece.astype(BF)


def unpack(rows):
    packed = rows.shape[0]
    slots, width = packed // ROWS * CAP, rows.shape[1] // 6 * 4
    return pl.pallas_call(
        unpack_kernel,
        out_shape=[jax.ShapeDtypeStruct((slots, width // COLUMN_PIECES), BF)] * (2 * COLUMN_PIECES),
        compiler_params=pltpu.CompilerParams(vmem_limit_bytes=SMALL_VMEM),
        cost_estimate=pl.CostEstimate(flops=FIRST_FLOPS, bytes_accessed=FIRST_FLOPS, transcendentals=0),
        name="unpack",
    )(rows)


def row_copies(pieces, full, sems):
    slots, wide = pieces[0].shape
    return [
        pltpu.make_async_copy(
            piece,
            full.at[pl.ds(i // COLUMN_PIECES * slots, slots), pl.ds(i % COLUMN_PIECES * wide, wide)],
            sems.at[i],
        )
        for i, piece in enumerate(pieces)
    ]


def first_kernel(ranges, *refs):
    count = 2 * COLUMN_PIECES
    x_pieces, dy_pieces, refs = refs[:count], refs[count : 2 * count], refs[2 * count :]
    pieces, refs = refs[: sum(map(len, ranges))], refs[sum(map(len, ranges)) :]
    sum_hbm, term_ref, x, dy, gu, down, grads, total, sems = refs
    part = x.shape[1] // 4
    x_copies = row_copies(x_pieces, x, sems.at[pl.ds(0, count)])
    dy_copies = row_copies(dy_pieces, dy, sems.at[pl.ds(count, count)])
    up_copies, down_copies, used = [], [], 0
    for b, block in enumerate(ranges):
        here = pieces[used : used + len(block)]
        ups, downs = block_copies(here, block, gu, down, b, sems.at[pl.ds(2 * count + 4 + 2 * used, 2 * len(block))])
        used += len(block)
        up_copies.append(ups)
        down_copies.append(downs)
    for copies in [x_copies] + up_copies + [dy_copies] + down_copies:
        for copy in copies:
            copy.start()
    for copy in x_copies:
        copy.wait()
    term_ref[...] = hidden_grads(x, dy, gu, down, grads, up_copies, down_copies + [dy_copies])
    outs = []
    for j in range(4):
        cols = pl.ds(j * part, part)
        total[:, cols] = row_grads(grads, gu, j).astype(BF)
        outs.append(pltpu.make_async_copy(total.at[:, cols], sum_hbm.at[:, cols], sems.at[2 * count + j]))
        outs[j].start()
    for copy in outs:
        copy.wait()


def first_blocks(x, dy, blocks, ranges):
    slots, wide = x[0].shape
    width = wide * COLUMN_PIECES
    hidden, span = blocks[0][0].shape[1:]
    count = len(blocks)
    pieces = [piece for block in blocks for piece in block]
    any_spec = pl.BlockSpec(memory_space=pl.ANY)
    return pl.pallas_call(
        functools.partial(first_kernel, ranges),
        out_shape=(jax.ShapeDtypeStruct((2 * slots, width), BF), jax.ShapeDtypeStruct((2 * slots, hidden), F32)),
        in_specs=[any_spec] * (len(x) + len(dy) + len(pieces)),
        out_specs=(any_spec, pl.BlockSpec(memory_space=pltpu.VMEM)),
        scratch_shapes=[
            pltpu.VMEM((2 * slots, width), BF),
            pltpu.VMEM((2 * slots, width), BF),
            pltpu.VMEM((UP_PARTS, hidden, count * span), BF),
            pltpu.VMEM((PARTS - UP_PARTS, count * hidden, span), BF),
            pltpu.VMEM((2 * slots, count * span), BF),
            pltpu.VMEM((2 * slots, width), BF),
            pltpu.SemaphoreType.DMA((4 * COLUMN_PIECES + 4 + 2 * len(pieces),)),
        ],
        compiler_params=pltpu.CompilerParams(vmem_limit_bytes=FIRST_VMEM),
        cost_estimate=pl.CostEstimate(flops=FIRST_FLOPS, bytes_accessed=FIRST_FLOPS, transcendentals=0),
        name="first",
    )(*x, *dy, *pieces)


def last_kernel(ranges, *refs):
    count = 2 * COLUMN_PIECES
    x_pieces, dy_pieces, refs = refs[:count], refs[count : 2 * count], refs[2 * count :]
    pieces, refs = refs[: len(ranges)], refs[len(ranges) :]
    sum_hbm, term_ref, own_ref, other_ref, x, dy, gu, down, total, grads, sems = refs
    slots, part = x.shape[0] // 2, x.shape[1] // 4
    x_copies = row_copies(x_pieces, x, sems.at[pl.ds(0, count)])
    dy_copies = row_copies(dy_pieces, dy, sems.at[pl.ds(count, count)])
    up_copies, down_copies = block_copies(pieces, ranges, gu, down, 0, sems.at[pl.ds(2 * count + 1, 2 * len(ranges))])
    sum_copy = pltpu.make_async_copy(sum_hbm, total, sems.at[2 * count])
    for copy in x_copies + up_copies + dy_copies + down_copies + [sum_copy]:
        copy.start()
    for copy in x_copies:
        copy.wait()
    terms = hidden_grads(x, dy, gu, down, grads, [up_copies], [down_copies + dy_copies]) + term_ref[...]
    terms = jnp.broadcast_to(jnp.sum(terms, axis=1, keepdims=True), (2 * slots, TERM_LANES)).astype(BF)
    own_ref[:, 4 * part :] = terms[:slots]
    other_ref[:, 4 * part :] = terms[slots:]
    sum_copy.wait()
    for j in range(4):
        cols = slice(j * part, (j + 1) * part)
        rows = (total[:, cols].astype(F32) + row_grads(grads, gu, j)).astype(BF)
        own_ref[:, cols] = rows[:slots]
        other_ref[:, cols] = rows[slots:]


def last_block(x, dy, pieces, ranges, total, term):
    rows, width = total.shape
    hidden, span = pieces[0].shape[1:]
    out = jax.ShapeDtypeStruct((rows // 2, width + TERM_LANES), BF)
    any_spec = pl.BlockSpec(memory_space=pl.ANY)
    vmem_spec = pl.BlockSpec(memory_space=pltpu.VMEM)
    return pl.pallas_call(
        functools.partial(last_kernel, ranges),
        out_shape=(out, out),
        in_specs=[any_spec] * (len(x) + len(dy) + len(pieces) + 1) + [vmem_spec],
        out_specs=(vmem_spec, vmem_spec),
        scratch_shapes=[
            pltpu.VMEM((rows, width), BF),
            pltpu.VMEM((rows, width), BF),
            pltpu.VMEM((UP_PARTS, hidden, span), BF),
            pltpu.VMEM((PARTS - UP_PARTS, hidden, span), BF),
            pltpu.VMEM((rows, width), BF),
            pltpu.VMEM((rows, span), BF),
            pltpu.SemaphoreType.DMA((4 * COLUMN_PIECES + 1 + 2 * len(pieces),)),
        ],
        compiler_params=pltpu.CompilerParams(vmem_limit_bytes=LAST_VMEM),
        cost_estimate=pl.CostEstimate(
            flops=2 * rows * width * hidden * 5,
            bytes_accessed=2 * (3 * width * hidden + 5 * rows * width),
            transcendentals=rows * hidden,
        ),
        name="last",
    )(*x, *dy, *pieces, total, term)


def add_pack_kernel(a_ref, b_ref, out_ref):
    slots, packed = a_ref.shape[0], out_ref.shape[0]
    part = (a_ref.shape[1] - TERM_LANES) // 4
    gather = slot_matrix(slots, packed, 1, None)
    gather_tail = [slot_matrix(slots, packed, 1, j) for j in range(3)]

    def total(low, size):
        cols = pl.ds(low, size)
        return (a_ref[:, cols].astype(F32) + b_ref[:, cols].astype(F32)).astype(BF)

    out_ref[:, 3 * part :] = dot(gather, total(4 * part, TERM_LANES)).astype(BF)
    last = total(3 * part, part)
    for j in range(3):
        out_ref[:, j * part : (j + 1) * part] = (
            dot(gather, total(j * part, part)) + dot(gather_tail[j], last)
        ).astype(BF)


def add_pack(a, b):
    slots, columns = a.shape
    packed, part = slots // CAP * ROWS, (columns - TERM_LANES) // 4
    return pl.pallas_call(
        add_pack_kernel,
        out_shape=jax.ShapeDtypeStruct((packed, 3 * part + TERM_LANES), BF),
        compiler_params=pltpu.CompilerParams(vmem_limit_bytes=SMALL_VMEM),
        cost_estimate=pl.CostEstimate(
            flops=2 * packed * slots * part * 6, bytes_accessed=6 * slots * columns, transcendentals=0
        ),
        name="add_pack",
    )(a, b)


def combine_kernel(route_ref, gate_ref, own_term_ref, out_grad_ref, ret_ref, token_grad_ref, gate_grad_ref):
    n, width = out_grad_ref.shape
    packed = ret_ref.shape[0]
    part = width // 4
    experts = packed // ROWS
    route_row = route_ref[...]
    main, tail, block = (to_column(v) for v in places(route_row))
    routed = to_column(route_row) < experts
    gate = to_column(gate_ref[...])
    row = lax.broadcasted_iota(jnp.int32, (n, packed), 1)
    select = jnp.where(row == main, 1.0, 0.0).astype(BF)
    last = jnp.zeros((n, part), F32)
    for j in range(4):
        cols = pl.ds(j * part, part)
        if j < 3:
            tail_select = jnp.where((row == tail) & (block == j), 1.0, 0.0).astype(BF)
            piece = ret_ref[:, cols]
            rows = dot(select, piece)
            last += dot(tail_select, piece)
        else:
            rows = last
        rows = jnp.where(routed, rows, out_grad_ref[:, cols].astype(F32))
        token_grad_ref[:, cols] = (gate * rows).astype(BF)
    terms = dot(select, ret_ref[:, 3 * part :])[:, :1]
    gate_grad_ref[...] = jnp.where(route_row < experts, to_row(terms), own_term_ref[...]).astype(BF)


def combine(route_row, gate_row, own_term, out_grad, ret):
    n, width = out_grad.shape
    return pl.pallas_call(
        combine_kernel,
        out_shape=(jax.ShapeDtypeStruct((n, width), BF), jax.ShapeDtypeStruct((1, n), BF)),
        compiler_params=pltpu.CompilerParams(vmem_limit_bytes=SMALL_VMEM),
        cost_estimate=pl.CostEstimate(
            flops=2 * ret.shape[0] * n * width * 3 // 2,
            bytes_accessed=2 * (2 * out_grad.size + ret.size),
            transcendentals=0,
        ),
        name="combine",
    )(route_row, gate_row, own_term, out_grad, ret)


def per_device(tokens, out_grad, gate, route, gate_weight, up_weight, down_weight):
    experts = lax.axis_size("expert")
    groups = lax.axis_size("tensor")
    n, width = tokens.shape
    swap = [(0, 1), (1, 0)]
    up = [(i, (i + 1) % groups) for i in range(groups)]
    down = [(i, (i - 1) % groups) for i in range(groups)]
    route_row = route.reshape(1, n)

    core = lax.axis_index("dp").reshape(1)
    weights = (gate_weight[0], up_weight[0], down_weight[0])
    head, up_rest, down_rest, tail = weight_parts(core, weights)
    up_head = lax.ppermute(head, "tensor", up)
    down_tail = lax.ppermute(tail, "tensor", down)
    from_up = lax.ppermute(up_rest, "tensor", up)
    from_down = lax.ppermute(down_rest, "tensor", down)
    far_head = lax.ppermute(up_head, "tensor", up)
    far_tail = lax.ppermute(down_tail, "tensor", down)

    route_row, head = lax.optimization_barrier((route_row, head))
    packed = pack(route_row, tokens, out_grad, experts)
    got = lax.all_to_all(
        packed.reshape(experts, ROWS, -1), "expert", split_axis=0, concat_axis=0, tiled=True
    ).reshape(experts * ROWS, -1)

    from_up, from_down, far_head, far_tail = lax.optimization_barrier((from_up, from_down, far_head, far_tail))
    far_up, far_down = far_parts(from_up, from_down, ((0, 0, HALF - HEAD), (1, HALF, PARTS - HEAD)))
    got, far_up, far_down = lax.optimization_barrier((got, far_up, far_down))
    far_up = lax.ppermute(far_up, "tensor", up)
    far_down = lax.ppermute(far_down, "tensor", down)
    rows = list(unpack(got))
    other_rows = [lax.ppermute(piece, "dp", swap) for piece in rows]
    x = rows[:COLUMN_PIECES] + other_rows[:COLUMN_PIECES]
    dy = rows[COLUMN_PIECES:] + other_rows[COLUMN_PIECES:]

    part = width // UP_PARTS
    squares = lambda piece: piece.reshape(-1, part, 2 * part)
    blocks = [list(map(squares, b)) for b in ((head, up_rest), (up_head, from_up), (from_down, down_tail))]
    ranges = ((ENDS[0], RESTS[0]),) * 2 + ((RESTS[1], ENDS[1]),)
    far = (far_head, far_up, far_down, far_tail)
    far_ranges = (ENDS[0], (HEAD, HALF), (HALF, PARTS - HEAD), ENDS[1])
    total, term = first_blocks(x, dy, blocks, ranges)
    own, other = last_block(x, dy, list(map(squares, far)), far_ranges, total, term)
    back = add_pack(own, lax.ppermute(other, "dp", swap)).reshape(experts, ROWS, -1)
    ret = lax.all_to_all(back, "expert", split_axis=0, concat_axis=0, tiled=True)
    own_term = jnp.sum(out_grad.astype(F32) * tokens.astype(F32), axis=1)
    token_grad, gate_grad = combine(
        route_row, gate.reshape(1, n), own_term.reshape(1, n), out_grad, ret.reshape(experts * ROWS, -1)
    )
    return token_grad, gate_grad.reshape(n)


def solution(mesh):
    rows = P(("dp", "expert", "tensor"), None)
    return jax.shard_map(
        per_device,
        mesh=mesh,
        in_specs=(
            rows,
            rows,
            P(("dp", "expert", "tensor")),
            rows,
            P("expert", None, "tensor"),
            P("expert", None, "tensor"),
            P("expert", "tensor", None),
        ),
        out_specs=(rows, P(("dp", "expert", "tensor"))),
        check_vma=False,
    )
```

```python
import functools

import jax
import jax.numpy as jnp
from jax import lax
from jax.experimental import pallas as pl
from jax.experimental.pallas import tpu as pltpu
from jax.sharding import PartitionSpec as P

BF = jnp.bfloat16
F32 = jnp.float32
CAP = 6
ROWS = 8
TERM_LANES = 128
PARTS = 60
UP_PARTS = 40
HALF = 30
HEAD = 15
ENDS = ((0, HEAD), (PARTS - HEAD, PARTS))
RESTS = ((HEAD, PARTS), (0, PARTS - HEAD))
WEIGHT_CHUNKS = (ENDS[0], ENDS[1], (HEAD, PARTS - HEAD))
FAR_FLOPS = 62000000000
FIRST_FLOPS = 1000
VMEM_ALL = 56 * 1024 * 1024
SMALL_VMEM = 20 * 1024 * 1024
FIRST_VMEM = 46 * 1024 * 1024
LAST_VMEM = 46 * 1024 * 1024
COLUMN_PIECES = 1


def dot(a, b):
    return jnp.dot(a, b, preferred_element_type=F32)


def dot_t(a, b):
    return lax.dot_general(a, b, (((1,), (1,)), ((), ())), preferred_element_type=F32)


def eye(n):
    return lax.broadcasted_iota(jnp.int32, (n, n), 0) == lax.broadcasted_iota(jnp.int32, (n, n), 1)


def to_column(row):
    n = row.shape[1]
    return jnp.sum(jnp.where(eye(n), jnp.broadcast_to(row, (n, n)), 0), axis=1, keepdims=True)


def to_row(column):
    n = column.shape[0]
    return jnp.sum(jnp.where(eye(n), jnp.broadcast_to(column, (n, n)), 0), axis=0, keepdims=True)


def places(route_row):
    n = route_row.shape[1]
    across = jnp.broadcast_to(route_row, (n, n))
    down = jnp.broadcast_to(to_column(route_row), (n, n))
    earlier = lax.broadcasted_iota(jnp.int32, (n, n), 0) < lax.broadcasted_iota(jnp.int32, (n, n), 1)
    slot = jnp.sum(jnp.where((across == down) & earlier, 1, 0), axis=0, keepdims=True)
    second = jnp.where(slot >= 3, 1, 0)
    base = route_row * ROWS
    return base + slot, base + CAP + second, slot - 3 * second


def pack_kernel(route_ref, x_ref, dy_ref, out_ref):
    n, width = x_ref.shape
    total = out_ref.shape[0]
    part = width // 4
    main, tail, block = places(route_ref[...])
    row = lax.broadcasted_iota(jnp.int32, (total, n), 0)
    select = jnp.where(row == main, 1.0, 0.0).astype(BF)
    for j in range(3):
        tail_select = jnp.where((row == tail) & (block == j), 1.0, 0.0).astype(BF)
        cols = pl.ds(j * part, part)
        for i, rows_ref in enumerate((x_ref, dy_ref)):
            last = rows_ref[:, 3 * part :]
            out_ref[:, pl.ds((3 * i + j) * part, part)] = (
                dot(select, rows_ref[:, cols]) + dot(tail_select, last)
            ).astype(BF)


def pack(route_row, x, dy, experts):
    n, width = x.shape
    return pl.pallas_call(
        pack_kernel,
        out_shape=jax.ShapeDtypeStruct((experts * ROWS, width // 4 * 6), BF),
        compiler_params=pltpu.CompilerParams(vmem_limit_bytes=VMEM_ALL),
        cost_estimate=pl.CostEstimate(
            flops=2 * experts * ROWS * n * width * 3,
            bytes_accessed=4 * width * (n + experts * CAP),
            transcendentals=0,
        ),
        name="pack",
    )(route_row, x, dy)


def part_copies(weights, core, low, high, out, sems):
    gate, up, down = weights
    hidden, span = out.shape[0] // (high - low), out.shape[1]
    columns = pl.ds(pl.multiple_of(core * hidden, hidden), hidden)
    last_up = min(high, UP_PARTS)
    copies = []
    if low < last_up:
        rows = slice(low * hidden, last_up * hidden)
        for i, ref in enumerate((gate, up)):
            dst = out.at[0 : (last_up - low) * hidden, i * hidden : (i + 1) * hidden]
            copies.append(pltpu.make_async_copy(ref.at[rows, columns], dst, sems.at[len(copies)]))
    for k in range(max(low, UP_PARTS), high):
        src = down.at[columns, (k - UP_PARTS) * span : (k - UP_PARTS + 1) * span]
        dst = out.at[(k - low) * hidden : (k - low + 1) * hidden, :]
        copies.append(pltpu.make_async_copy(src, dst, sems.at[len(copies)]))
    return copies


def weights_kernel(core_ref, gate, up, down, head, up_rest, down_rest, tail, held, read_sems, write_sems):
    hidden = held.shape[1] // 2
    reads = []
    for low, high in WEIGHT_CHUNKS:
        rows = held.at[pl.ds(low * hidden, (high - low) * hidden)]
        sems = read_sems.at[pl.ds(2 * low, 2 * (high - low))]
        reads.append(part_copies((gate, up, down), core_ref[0], low, high, rows, sems))
    writes = [
        pltpu.make_async_copy(held.at[pl.ds(low * hidden, (high - low) * hidden)], out, write_sems.at[i])
        for i, (out, (low, high)) in enumerate(
            ((head, ENDS[0]), (tail, ENDS[1]), (up_rest, RESTS[0]), (down_rest, RESTS[1]))
        )
    ]
    for copies in reads:
        for copy in copies:
            copy.start()
    for copies, write in zip(reads, writes):
        for copy in copies:
            copy.wait()
        write.start()
    writes[3].start()
    for write in writes:
        write.wait()


def weight_parts(core, weights):
    width, span = weights[0].shape
    hidden = span // 2
    any_spec = pl.BlockSpec(memory_space=pl.ANY)
    size = lambda parts: jax.ShapeDtypeStruct(((parts[1] - parts[0]) * hidden, span), BF)
    return pl.pallas_call(
        weights_kernel,
        out_shape=[size(parts) for parts in (ENDS[0],) + RESTS + (ENDS[1],)],
        in_specs=[pl.BlockSpec(memory_space=pltpu.SMEM)] + [any_spec] * 3,
        out_specs=[any_spec] * 4,
        scratch_shapes=[
            pltpu.VMEM((PARTS * hidden, span), BF),
            pltpu.SemaphoreType.DMA((2 * PARTS,)),
            pltpu.SemaphoreType.DMA((4,)),
        ],
        compiler_params=pltpu.CompilerParams(vmem_limit_bytes=VMEM_ALL),
        cost_estimate=pl.CostEstimate(flops=0, bytes_accessed=6 * PARTS * hidden * span, transcendentals=0),
        name="weights",
    )(core, *weights)


def far_kernel(ranges, up_hbm, down_hbm, *refs):
    count = len(ranges)
    outs, held, sems = refs[:count], refs[count : 2 * count], refs[-1]
    reads, writes = [], []
    for i, (side, low, high) in enumerate(ranges):
        hidden = outs[i].shape[0] // (high - low)
        src = (up_hbm, down_hbm)[side].at[low * hidden : high * hidden, :]
        reads.append(pltpu.make_async_copy(src, held[i], sems.at[i]))
        writes.append(pltpu.make_async_copy(held[i], outs[i], sems.at[count + i]))
    for read in reads:
        read.start()
    for read, write in zip(reads, writes):
        read.wait()
        write.start()
    for write in writes:
        write.wait()


def far_parts(from_up, from_down, ranges):
    rows, span = from_up.shape
    hidden = span // 2
    any_spec = pl.BlockSpec(memory_space=pl.ANY)
    return pl.pallas_call(
        functools.partial(far_kernel, ranges),
        out_shape=[jax.ShapeDtypeStruct(((high - low) * hidden, span), BF) for _, low, high in ranges],
        in_specs=[any_spec] * 2,
        out_specs=[any_spec] * len(ranges),
        scratch_shapes=[pltpu.VMEM(((high - low) * hidden, span), BF) for _, low, high in ranges]
        + [pltpu.SemaphoreType.DMA((2 * len(ranges),))],
        compiler_params=pltpu.CompilerParams(vmem_limit_bytes=VMEM_ALL),
        cost_estimate=pl.CostEstimate(flops=FAR_FLOPS, bytes_accessed=0, transcendentals=0),
        name="far",
    )(from_up, from_down)


def block_copies(pieces, ranges, gu, down, place, sems):
    hidden, span = pieces[0].shape[1:]
    up_copies, down_copies = [], []
    for i, (piece, (low, high)) in enumerate(zip(pieces, ranges)):
        middle = min(max(low, UP_PARTS), high)
        if low < middle:
            up_copies.append(
                pltpu.make_async_copy(
                    piece.at[pl.ds(0, middle - low)],
                    gu.at[pl.ds(low, middle - low), :, pl.ds(place * span, span)],
                    sems.at[2 * i],
                )
            )
        if middle < high:
            down_copies.append(
                pltpu.make_async_copy(
                    piece.at[pl.ds(middle - low, high - middle)],
                    down.at[pl.ds(middle - UP_PARTS, high - middle), pl.ds(place * hidden, hidden)],
                    sems.at[2 * i + 1],
                )
            )
    return up_copies, down_copies


def slot_matrix(slots, packed, slot_dim, tail):
    shape = (slots, packed) if slot_dim == 0 else (packed, slots)
    slot = lax.broadcasted_iota(jnp.int32, shape, slot_dim)
    row = lax.broadcasted_iota(jnp.int32, shape, 1 - slot_dim)
    group, place = row >> 3, row & 7
    if tail is None:
        hit = (slot == group * CAP + place) & (place < CAP)
    else:
        hit = (slot == group * CAP + (place - CAP) * 3 + tail) & (place >= CAP)
    return jnp.where(hit, 1.0, 0.0).astype(BF)


def hidden_grads(x, dy, gu, down, grads, up_copies, down_copies):
    spans, total, span = down.shape
    blocks = len(up_copies)
    hidden = total // blocks
    width = x.shape[1]
    pres = []
    for b in range(blocks):
        for copy in up_copies[b]:
            copy.wait()
        pres.append(dot(x[...], gu[:, :, b * span : (b + 1) * span].reshape(width, span)))
    for copies in down_copies:
        for copy in copies:
            copy.wait()
    back = dot_t(dy[:, :span], down[0])
    for k in range(1, spans):
        back += dot_t(dy[:, k * span : (k + 1) * span], down[k])
    terms = None
    for b in range(blocks):
        pre_gate, pre_up = pres[b][:, :hidden], pres[b][:, hidden:]
        here = back[:, b * hidden : (b + 1) * hidden]
        s = jax.nn.sigmoid(pre_gate)
        activated = pre_gate * s
        slope = s * (1.0 + pre_gate * (1.0 - s))
        low = b * span
        grads[:, low : low + hidden] = (here * pre_up * slope).astype(BF)
        grads[:, low + hidden : low + span] = (here * activated).astype(BF)
        term = activated * pre_up * here
        terms = term if terms is None else terms + term
    return terms


def row_grads(grads, gu, j):
    parts, hidden, columns = gu.shape
    rows = slice(j * parts // 4, (j + 1) * parts // 4)
    return dot_t(grads[...], gu[rows].reshape(parts // 4 * hidden, columns))


def unpack_kernel(rows_ref, *outs):
    packed = rows_ref.shape[0]
    slots, width = outs[0].shape[0], rows_ref.shape[1] // 6 * 4
    part = width // 4
    per = len(outs) // 2
    spread = slot_matrix(slots, packed, 0, None)
    spread_tail = [slot_matrix(slots, packed, 0, j) for j in range(3)]
    for k in range(2):
        cols = [slice((3 * k + j) * part, (3 * k + j + 1) * part) for j in range(3)]
        pieces = [dot(spread, rows_ref[:, cols[j]]) for j in range(3)]
        last = dot(spread_tail[0], rows_ref[:, cols[0]])
        last += dot(spread_tail[1], rows_ref[:, cols[1]])
        last += dot(spread_tail[2], rows_ref[:, cols[2]])
        wide = width // per
        for j, piece in enumerate(pieces + [last]):
            low = j * part % wide
            outs[k * per + j * part // wide][:, low : low + part] = piece.astype(BF)


def unpack(rows):
    packed = rows.shape[0]
    slots, width = packed // ROWS * CAP, rows.shape[1] // 6 * 4
    return pl.pallas_call(
        unpack_kernel,
        out_shape=[jax.ShapeDtypeStruct((slots, width // COLUMN_PIECES), BF)] * (2 * COLUMN_PIECES),
        compiler_params=pltpu.CompilerParams(vmem_limit_bytes=SMALL_VMEM),
        cost_estimate=pl.CostEstimate(flops=FIRST_FLOPS, bytes_accessed=FIRST_FLOPS, transcendentals=0),
        name="unpack",
    )(rows)


def row_copies(pieces, full, sems):
    slots, wide = pieces[0].shape
    return [
        pltpu.make_async_copy(
            piece,
            full.at[pl.ds(i // COLUMN_PIECES * slots, slots), pl.ds(i % COLUMN_PIECES * wide, wide)],
            sems.at[i],
        )
        for i, piece in enumerate(pieces)
    ]


def first_kernel(ranges, *refs):
    count = 2 * COLUMN_PIECES
    x_pieces, dy_pieces, refs = refs[:count], refs[count : 2 * count], refs[2 * count :]
    pieces, refs = refs[: sum(map(len, ranges))], refs[sum(map(len, ranges)) :]
    sum_hbm, term_ref, x, dy, gu, down, grads, total, sems = refs
    part = x.shape[1] // 4
    x_copies = row_copies(x_pieces, x, sems.at[pl.ds(0, count)])
    dy_copies = row_copies(dy_pieces, dy, sems.at[pl.ds(count, count)])
    up_copies, down_copies, used = [], [], 0
    for b, block in enumerate(ranges):
        here = pieces[used : used + len(block)]
        ups, downs = block_copies(here, block, gu, down, b, sems.at[pl.ds(2 * count + 4 + 2 * used, 2 * len(block))])
        used += len(block)
        up_copies.append(ups)
        down_copies.append(downs)
    for copies in [x_copies] + up_copies + [dy_copies] + down_copies:
        for copy in copies:
            copy.start()
    for copy in x_copies:
        copy.wait()
    term_ref[...] = hidden_grads(x, dy, gu, down, grads, up_copies, down_copies + [dy_copies])
    outs = []
    for j in range(4):
        cols = pl.ds(j * part, part)
        total[:, cols] = row_grads(grads, gu, j).astype(BF)
        outs.append(pltpu.make_async_copy(total.at[:, cols], sum_hbm.at[:, cols], sems.at[2 * count + j]))
        outs[j].start()
    for copy in outs:
        copy.wait()


def first_blocks(x, dy, blocks, ranges):
    slots, wide = x[0].shape
    width = wide * COLUMN_PIECES
    hidden, span = blocks[0][0].shape[1:]
    count = len(blocks)
    pieces = [piece for block in blocks for piece in block]
    any_spec = pl.BlockSpec(memory_space=pl.ANY)
    return pl.pallas_call(
        functools.partial(first_kernel, ranges),
        out_shape=(jax.ShapeDtypeStruct((2 * slots, width), BF), jax.ShapeDtypeStruct((2 * slots, hidden), F32)),
        in_specs=[any_spec] * (len(x) + len(dy) + len(pieces)),
        out_specs=(any_spec, pl.BlockSpec(memory_space=pltpu.VMEM)),
        scratch_shapes=[
            pltpu.VMEM((2 * slots, width), BF),
            pltpu.VMEM((2 * slots, width), BF),
            pltpu.VMEM((UP_PARTS, hidden, count * span), BF),
            pltpu.VMEM((PARTS - UP_PARTS, count * hidden, span), BF),
            pltpu.VMEM((2 * slots, count * span), BF),
            pltpu.VMEM((2 * slots, width), BF),
            pltpu.SemaphoreType.DMA((4 * COLUMN_PIECES + 4 + 2 * len(pieces),)),
        ],
        compiler_params=pltpu.CompilerParams(vmem_limit_bytes=FIRST_VMEM),
        cost_estimate=pl.CostEstimate(flops=FIRST_FLOPS, bytes_accessed=FIRST_FLOPS, transcendentals=0),
        name="first",
    )(*x, *dy, *pieces)


def last_kernel(ranges, *refs):
    count = 2 * COLUMN_PIECES
    x_pieces, dy_pieces, refs = refs[:count], refs[count : 2 * count], refs[2 * count :]
    pieces, refs = refs[: len(ranges)], refs[len(ranges) :]
    sum_hbm, term_ref, own_ref, other_ref, x, dy, gu, down, total, grads, sems = refs
    slots, part = x.shape[0] // 2, x.shape[1] // 4
    x_copies = row_copies(x_pieces, x, sems.at[pl.ds(0, count)])
    dy_copies = row_copies(dy_pieces, dy, sems.at[pl.ds(count, count)])
    up_copies, down_copies = block_copies(pieces, ranges, gu, down, 0, sems.at[pl.ds(2 * count + 1, 2 * len(ranges))])
    sum_copy = pltpu.make_async_copy(sum_hbm, total, sems.at[2 * count])
    for copy in x_copies + up_copies + dy_copies + down_copies + [sum_copy]:
        copy.start()
    for copy in x_copies:
        copy.wait()
    terms = hidden_grads(x, dy, gu, down, grads, [up_copies], [down_copies + dy_copies]) + term_ref[...]
    terms = jnp.broadcast_to(jnp.sum(terms, axis=1, keepdims=True), (2 * slots, TERM_LANES)).astype(BF)
    own_ref[:, 4 * part :] = terms[:slots]
    other_ref[:, 4 * part :] = terms[slots:]
    sum_copy.wait()
    for j in range(4):
        cols = slice(j * part, (j + 1) * part)
        rows = (total[:, cols].astype(F32) + row_grads(grads, gu, j)).astype(BF)
        own_ref[:, cols] = rows[:slots]
        other_ref[:, cols] = rows[slots:]


def last_block(x, dy, pieces, ranges, total, term):
    rows, width = total.shape
    hidden, span = pieces[0].shape[1:]
    out = jax.ShapeDtypeStruct((rows // 2, width + TERM_LANES), BF)
    any_spec = pl.BlockSpec(memory_space=pl.ANY)
    vmem_spec = pl.BlockSpec(memory_space=pltpu.VMEM)
    return pl.pallas_call(
        functools.partial(last_kernel, ranges),
        out_shape=(out, out),
        in_specs=[any_spec] * (len(x) + len(dy) + len(pieces) + 1) + [vmem_spec],
        out_specs=(vmem_spec, vmem_spec),
        scratch_shapes=[
            pltpu.VMEM((rows, width), BF),
            pltpu.VMEM((rows, width), BF),
            pltpu.VMEM((UP_PARTS, hidden, span), BF),
            pltpu.VMEM((PARTS - UP_PARTS, hidden, span), BF),
            pltpu.VMEM((rows, width), BF),
            pltpu.VMEM((rows, span), BF),
            pltpu.SemaphoreType.DMA((4 * COLUMN_PIECES + 1 + 2 * len(pieces),)),
        ],
        compiler_params=pltpu.CompilerParams(vmem_limit_bytes=LAST_VMEM),
        cost_estimate=pl.CostEstimate(
            flops=2 * rows * width * hidden * 5,
            bytes_accessed=2 * (3 * width * hidden + 5 * rows * width),
            transcendentals=rows * hidden,
        ),
        name="last",
    )(*x, *dy, *pieces, total, term)


def add_pack_kernel(a_ref, b_ref, out_ref):
    slots, packed = a_ref.shape[0], out_ref.shape[0]
    part = (a_ref.shape[1] - TERM_LANES) // 4
    gather = slot_matrix(slots, packed, 1, None)
    gather_tail = [slot_matrix(slots, packed, 1, j) for j in range(3)]

    def total(low, size):
        cols = pl.ds(low, size)
        return (a_ref[:, cols].astype(F32) + b_ref[:, cols].astype(F32)).astype(BF)

    out_ref[:, 3 * part :] = dot(gather, total(4 * part, TERM_LANES)).astype(BF)
    last = total(3 * part, part)
    for j in range(3):
        out_ref[:, j * part : (j + 1) * part] = (
            dot(gather, total(j * part, part)) + dot(gather_tail[j], last)
        ).astype(BF)


def add_pack(a, b):
    slots, columns = a.shape
    packed, part = slots // CAP * ROWS, (columns - TERM_LANES) // 4
    return pl.pallas_call(
        add_pack_kernel,
        out_shape=jax.ShapeDtypeStruct((packed, 3 * part + TERM_LANES), BF),
        compiler_params=pltpu.CompilerParams(vmem_limit_bytes=SMALL_VMEM),
        cost_estimate=pl.CostEstimate(
            flops=2 * packed * slots * part * 6, bytes_accessed=6 * slots * columns, transcendentals=0
        ),
        name="add_pack",
    )(a, b)


def combine_kernel(route_ref, gate_ref, own_term_ref, out_grad_ref, ret_ref, token_grad_ref, gate_grad_ref):
    n, width = out_grad_ref.shape
    packed = ret_ref.shape[0]
    part = width // 4
    experts = packed // ROWS
    route_row = route_ref[...]
    main, tail, block = (to_column(v) for v in places(route_row))
    routed = to_column(route_row) < experts
    gate = to_column(gate_ref[...])
    row = lax.broadcasted_iota(jnp.int32, (n, packed), 1)
    select = jnp.where(row == main, 1.0, 0.0).astype(BF)
    last = jnp.zeros((n, part), F32)
    for j in range(4):
        cols = pl.ds(j * part, part)
        if j < 3:
            tail_select = jnp.where((row == tail) & (block == j), 1.0, 0.0).astype(BF)
            piece = ret_ref[:, cols]
            rows = dot(select, piece)
            last += dot(tail_select, piece)
        else:
            rows = last
        rows = jnp.where(routed, rows, out_grad_ref[:, cols].astype(F32))
        token_grad_ref[:, cols] = (gate * rows).astype(BF)
    terms = dot(select, ret_ref[:, 3 * part :])[:, :1]
    gate_grad_ref[...] = jnp.where(route_row < experts, to_row(terms), own_term_ref[...]).astype(BF)


def combine(route_row, gate_row, own_term, out_grad, ret):
    n, width = out_grad.shape
    return pl.pallas_call(
        combine_kernel,
        out_shape=(jax.ShapeDtypeStruct((n, width), BF), jax.ShapeDtypeStruct((1, n), BF)),
        compiler_params=pltpu.CompilerParams(vmem_limit_bytes=SMALL_VMEM),
        cost_estimate=pl.CostEstimate(
            flops=2 * ret.shape[0] * n * width * 3 // 2,
            bytes_accessed=2 * (2 * out_grad.size + ret.size),
            transcendentals=0,
        ),
        name="combine",
    )(route_row, gate_row, own_term, out_grad, ret)


def per_device(tokens, out_grad, gate, route, gate_weight, up_weight, down_weight):
    experts = lax.axis_size("expert")
    groups = lax.axis_size("tensor")
    n, width = tokens.shape
    swap = [(0, 1), (1, 0)]
    up = [(i, (i + 1) % groups) for i in range(groups)]
    down = [(i, (i - 1) % groups) for i in range(groups)]
    route_row = route.reshape(1, n)

    core = lax.axis_index("dp").reshape(1)
    weights = (gate_weight[0], up_weight[0], down_weight[0])
    head, up_rest, down_rest, tail = weight_parts(core, weights)
    up_head = lax.ppermute(head, "tensor", up)
    down_tail = lax.ppermute(tail, "tensor", down)
    from_up = lax.ppermute(up_rest, "tensor", up)
    from_down = lax.ppermute(down_rest, "tensor", down)
    far_head = lax.ppermute(up_head, "tensor", up)
    far_tail = lax.ppermute(down_tail, "tensor", down)

    route_row, head = lax.optimization_barrier((route_row, head))
    packed = pack(route_row, tokens, out_grad, experts)
    got = lax.all_to_all(
        packed.reshape(experts, ROWS, -1), "expert", split_axis=0, concat_axis=0, tiled=True
    ).reshape(experts * ROWS, -1)

    far_up, far_down = far_parts(from_up, from_down, ((0, 0, HALF - HEAD), (1, HALF, PARTS - HEAD)))
    got, far_up, far_down, far_head, far_tail = lax.optimization_barrier(
        (got, far_up, far_down, far_head, far_tail)
    )
    far_up = lax.ppermute(far_up, "tensor", up)
    far_down = lax.ppermute(far_down, "tensor", down)
    rows = list(unpack(got))
    other_rows = [lax.ppermute(piece, "dp", swap) for piece in rows]
    x = rows[:COLUMN_PIECES] + other_rows[:COLUMN_PIECES]
    dy = rows[COLUMN_PIECES:] + other_rows[COLUMN_PIECES:]

    part = width // UP_PARTS
    squares = lambda piece: piece.reshape(-1, part, 2 * part)
    blocks = [list(map(squares, b)) for b in ((head, up_rest), (up_head, from_up), (from_down, down_tail))]
    ranges = ((ENDS[0], RESTS[0]),) * 2 + ((RESTS[1], ENDS[1]),)
    far = (far_head, far_up, far_down, far_tail)
    far_ranges = (ENDS[0], (HEAD, HALF), (HALF, PARTS - HEAD), ENDS[1])
    total, term = first_blocks(x, dy, blocks, ranges)
    own, other = last_block(x, dy, list(map(squares, far)), far_ranges, total, term)
    back = add_pack(own, lax.ppermute(other, "dp", swap)).reshape(experts, ROWS, -1)
    ret = lax.all_to_all(back, "expert", split_axis=0, concat_axis=0, tiled=True)
    own_term = jnp.sum(out_grad.astype(F32) * tokens.astype(F32), axis=1)
    token_grad, gate_grad = combine(
        route_row, gate.reshape(1, n), own_term.reshape(1, n), out_grad, ret.reshape(experts * ROWS, -1)
    )
    return token_grad, gate_grad.reshape(n)


def solution(mesh):
    rows = P(("dp", "expert", "tensor"), None)
    return jax.shard_map(
        per_device,
        mesh=mesh,
        in_specs=(
            rows,
            rows,
            P(("dp", "expert", "tensor")),
            rows,
            P("expert", None, "tensor"),
            P("expert", None, "tensor"),
            P("expert", "tensor", None),
        ),
        out_specs=(rows, P(("dp", "expert", "tensor"))),
        check_vma=False,
    )
```

```python
import functools

import jax
import jax.numpy as jnp
from jax import lax
from jax.experimental import pallas as pl
from jax.experimental.pallas import tpu as pltpu
from jax.sharding import PartitionSpec as P

BF = jnp.bfloat16
F32 = jnp.float32
CAP = 6
ROWS = 8
TERM_LANES = 128
PARTS = 60
UP_PARTS = 40
HALF = 30
HEAD = 15
ENDS = ((0, HEAD), (PARTS - HEAD, PARTS))
RESTS = ((HEAD, PARTS), (0, PARTS - HEAD))
MIDDLE = (PARTS - 2 * HEAD) // 3
WEIGHT_CUTS = (0, HEAD, HEAD + MIDDLE, HEAD + 2 * MIDDLE, PARTS - HEAD, PARTS)
FAR_FLOPS = 62000000000
FIRST_FLOPS = 1000
LAST_FLOPS = 1000
VMEM_ALL = 56 * 1024 * 1024
SMALL_VMEM = 20 * 1024 * 1024
FIRST_VMEM = 28 * 1024 * 1024
LAST_VMEM = 20 * 1024 * 1024
COLUMN_PIECES = 1


def dot(a, b):
    return jnp.dot(a, b, preferred_element_type=F32)


def dot_t(a, b):
    return lax.dot_general(a, b, (((1,), (1,)), ((), ())), preferred_element_type=F32)


def eye(n):
    return lax.broadcasted_iota(jnp.int32, (n, n), 0) == lax.broadcasted_iota(jnp.int32, (n, n), 1)


def to_column(row):
    n = row.shape[1]
    return jnp.sum(jnp.where(eye(n), jnp.broadcast_to(row, (n, n)), 0), axis=1, keepdims=True)


def to_row(column):
    n = column.shape[0]
    return jnp.sum(jnp.where(eye(n), jnp.broadcast_to(column, (n, n)), 0), axis=0, keepdims=True)


def places(route_row):
    n = route_row.shape[1]
    across = jnp.broadcast_to(route_row, (n, n))
    down = jnp.broadcast_to(to_column(route_row), (n, n))
    earlier = lax.broadcasted_iota(jnp.int32, (n, n), 0) < lax.broadcasted_iota(jnp.int32, (n, n), 1)
    slot = jnp.sum(jnp.where((across == down) & earlier, 1, 0), axis=0, keepdims=True)
    second = jnp.where(slot >= 3, 1, 0)
    base = route_row * ROWS
    return base + slot, base + CAP + second, slot - 3 * second


def pack_kernel(route_ref, x_hbm, dy_hbm, out_hbm, x, dy, out, in_sems, out_sems):
    n, width = x.shape
    total = out.shape[0]
    part = width // 4
    columns = [pl.ds(j * part, part) for j in range(4)]
    reads = [
        [pltpu.make_async_copy(src.at[:, columns[j]], dst.at[:, columns[j]], in_sems.at[4 * i + j]) for j in range(4)]
        for i, (src, dst) in enumerate(((x_hbm, x), (dy_hbm, dy)))
    ]
    for copies in reads:
        for j in (3, 0, 1, 2):
            copies[j].start()
    main, tail, block = places(route_ref[...])
    row = lax.broadcasted_iota(jnp.int32, (total, n), 0)
    select = jnp.where(row == main, 1.0, 0.0).astype(BF)
    tail_select = [jnp.where((row == tail) & (block == j), 1.0, 0.0).astype(BF) for j in range(3)]
    writes = []
    for i, rows in enumerate((x, dy)):
        reads[i][3].wait()
        for j in range(3):
            reads[i][j].wait()
            cols = pl.ds((3 * i + j) * part, part)
            out[:, cols] = (dot(select, rows[:, columns[j]]) + dot(tail_select[j], rows[:, columns[3]])).astype(BF)
            writes.append(pltpu.make_async_copy(out.at[:, cols], out_hbm.at[:, cols], out_sems.at[3 * i + j]))
            writes[-1].start()
    for write in writes:
        write.wait()


def pack(route_row, x, dy, experts):
    n, width = x.shape
    shape = (experts * ROWS, width // 4 * 6)
    any_spec = pl.BlockSpec(memory_space=pl.ANY)
    return pl.pallas_call(
        pack_kernel,
        out_shape=jax.ShapeDtypeStruct(shape, BF),
        in_specs=[pl.BlockSpec(memory_space=pltpu.VMEM), any_spec, any_spec],
        out_specs=any_spec,
        scratch_shapes=[
            pltpu.VMEM((n, width), BF),
            pltpu.VMEM((n, width), BF),
            pltpu.VMEM(shape, BF),
            pltpu.SemaphoreType.DMA((8,)),
            pltpu.SemaphoreType.DMA((6,)),
        ],
        compiler_params=pltpu.CompilerParams(vmem_limit_bytes=VMEM_ALL),
        cost_estimate=pl.CostEstimate(
            flops=2 * experts * ROWS * n * width * 3,
            bytes_accessed=4 * width * (n + experts * CAP),
            transcendentals=0,
        ),
        name="pack",
    )(route_row, x, dy)


def part_copies(weights, core, low, high, out, sems):
    gate, up, down = weights
    hidden, span = out.shape[0] // (high - low), out.shape[1]
    columns = pl.ds(pl.multiple_of(core * hidden, hidden), hidden)
    last_up = min(high, UP_PARTS)
    copies = []
    if low < last_up:
        rows = slice(low * hidden, last_up * hidden)
        for i, ref in enumerate((gate, up)):
            dst = out.at[0 : (last_up - low) * hidden, i * hidden : (i + 1) * hidden]
            copies.append(pltpu.make_async_copy(ref.at[rows, columns], dst, sems.at[len(copies)]))
    for k in range(max(low, UP_PARTS), high):
        src = down.at[columns, (k - UP_PARTS) * span : (k - UP_PARTS + 1) * span]
        dst = out.at[(k - low) * hidden : (k - low + 1) * hidden, :]
        copies.append(pltpu.make_async_copy(src, dst, sems.at[len(copies)]))
    return copies


def weights_kernel(core_ref, gate, up, down, head, up_rest, down_rest, tail, held, read_sems, write_sems):
    hidden = held.shape[1] // 2
    reads, writes = [], []
    outs = ((head, ENDS[0]), (tail, ENDS[1]), (up_rest, RESTS[0]), (down_rest, RESTS[1]))
    for low, high in zip(WEIGHT_CUTS, WEIGHT_CUTS[1:]):
        rows = held.at[pl.ds(low * hidden, (high - low) * hidden)]
        sems = read_sems.at[pl.ds(2 * low, 2 * (high - low))]
        reads.append(part_copies((gate, up, down), core_ref[0], low, high, rows, sems))
        writes.append([])
        for i, (out, (first, last)) in enumerate(outs):
            if first <= low and high <= last:
                dst = out.at[pl.ds((low - first) * hidden, (high - low) * hidden)]
                writes[-1].append(pltpu.make_async_copy(rows, dst, write_sems.at[4 * len(writes) + i - 4]))
    for copies in reads:
        for copy in copies:
            copy.start()
    for copies, ready in zip(reads, writes):
        for copy in copies:
            copy.wait()
        for copy in ready:
            copy.start()
    for copies in writes:
        for copy in copies:
            copy.wait()


def weight_parts(core, weights):
    width, span = weights[0].shape
    hidden = span // 2
    any_spec = pl.BlockSpec(memory_space=pl.ANY)
    size = lambda parts: jax.ShapeDtypeStruct(((parts[1] - parts[0]) * hidden, span), BF)
    return pl.pallas_call(
        weights_kernel,
        out_shape=[size(parts) for parts in (ENDS[0],) + RESTS + (ENDS[1],)],
        in_specs=[pl.BlockSpec(memory_space=pltpu.SMEM)] + [any_spec] * 3,
        out_specs=[any_spec] * 4,
        scratch_shapes=[
            pltpu.VMEM((PARTS * hidden, span), BF),
            pltpu.SemaphoreType.DMA((2 * PARTS,)),
            pltpu.SemaphoreType.DMA((4 * len(WEIGHT_CUTS),)),
        ],
        compiler_params=pltpu.CompilerParams(vmem_limit_bytes=VMEM_ALL),
        cost_estimate=pl.CostEstimate(flops=0, bytes_accessed=6 * PARTS * hidden * span, transcendentals=0),
        name="weights",
    )(core, *weights)


def far_kernel(ranges, up_hbm, down_hbm, *refs):
    count = len(ranges)
    outs, held, sems = refs[:count], refs[count : 2 * count], refs[-1]
    reads, writes = [], []
    for i, (side, low, high) in enumerate(ranges):
        hidden = outs[i].shape[0] // (high - low)
        src = (up_hbm, down_hbm)[side].at[low * hidden : high * hidden, :]
        reads.append(pltpu.make_async_copy(src, held[i], sems.at[i]))
        writes.append(pltpu.make_async_copy(held[i], outs[i], sems.at[count + i]))
    for read in reads:
        read.start()
    for read, write in zip(reads, writes):
        read.wait()
        write.start()
    for write in writes:
        write.wait()


def far_parts(from_up, from_down, ranges):
    rows, span = from_up.shape
    hidden = span // 2
    any_spec = pl.BlockSpec(memory_space=pl.ANY)
    return pl.pallas_call(
        functools.partial(far_kernel, ranges),
        out_shape=[jax.ShapeDtypeStruct(((high - low) * hidden, span), BF) for _, low, high in ranges],
        in_specs=[any_spec] * 2,
        out_specs=[any_spec] * len(ranges),
        scratch_shapes=[pltpu.VMEM(((high - low) * hidden, span), BF) for _, low, high in ranges]
        + [pltpu.SemaphoreType.DMA((2 * len(ranges),))],
        compiler_params=pltpu.CompilerParams(vmem_limit_bytes=VMEM_ALL),
        cost_estimate=pl.CostEstimate(flops=FAR_FLOPS, bytes_accessed=0, transcendentals=0),
        name="far",
    )(from_up, from_down)


def block_copies(pieces, ranges, gu, down, place, sems):
    hidden, span = pieces[0].shape[1:]
    up_copies, down_copies = [], []
    for i, (piece, (low, high)) in enumerate(zip(pieces, ranges)):
        middle = min(max(low, UP_PARTS), high)
        if low < middle:
            up_copies.append(
                pltpu.make_async_copy(
                    piece.at[pl.ds(0, middle - low)],
                    gu.at[pl.ds(low, middle - low), :, pl.ds(place * span, span)],
                    sems.at[2 * i],
                )
            )
        if middle < high:
            down_copies.append(
                pltpu.make_async_copy(
                    piece.at[pl.ds(middle - low, high - middle)],
                    down.at[pl.ds(middle - UP_PARTS, high - middle), pl.ds(place * hidden, hidden)],
                    sems.at[2 * i + 1],
                )
            )
    return up_copies, down_copies


def slot_matrix(slots, packed, slot_dim, tail):
    shape = (slots, packed) if slot_dim == 0 else (packed, slots)
    slot = lax.broadcasted_iota(jnp.int32, shape, slot_dim)
    row = lax.broadcasted_iota(jnp.int32, shape, 1 - slot_dim)
    group, place = row >> 3, row & 7
    if tail is None:
        hit = (slot == group * CAP + place) & (place < CAP)
    else:
        hit = (slot == group * CAP + (place - CAP) * 3 + tail) & (place >= CAP)
    return jnp.where(hit, 1.0, 0.0).astype(BF)


def hidden_grads(x, dy, gu, down, grads, up_copies, down_copies):
    spans, total, span = down.shape
    blocks = len(up_copies)
    hidden = total // blocks
    width = x.shape[1]
    pres = []
    for b in range(blocks):
        for copy in up_copies[b]:
            copy.wait()
        pres.append(dot(x[...], gu[:, :, b * span : (b + 1) * span].reshape(width, span)))
    for copies in down_copies:
        for copy in copies:
            copy.wait()
    back = dot_t(dy[:, :span], down[0])
    for k in range(1, spans):
        back += dot_t(dy[:, k * span : (k + 1) * span], down[k])
    terms = None
    for b in range(blocks):
        pre_gate, pre_up = pres[b][:, :hidden], pres[b][:, hidden:]
        here = back[:, b * hidden : (b + 1) * hidden]
        s = jax.nn.sigmoid(pre_gate)
        activated = pre_gate * s
        slope = s * (1.0 + pre_gate * (1.0 - s))
        low = b * span
        grads[:, low : low + hidden] = (here * pre_up * slope).astype(BF)
        grads[:, low + hidden : low + span] = (here * activated).astype(BF)
        term = activated * pre_up * here
        terms = term if terms is None else terms + term
    return terms


def row_grads(grads, gu, j):
    parts, hidden, columns = gu.shape
    rows = slice(j * parts // 4, (j + 1) * parts // 4)
    return dot_t(grads[...], gu[rows].reshape(parts // 4 * hidden, columns))


def unpack_kernel(rows_hbm, *refs):
    outs, rows, sems = refs[:-2], refs[-2], refs[-1]
    packed = rows.shape[0]
    slots, width = outs[0].shape[0], rows.shape[1] // 6 * 4
    part = width // 4
    per = len(outs) // 2
    cols = [slice(j * part, (j + 1) * part) for j in range(6)]
    copies = [pltpu.make_async_copy(rows_hbm.at[:, c], rows.at[:, c], sems.at[j]) for j, c in enumerate(cols)]
    for copy in copies:
        copy.start()
    spread = slot_matrix(slots, packed, 0, None)
    spread_tail = [slot_matrix(slots, packed, 0, j) for j in range(3)]
    wide = width // per
    for k in range(2):
        last = None
        for j in range(4):
            if j < 3:
                copies[3 * k + j].wait()
                piece = dot(spread, rows[:, cols[3 * k + j]])
                more = dot(spread_tail[j], rows[:, cols[3 * k + j]])
                last = more if last is None else last + more
            else:
                piece = last
            low = j * part % wide
            outs[k * per + j * part // wide][:, low : low + part] = piece.astype(BF)


def unpack(rows):
    packed = rows.shape[0]
    slots, width = packed // ROWS * CAP, rows.shape[1] // 6 * 4
    return pl.pallas_call(
        unpack_kernel,
        out_shape=[jax.ShapeDtypeStruct((slots, width // COLUMN_PIECES), BF)] * (2 * COLUMN_PIECES),
        in_specs=[pl.BlockSpec(memory_space=pl.ANY)],
        scratch_shapes=[pltpu.VMEM(rows.shape, BF), pltpu.SemaphoreType.DMA((6,))],
        compiler_params=pltpu.CompilerParams(vmem_limit_bytes=SMALL_VMEM),
        cost_estimate=pl.CostEstimate(flops=FIRST_FLOPS, bytes_accessed=FIRST_FLOPS, transcendentals=0),
        name="unpack",
    )(rows)


def row_copies(pieces, full, sems):
    wide = pieces[0].shape[1]
    return [
        pltpu.make_async_copy(piece, full.at[:, pl.ds(i * wide, wide)], sems.at[i]) for i, piece in enumerate(pieces)
    ]


def first_kernel(ranges, *refs):
    count = COLUMN_PIECES
    x_pieces, dy_pieces, refs = refs[:count], refs[count : 2 * count], refs[2 * count :]
    pieces, refs = refs[: sum(map(len, ranges))], refs[sum(map(len, ranges)) :]
    sum_hbm, term_ref, x, dy, gu, down, grads, total, sems = refs
    part = x.shape[1] // 4
    x_copies = row_copies(x_pieces, x, sems.at[pl.ds(0, count)])
    dy_copies = row_copies(dy_pieces, dy, sems.at[pl.ds(count, count)])
    up_copies, down_copies, used = [], [], 0
    for b, block in enumerate(ranges):
        here = pieces[used : used + len(block)]
        ups, downs = block_copies(here, block, gu, down, b, sems.at[pl.ds(2 * count + 4 + 2 * used, 2 * len(block))])
        used += len(block)
        up_copies.append(ups)
        down_copies.append(downs)
    for copies in [x_copies] + up_copies + [dy_copies] + down_copies:
        for copy in copies:
            copy.start()
    for copy in x_copies:
        copy.wait()
    term_ref[...] = hidden_grads(x, dy, gu, down, grads, up_copies, down_copies + [dy_copies])
    outs = []
    for j in range(4):
        cols = pl.ds(j * part, part)
        total[:, cols] = row_grads(grads, gu, j).astype(BF)
        outs.append(pltpu.make_async_copy(total.at[:, cols], sum_hbm.at[:, cols], sems.at[2 * count + j]))
        outs[j].start()
    for copy in outs:
        copy.wait()


def first_blocks(x, dy, blocks, ranges):
    slots, wide = x[0].shape
    width = wide * COLUMN_PIECES
    hidden, span = blocks[0][0].shape[1:]
    count = len(blocks)
    pieces = [piece for block in blocks for piece in block]
    any_spec = pl.BlockSpec(memory_space=pl.ANY)
    return pl.pallas_call(
        functools.partial(first_kernel, ranges),
        out_shape=(jax.ShapeDtypeStruct((slots, width), BF), jax.ShapeDtypeStruct((slots, hidden), F32)),
        in_specs=[any_spec] * (len(x) + len(dy) + len(pieces)),
        out_specs=(any_spec, pl.BlockSpec(memory_space=pltpu.VMEM)),
        scratch_shapes=[
            pltpu.VMEM((slots, width), BF),
            pltpu.VMEM((slots, width), BF),
            pltpu.VMEM((UP_PARTS, hidden, count * span), BF),
            pltpu.VMEM((PARTS - UP_PARTS, count * hidden, span), BF),
            pltpu.VMEM((slots, count * span), BF),
            pltpu.VMEM((slots, width), BF),
            pltpu.SemaphoreType.DMA((2 * COLUMN_PIECES + 4 + 2 * len(pieces),)),
        ],
        compiler_params=pltpu.CompilerParams(vmem_limit_bytes=FIRST_VMEM),
        cost_estimate=pl.CostEstimate(flops=FIRST_FLOPS, bytes_accessed=FIRST_FLOPS, transcendentals=0),
        name="first",
    )(*x, *dy, *pieces)


def last_kernel(ranges, *refs):
    count = COLUMN_PIECES
    x_pieces, dy_pieces, refs = refs[:count], refs[count : 2 * count], refs[2 * count :]
    pieces, refs = refs[: len(ranges)], refs[len(ranges) :]
    sum_hbm, term_ref, out_ref, x, dy, gu, down, total, grads, sems = refs
    slots, part = x.shape[0], x.shape[1] // 4
    x_copies = row_copies(x_pieces, x, sems.at[pl.ds(0, count)])
    dy_copies = row_copies(dy_pieces, dy, sems.at[pl.ds(count, count)])
    up_copies, down_copies = block_copies(pieces, ranges, gu, down, 0, sems.at[pl.ds(2 * count + 1, 2 * len(ranges))])
    sum_copy = pltpu.make_async_copy(sum_hbm, total, sems.at[2 * count])
    for copy in x_copies + up_copies + dy_copies + down_copies + [sum_copy]:
        copy.start()
    for copy in x_copies:
        copy.wait()
    terms = hidden_grads(x, dy, gu, down, grads, [up_copies], [down_copies + dy_copies]) + term_ref[...]
    terms = jnp.broadcast_to(jnp.sum(terms, axis=1, keepdims=True), (slots, TERM_LANES))
    out_ref[:, 4 * part :] = terms.astype(BF)
    sum_copy.wait()
    for j in range(4):
        cols = slice(j * part, (j + 1) * part)
        out_ref[:, cols] = (total[:, cols].astype(F32) + row_grads(grads, gu, j)).astype(BF)


def last_block(x, dy, pieces, ranges, total, term):
    rows, width = total.shape
    hidden, span = pieces[0].shape[1:]
    any_spec = pl.BlockSpec(memory_space=pl.ANY)
    vmem_spec = pl.BlockSpec(memory_space=pltpu.VMEM)
    return pl.pallas_call(
        functools.partial(last_kernel, ranges),
        out_shape=jax.ShapeDtypeStruct((rows, width + TERM_LANES), BF),
        in_specs=[any_spec] * (len(x) + len(dy) + len(pieces) + 1) + [vmem_spec],
        out_specs=vmem_spec,
        scratch_shapes=[
            pltpu.VMEM((rows, width), BF),
            pltpu.VMEM((rows, width), BF),
            pltpu.VMEM((UP_PARTS, hidden, span), BF),
            pltpu.VMEM((PARTS - UP_PARTS, hidden, span), BF),
            pltpu.VMEM((rows, width), BF),
            pltpu.VMEM((rows, span), BF),
            pltpu.SemaphoreType.DMA((2 * COLUMN_PIECES + 1 + 2 * len(pieces),)),
        ],
        compiler_params=pltpu.CompilerParams(vmem_limit_bytes=LAST_VMEM),
        cost_estimate=pl.CostEstimate(flops=LAST_FLOPS, bytes_accessed=LAST_FLOPS, transcendentals=0),
        name="last",
    )(*x, *dy, *pieces, total, term)


def add_pack_kernel(a_ref, b_ref, out_ref):
    slots, packed = a_ref.shape[0], out_ref.shape[0]
    part = (a_ref.shape[1] - TERM_LANES) // 4
    gather = slot_matrix(slots, packed, 1, None)
    gather_tail = [slot_matrix(slots, packed, 1, j) for j in range(3)]

    def total(low, size):
        cols = pl.ds(low, size)
        return (a_ref[:, cols].astype(F32) + b_ref[:, cols].astype(F32)).astype(BF)

    out_ref[:, 3 * part :] = dot(gather, total(4 * part, TERM_LANES)).astype(BF)
    last = total(3 * part, part)
    for j in range(3):
        out_ref[:, j * part : (j + 1) * part] = (
            dot(gather, total(j * part, part)) + dot(gather_tail[j], last)
        ).astype(BF)


def add_pack(a, b):
    slots, columns = a.shape
    packed, part = slots // CAP * ROWS, (columns - TERM_LANES) // 4
    return pl.pallas_call(
        add_pack_kernel,
        out_shape=jax.ShapeDtypeStruct((packed, 3 * part + TERM_LANES), BF),
        compiler_params=pltpu.CompilerParams(vmem_limit_bytes=SMALL_VMEM),
        cost_estimate=pl.CostEstimate(
            flops=2 * packed * slots * part * 6, bytes_accessed=6 * slots * columns, transcendentals=0
        ),
        name="add_pack",
    )(a, b)


def combine_kernel(route_ref, gate_ref, own_term_ref, out_grad_ref, ret_ref, token_grad_ref, gate_grad_ref):
    n, width = out_grad_ref.shape
    packed = ret_ref.shape[0]
    part = width // 4
    experts = packed // ROWS
    route_row = route_ref[...]
    main, tail, block = (to_column(v) for v in places(route_row))
    routed = to_column(route_row) < experts
    gate = to_column(gate_ref[...])
    row = lax.broadcasted_iota(jnp.int32, (n, packed), 1)
    select = jnp.where(row == main, 1.0, 0.0).astype(BF)
    last = jnp.zeros((n, part), F32)
    for j in range(4):
        cols = pl.ds(j * part, part)
        if j < 3:
            tail_select = jnp.where((row == tail) & (block == j), 1.0, 0.0).astype(BF)
            piece = ret_ref[:, cols]
            rows = dot(select, piece)
            last += dot(tail_select, piece)
        else:
            rows = last
        rows = jnp.where(routed, rows, out_grad_ref[:, cols].astype(F32))
        token_grad_ref[:, cols] = (gate * rows).astype(BF)
    terms = dot(select, ret_ref[:, 3 * part :])[:, :1]
    gate_grad_ref[...] = jnp.where(route_row < experts, to_row(terms), own_term_ref[...]).astype(BF)


def combine(route_row, gate_row, own_term, out_grad, ret):
    n, width = out_grad.shape
    return pl.pallas_call(
        combine_kernel,
        out_shape=(jax.ShapeDtypeStruct((n, width), BF), jax.ShapeDtypeStruct((1, n), BF)),
        compiler_params=pltpu.CompilerParams(vmem_limit_bytes=SMALL_VMEM),
        cost_estimate=pl.CostEstimate(
            flops=2 * ret.shape[0] * n * width * 3 // 2,
            bytes_accessed=2 * (2 * out_grad.size + ret.size),
            transcendentals=0,
        ),
        name="combine",
    )(route_row, gate_row, own_term, out_grad, ret)


def per_device(tokens, out_grad, gate, route, gate_weight, up_weight, down_weight):
    experts = lax.axis_size("expert")
    groups = lax.axis_size("tensor")
    n, width = tokens.shape
    swap = [(0, 1), (1, 0)]
    up = [(i, (i + 1) % groups) for i in range(groups)]
    down = [(i, (i - 1) % groups) for i in range(groups)]
    route_row = route.reshape(1, n)

    core = lax.axis_index("dp").reshape(1)
    weights = (gate_weight[0], up_weight[0], down_weight[0])
    head, up_rest, down_rest, tail = weight_parts(core, weights)
    up_head = lax.ppermute(head, "tensor", up)
    down_tail = lax.ppermute(tail, "tensor", down)
    from_up = lax.ppermute(up_rest, "tensor", up)
    from_down = lax.ppermute(down_rest, "tensor", down)
    far_head = lax.ppermute(up_head, "tensor", up)
    far_tail = lax.ppermute(down_tail, "tensor", down)

    route_row, head = lax.optimization_barrier((route_row, head))
    packed = pack(route_row, tokens, out_grad, experts)
    got = lax.all_to_all(
        packed.reshape(experts, ROWS, -1), "expert", split_axis=0, concat_axis=0, tiled=True
    ).reshape(experts * ROWS, -1)

    far_up, far_down = far_parts(from_up, from_down, ((0, 0, HALF - HEAD), (1, HALF, PARTS - HEAD)))
    got, far_up, far_down, far_head, far_tail = lax.optimization_barrier(
        (got, far_up, far_down, far_head, far_tail)
    )
    far_up = lax.ppermute(far_up, "tensor", up)
    far_down = lax.ppermute(far_down, "tensor", down)
    rows = list(unpack(got))
    other_rows = [lax.ppermute(piece, "dp", swap) for piece in rows]
    part = width // UP_PARTS
    squares = lambda piece: piece.reshape(-1, part, 2 * part)
    blocks = [list(map(squares, b)) for b in ((head, up_rest), (up_head, from_up), (from_down, down_tail))]
    ranges = ((ENDS[0], RESTS[0]),) * 2 + ((RESTS[1], ENDS[1]),)
    far = (far_head, far_up, far_down, far_tail)
    far_ranges = (ENDS[0], (HEAD, HALF), (HALF, PARTS - HEAD), ENDS[1])
    cut = lambda r: (r[:COLUMN_PIECES], r[COLUMN_PIECES:])
    own_total, own_gate_term = first_blocks(*cut(rows), blocks, ranges)
    own_total, *other_rows = lax.optimization_barrier((own_total, *other_rows))
    total, term = first_blocks(*cut(other_rows), blocks, ranges)
    far = list(map(squares, far))
    other_sums = lax.ppermute(last_block(*cut(other_rows), far, far_ranges, total, term), "dp", swap)
    own_sums = last_block(*cut(rows), far, far_ranges, own_total, own_gate_term)
    back = add_pack(own_sums, other_sums).reshape(experts, ROWS, -1)
    ret = lax.all_to_all(back, "expert", split_axis=0, concat_axis=0, tiled=True)
    own_term = jnp.sum(out_grad.astype(F32) * tokens.astype(F32), axis=1)
    token_grad, gate_grad = combine(
        route_row, gate.reshape(1, n), own_term.reshape(1, n), out_grad, ret.reshape(experts * ROWS, -1)
    )
    return token_grad, gate_grad.reshape(n)


def solution(mesh):
    rows = P(("dp", "expert", "tensor"), None)
    return jax.shard_map(
        per_device,
        mesh=mesh,
        in_specs=(
            rows,
            rows,
            P(("dp", "expert", "tensor")),
            rows,
            P("expert", None, "tensor"),
            P("expert", None, "tensor"),
            P("expert", "tensor", None),
        ),
        out_specs=(rows, P(("dp", "expert", "tensor"))),
        check_vma=False,
    )
```

```python
import functools

import jax
import jax.numpy as jnp
from jax import lax
from jax.experimental import pallas as pl
from jax.experimental.pallas import tpu as pltpu
from jax.sharding import PartitionSpec as P

BF = jnp.bfloat16
F32 = jnp.float32
CAP = 6
ROWS = 8
TERM_LANES = 128
PARTS = 60
UP_PARTS = 40
HALF = 30
HEAD = 16
ENDS = ((0, HEAD), (PARTS - HEAD, PARTS))
RESTS = ((HEAD, PARTS), (0, PARTS - HEAD))
MIDDLE = (PARTS - 2 * HEAD) // 3
WEIGHT_CUTS = (0, HEAD, HEAD + MIDDLE, HEAD + 2 * MIDDLE, PARTS - HEAD, PARTS)
FAR_FLOPS = 62000000000
FIRST_FLOPS = 1000
LAST_FLOPS = 1000
VMEM_ALL = 56 * 1024 * 1024
SMALL_VMEM = 20 * 1024 * 1024
FIRST_VMEM = 38 * 1024 * 1024
LAST_VMEM = 24 * 1024 * 1024


def dot(a, b):
    return jnp.dot(a, b, preferred_element_type=F32)


def dot_t(a, b):
    return lax.dot_general(a, b, (((1,), (1,)), ((), ())), preferred_element_type=F32)


def eye(n):
    return lax.broadcasted_iota(jnp.int32, (n, n), 0) == lax.broadcasted_iota(jnp.int32, (n, n), 1)


def to_column(row):
    n = row.shape[1]
    return jnp.sum(jnp.where(eye(n), jnp.broadcast_to(row, (n, n)), 0), axis=1, keepdims=True)


def to_row(column):
    n = column.shape[0]
    return jnp.sum(jnp.where(eye(n), jnp.broadcast_to(column, (n, n)), 0), axis=0, keepdims=True)


def places(route_row):
    n = route_row.shape[1]
    across = jnp.broadcast_to(route_row, (n, n))
    down = jnp.broadcast_to(to_column(route_row), (n, n))
    earlier = lax.broadcasted_iota(jnp.int32, (n, n), 0) < lax.broadcasted_iota(jnp.int32, (n, n), 1)
    slot = jnp.sum(jnp.where((across == down) & earlier, 1, 0), axis=0, keepdims=True)
    second = jnp.where(slot >= 3, 1, 0)
    base = route_row * ROWS
    return base + slot, base + CAP + second, slot - 3 * second


def pack_kernel(route_ref, x_hbm, dy_hbm, out_hbm, rows, out, in_sems, out_sems):
    n, total = route_ref.shape[1], out.shape[0]
    part = rows.shape[2]
    reads = []
    for i, src in enumerate((x_hbm, dy_hbm)):
        for j in range(3):
            k = 3 * i + j
            reads.append(
                [
                    pltpu.make_async_copy(
                        src.at[:, pl.ds(quarter * part, part)], rows.at[k, pl.ds(low, n)], in_sems.at[2 * k + low // n]
                    )
                    for quarter, low in ((j, 0), (3, n))
                ]
            )
            for copy in reads[-1]:
                copy.start()
    main, tail, block = places(route_ref[...])
    row = lax.broadcasted_iota(jnp.int32, (total, n), 0)
    select = jnp.where(row == main, 1.0, 0.0).astype(BF)
    selects = [
        jnp.concatenate([select, jnp.where((row == tail) & (block == j), 1.0, 0.0).astype(BF)], axis=1)
        for j in range(3)
    ]
    writes = []
    for k in range(6):
        for copy in reads[k]:
            copy.wait()
        cols = pl.ds(k * part, part)
        out[:, cols] = dot(selects[k % 3], rows[k]).astype(BF)
        writes.append(pltpu.make_async_copy(out.at[:, cols], out_hbm.at[:, cols], out_sems.at[k]))
        writes[-1].start()
    for write in writes:
        write.wait()


def pack(route_row, x, dy, experts):
    n, width = x.shape
    shape = (experts * ROWS, width // 4 * 6)
    any_spec = pl.BlockSpec(memory_space=pl.ANY)
    return pl.pallas_call(
        pack_kernel,
        out_shape=jax.ShapeDtypeStruct(shape, BF),
        in_specs=[pl.BlockSpec(memory_space=pltpu.VMEM), any_spec, any_spec],
        out_specs=any_spec,
        scratch_shapes=[
            pltpu.VMEM((6, 2 * n, width // 4), BF),
            pltpu.VMEM(shape, BF),
            pltpu.SemaphoreType.DMA((12,)),
            pltpu.SemaphoreType.DMA((6,)),
        ],
        compiler_params=pltpu.CompilerParams(vmem_limit_bytes=VMEM_ALL),
        cost_estimate=pl.CostEstimate(
            flops=2 * experts * ROWS * n * width * 3,
            bytes_accessed=4 * width * (n + experts * CAP),
            transcendentals=0,
        ),
        name="pack",
    )(route_row, x, dy)


def part_copies(weights, core, low, high, out, sems):
    gate, up, down = weights
    hidden, span = out.shape[0] // (high - low), out.shape[1]
    columns = pl.ds(pl.multiple_of(core * hidden, hidden), hidden)
    last_up = min(high, UP_PARTS)
    copies = []
    if low < last_up:
        rows = slice(low * hidden, last_up * hidden)
        for i, ref in enumerate((gate, up)):
            dst = out.at[0 : (last_up - low) * hidden, i * hidden : (i + 1) * hidden]
            copies.append(pltpu.make_async_copy(ref.at[rows, columns], dst, sems.at[len(copies)]))
    for k in range(max(low, UP_PARTS), high):
        src = down.at[columns, (k - UP_PARTS) * span : (k - UP_PARTS + 1) * span]
        dst = out.at[(k - low) * hidden : (k - low + 1) * hidden, :]
        copies.append(pltpu.make_async_copy(src, dst, sems.at[len(copies)]))
    return copies


def weights_kernel(core_ref, gate, up, down, head, up_rest, down_rest, tail, held, read_sems, write_sems):
    hidden = held.shape[1] // 2
    reads, writes = [], []
    outs = ((head, ENDS[0]), (tail, ENDS[1]), (up_rest, RESTS[0]), (down_rest, RESTS[1]))
    for low, high in zip(WEIGHT_CUTS, WEIGHT_CUTS[1:]):
        rows = held.at[pl.ds(low * hidden, (high - low) * hidden)]
        sems = read_sems.at[pl.ds(2 * low, 2 * (high - low))]
        reads.append(part_copies((gate, up, down), core_ref[0], low, high, rows, sems))
        writes.append([])
        for i, (out, (first, last)) in enumerate(outs):
            if first <= low and high <= last:
                dst = out.at[pl.ds((low - first) * hidden, (high - low) * hidden)]
                writes[-1].append(pltpu.make_async_copy(rows, dst, write_sems.at[4 * len(writes) + i - 4]))
    for copies in reads:
        for copy in copies:
            copy.start()
    for copies, ready in zip(reads, writes):
        for copy in copies:
            copy.wait()
        for copy in ready:
            copy.start()
    for copies in writes:
        for copy in copies:
            copy.wait()


def weight_parts(core, weights):
    width, span = weights[0].shape
    hidden = span // 2
    any_spec = pl.BlockSpec(memory_space=pl.ANY)
    size = lambda parts: jax.ShapeDtypeStruct(((parts[1] - parts[0]) * hidden, span), BF)
    return pl.pallas_call(
        weights_kernel,
        out_shape=[size(parts) for parts in (ENDS[0],) + RESTS + (ENDS[1],)],
        in_specs=[pl.BlockSpec(memory_space=pltpu.SMEM)] + [any_spec] * 3,
        out_specs=[any_spec] * 4,
        scratch_shapes=[
            pltpu.VMEM((PARTS * hidden, span), BF),
            pltpu.SemaphoreType.DMA((2 * PARTS,)),
            pltpu.SemaphoreType.DMA((4 * len(WEIGHT_CUTS),)),
        ],
        compiler_params=pltpu.CompilerParams(vmem_limit_bytes=VMEM_ALL),
        cost_estimate=pl.CostEstimate(flops=0, bytes_accessed=6 * PARTS * hidden * span, transcendentals=0),
        name="weights",
    )(core, *weights)


def far_kernel(ranges, up_hbm, down_hbm, *refs):
    count = len(ranges)
    outs, held, sems = refs[:count], refs[count : 2 * count], refs[-1]
    reads, writes = [], []
    for i, (side, low, high) in enumerate(ranges):
        hidden = outs[i].shape[0] // (high - low)
        src = (up_hbm, down_hbm)[side].at[low * hidden : high * hidden, :]
        reads.append(pltpu.make_async_copy(src, held[i], sems.at[i]))
        writes.append(pltpu.make_async_copy(held[i], outs[i], sems.at[count + i]))
    for read in reads:
        read.start()
    for read, write in zip(reads, writes):
        read.wait()
        write.start()
    for write in writes:
        write.wait()


def far_parts(from_up, from_down, ranges):
    rows, span = from_up.shape
    hidden = span // 2
    any_spec = pl.BlockSpec(memory_space=pl.ANY)
    return pl.pallas_call(
        functools.partial(far_kernel, ranges),
        out_shape=[jax.ShapeDtypeStruct(((high - low) * hidden, span), BF) for _, low, high in ranges],
        in_specs=[any_spec] * 2,
        out_specs=[any_spec] * len(ranges),
        scratch_shapes=[pltpu.VMEM(((high - low) * hidden, span), BF) for _, low, high in ranges]
        + [pltpu.SemaphoreType.DMA((2 * len(ranges),))],
        compiler_params=pltpu.CompilerParams(vmem_limit_bytes=VMEM_ALL),
        cost_estimate=pl.CostEstimate(flops=FAR_FLOPS, bytes_accessed=0, transcendentals=0),
        name="far",
    )(from_up, from_down)


def block_copies(pieces, ranges, gu, down, place, sems):
    hidden, span = pieces[0].shape[1:]
    up_copies, down_copies = [], []
    for i, (piece, (low, high)) in enumerate(zip(pieces, ranges)):
        middle = min(max(low, UP_PARTS), high)
        if low < middle:
            up_copies.append(
                pltpu.make_async_copy(
                    piece.at[pl.ds(0, middle - low)],
                    gu.at[pl.ds(low, middle - low), :, pl.ds(place * span, span)],
                    sems.at[2 * i],
                )
            )
        if middle < high:
            down_copies.append(
                pltpu.make_async_copy(
                    piece.at[pl.ds(middle - low, high - middle)],
                    down.at[pl.ds(middle - UP_PARTS, high - middle), pl.ds(place * hidden, hidden)],
                    sems.at[2 * i + 1],
                )
            )
    return up_copies, down_copies


def slot_matrix(slots, packed, slot_dim, tail):
    shape = (slots, packed) if slot_dim == 0 else (packed, slots)
    slot = lax.broadcasted_iota(jnp.int32, shape, slot_dim)
    row = lax.broadcasted_iota(jnp.int32, shape, 1 - slot_dim)
    group, place = row >> 3, row & 7
    if tail is None:
        hit = (slot == group * CAP + place) & (place < CAP)
    else:
        hit = (slot == group * CAP + (place - CAP) * 3 + tail) & (place >= CAP)
    return jnp.where(hit, 1.0, 0.0).astype(BF)


def hidden_grads(x, dy, gu, down, grads, up_copies, down_copies):
    spans, total, span = down.shape
    blocks = len(up_copies)
    hidden = total // blocks
    width = x.shape[1]
    pres = []
    for b in range(blocks):
        for copy in up_copies[b]:
            copy.wait()
        pres.append(dot(x[...], gu[:, :, b * span : (b + 1) * span].reshape(width, span)))
    for copies in down_copies:
        for copy in copies:
            copy.wait()
    back = dot_t(dy[:, :span], down[0])
    for k in range(1, spans):
        back += dot_t(dy[:, k * span : (k + 1) * span], down[k])
    terms = None
    for b in range(blocks):
        pre_gate, pre_up = pres[b][:, :hidden], pres[b][:, hidden:]
        here = back[:, b * hidden : (b + 1) * hidden]
        s = jax.nn.sigmoid(pre_gate)
        activated = pre_gate * s
        slope = s * (1.0 + pre_gate * (1.0 - s))
        low = b * span
        grads[:, low : low + hidden] = (here * pre_up * slope).astype(BF)
        grads[:, low + hidden : low + span] = (here * activated).astype(BF)
        term = activated * pre_up * here
        terms = term if terms is None else terms + term
    return terms


def row_grads(grads, gu, j):
    parts, hidden, columns = gu.shape
    rows = slice(j * parts // 4, (j + 1) * parts // 4)
    return dot_t(grads[...], gu[rows].reshape(parts // 4 * hidden, columns))


def unpack_kernel(rows_hbm, x_ref, dy_ref, rows, sems):
    packed = rows.shape[0]
    slots, width = x_ref.shape
    part = width // 4
    cols = [slice(j * part, (j + 1) * part) for j in range(6)]
    copies = [pltpu.make_async_copy(rows_hbm.at[:, c], rows.at[:, c], sems.at[j]) for j, c in enumerate(cols)]
    for copy in copies:
        copy.start()
    spread = slot_matrix(slots, packed, 0, None)
    both = [jnp.concatenate([spread, slot_matrix(slots, packed, 0, j)], axis=0) for j in range(3)]
    for k, out_ref in enumerate((x_ref, dy_ref)):
        last = None
        for j in range(3):
            copies[3 * k + j].wait()
            pieces = dot(both[j], rows[:, cols[3 * k + j]])
            out_ref[:, cols[j]] = pieces[:slots].astype(BF)
            last = pieces[slots:] if last is None else last + pieces[slots:]
        out_ref[:, cols[3]] = last.astype(BF)


def unpack(rows):
    packed = rows.shape[0]
    slots, width = packed // ROWS * CAP, rows.shape[1] // 6 * 4
    return pl.pallas_call(
        unpack_kernel,
        out_shape=[jax.ShapeDtypeStruct((slots, width), BF)] * 2,
        in_specs=[pl.BlockSpec(memory_space=pl.ANY)],
        scratch_shapes=[pltpu.VMEM(rows.shape, BF), pltpu.SemaphoreType.DMA((6,))],
        compiler_params=pltpu.CompilerParams(vmem_limit_bytes=SMALL_VMEM),
        cost_estimate=pl.CostEstimate(flops=FIRST_FLOPS, bytes_accessed=FIRST_FLOPS, transcendentals=0),
        name="unpack",
    )(rows)


def first_kernel(ranges, *refs):
    row_refs, refs = refs[:4], refs[4:]
    pieces, refs = refs[: sum(map(len, ranges))], refs[sum(map(len, ranges)) :]
    own_hbm, other_hbm, own_term, other_term, x, dy, gu, down, grads, total, sems = refs
    slots, part = x.shape[0] // 2, x.shape[1] // 4
    row_copies = [
        pltpu.make_async_copy(src, full.at[pl.ds(i * slots, slots)], sems.at[2 * k + i])
        for k, full in enumerate((x, dy))
        for i, src in enumerate(row_refs[2 * k : 2 * k + 2])
    ]
    up_copies, down_copies, used = [], [], 0
    for b, block in enumerate(ranges):
        here = pieces[used : used + len(block)]
        ups, downs = block_copies(here, block, gu, down, b, sems.at[pl.ds(12 + 2 * used, 2 * len(block))])
        used += len(block)
        up_copies.append(ups)
        down_copies.append(downs)
    for copies in [row_copies[:2]] + up_copies + [row_copies[2:]] + down_copies:
        for copy in copies:
            copy.start()
    for copy in row_copies[:2]:
        copy.wait()
    terms = hidden_grads(x, dy, gu, down, grads, up_copies, down_copies + [row_copies[2:]])
    own_term[...] = terms[:slots]
    other_term[...] = terms[slots:]
    outs = []
    for j in range(4):
        cols = pl.ds(j * part, part)
        total[:, cols] = row_grads(grads, gu, j).astype(BF)
        for i, out in enumerate((own_hbm, other_hbm)):
            src = total.at[pl.ds(i * slots, slots), cols]
            outs.append(pltpu.make_async_copy(src, out.at[:, cols], sems.at[4 + 2 * j + i]))
            outs[-1].start()
    for copy in outs:
        copy.wait()


def first_blocks(rows, blocks, ranges):
    slots, width = rows[0].shape
    hidden, span = blocks[0][0].shape[1:]
    count = len(blocks)
    pieces = [piece for block in blocks for piece in block]
    any_spec = pl.BlockSpec(memory_space=pl.ANY)
    vmem_spec = pl.BlockSpec(memory_space=pltpu.VMEM)
    return pl.pallas_call(
        functools.partial(first_kernel, ranges),
        out_shape=[jax.ShapeDtypeStruct((slots, width), BF)] * 2 + [jax.ShapeDtypeStruct((slots, hidden), F32)] * 2,
        in_specs=[any_spec] * (4 + len(pieces)),
        out_specs=[any_spec] * 2 + [vmem_spec] * 2,
        scratch_shapes=[
            pltpu.VMEM((2 * slots, width), BF),
            pltpu.VMEM((2 * slots, width), BF),
            pltpu.VMEM((UP_PARTS, hidden, count * span), BF),
            pltpu.VMEM((PARTS - UP_PARTS, count * hidden, span), BF),
            pltpu.VMEM((2 * slots, count * span), BF),
            pltpu.VMEM((2 * slots, width), BF),
            pltpu.SemaphoreType.DMA((12 + 2 * len(pieces),)),
        ],
        compiler_params=pltpu.CompilerParams(vmem_limit_bytes=FIRST_VMEM),
        cost_estimate=pl.CostEstimate(flops=FIRST_FLOPS, bytes_accessed=FIRST_FLOPS, transcendentals=0),
        name="first",
    )(*rows, *pieces)


def last_kernel(ranges, *refs):
    x_hbm, dy_hbm, refs = refs[0], refs[1], refs[2:]
    pieces, refs = refs[: len(ranges)], refs[len(ranges) :]
    sum_hbm, term_ref, out_ref, x, dy, gu, down, total, grads, sems = refs
    slots, part = x.shape[0], x.shape[1] // 4
    x_copy = pltpu.make_async_copy(x_hbm, x, sems.at[0])
    dy_copy = pltpu.make_async_copy(dy_hbm, dy, sems.at[1])
    sum_copy = pltpu.make_async_copy(sum_hbm, total, sems.at[2])
    up_copies, down_copies = block_copies(pieces, ranges, gu, down, 0, sems.at[pl.ds(3, 2 * len(ranges))])
    for copy in [x_copy] + up_copies + [dy_copy] + down_copies + [sum_copy]:
        copy.start()
    x_copy.wait()
    terms = hidden_grads(x, dy, gu, down, grads, [up_copies], [down_copies + [dy_copy]]) + term_ref[...]
    terms = jnp.broadcast_to(jnp.sum(terms, axis=1, keepdims=True), (slots, TERM_LANES))
    out_ref[:, 4 * part :] = terms.astype(BF)
    sum_copy.wait()
    for j in range(4):
        cols = slice(j * part, (j + 1) * part)
        out_ref[:, cols] = (total[:, cols].astype(F32) + row_grads(grads, gu, j)).astype(BF)


def last_block(x, dy, pieces, ranges, total, term):
    rows, width = total.shape
    hidden, span = pieces[0].shape[1:]
    any_spec = pl.BlockSpec(memory_space=pl.ANY)
    vmem_spec = pl.BlockSpec(memory_space=pltpu.VMEM)
    return pl.pallas_call(
        functools.partial(last_kernel, ranges),
        out_shape=jax.ShapeDtypeStruct((rows, width + TERM_LANES), BF),
        in_specs=[any_spec] * (len(pieces) + 3) + [vmem_spec],
        out_specs=vmem_spec,
        scratch_shapes=[
            pltpu.VMEM((rows, width), BF),
            pltpu.VMEM((rows, width), BF),
            pltpu.VMEM((UP_PARTS, hidden, span), BF),
            pltpu.VMEM((PARTS - UP_PARTS, hidden, span), BF),
            pltpu.VMEM((rows, width), BF),
            pltpu.VMEM((rows, span), BF),
            pltpu.SemaphoreType.DMA((3 + 2 * len(pieces),)),
        ],
        compiler_params=pltpu.CompilerParams(vmem_limit_bytes=LAST_VMEM),
        cost_estimate=pl.CostEstimate(flops=LAST_FLOPS, bytes_accessed=LAST_FLOPS, transcendentals=0),
        name="last",
    )(x, dy, *pieces, total, term)


def add_pack_kernel(a_ref, b_ref, out_ref):
    slots, packed = a_ref.shape[0], out_ref.shape[0]
    part = (a_ref.shape[1] - TERM_LANES) // 4
    gather = slot_matrix(slots, packed, 1, None)
    gather_tail = [slot_matrix(slots, packed, 1, j) for j in range(3)]

    def total(low, size):
        cols = pl.ds(low, size)
        return (a_ref[:, cols].astype(F32) + b_ref[:, cols].astype(F32)).astype(BF)

    out_ref[:, 3 * part :] = dot(gather, total(4 * part, TERM_LANES)).astype(BF)
    last = total(3 * part, part)
    for j in range(3):
        out_ref[:, j * part : (j + 1) * part] = (
            dot(gather, total(j * part, part)) + dot(gather_tail[j], last)
        ).astype(BF)


def add_pack(a, b):
    slots, columns = a.shape
    packed, part = slots // CAP * ROWS, (columns - TERM_LANES) // 4
    return pl.pallas_call(
        add_pack_kernel,
        out_shape=jax.ShapeDtypeStruct((packed, 3 * part + TERM_LANES), BF),
        compiler_params=pltpu.CompilerParams(vmem_limit_bytes=SMALL_VMEM),
        cost_estimate=pl.CostEstimate(
            flops=2 * packed * slots * part * 6, bytes_accessed=6 * slots * columns, transcendentals=0
        ),
        name="add_pack",
    )(a, b)


def combine_kernel(route_ref, gate_ref, own_term_ref, out_grad_ref, ret_ref, token_grad_ref, gate_grad_ref):
    n, width = out_grad_ref.shape
    packed = ret_ref.shape[0]
    part = width // 4
    experts = packed // ROWS
    route_row = route_ref[...]
    main, tail, block = (to_column(v) for v in places(route_row))
    routed = to_column(route_row) < experts
    gate = to_column(gate_ref[...])
    row = lax.broadcasted_iota(jnp.int32, (n, packed), 1)
    select = jnp.where(row == main, 1.0, 0.0).astype(BF)
    last = jnp.zeros((n, part), F32)
    for j in range(4):
        cols = pl.ds(j * part, part)
        if j < 3:
            tail_select = jnp.where((row == tail) & (block == j), 1.0, 0.0).astype(BF)
            piece = ret_ref[:, cols]
            rows = dot(select, piece)
            last += dot(tail_select, piece)
        else:
            rows = last
        rows = jnp.where(routed, rows, out_grad_ref[:, cols].astype(F32))
        token_grad_ref[:, cols] = (gate * rows).astype(BF)
    terms = dot(select, ret_ref[:, 3 * part :])[:, :1]
    gate_grad_ref[...] = jnp.where(route_row < experts, to_row(terms), own_term_ref[...]).astype(BF)


def combine(route_row, gate_row, own_term, out_grad, ret):
    n, width = out_grad.shape
    return pl.pallas_call(
        combine_kernel,
        out_shape=(jax.ShapeDtypeStruct((n, width), BF), jax.ShapeDtypeStruct((1, n), BF)),
        compiler_params=pltpu.CompilerParams(vmem_limit_bytes=SMALL_VMEM),
        cost_estimate=pl.CostEstimate(
            flops=2 * ret.shape[0] * n * width * 3 // 2,
            bytes_accessed=2 * (2 * out_grad.size + ret.size),
            transcendentals=0,
        ),
        name="combine",
    )(route_row, gate_row, own_term, out_grad, ret)


def per_device(tokens, out_grad, gate, route, gate_weight, up_weight, down_weight):
    experts = lax.axis_size("expert")
    groups = lax.axis_size("tensor")
    n, width = tokens.shape
    swap = [(0, 1), (1, 0)]
    up = [(i, (i + 1) % groups) for i in range(groups)]
    down = [(i, (i - 1) % groups) for i in range(groups)]
    route_row = route.reshape(1, n)

    core = lax.axis_index("dp").reshape(1)
    weights = (gate_weight[0], up_weight[0], down_weight[0])
    head, up_rest, down_rest, tail = weight_parts(core, weights)
    up_head = lax.ppermute(head, "tensor", up)
    down_tail = lax.ppermute(tail, "tensor", down)
    from_up = lax.ppermute(up_rest, "tensor", up)
    from_down = lax.ppermute(down_rest, "tensor", down)
    far_head = lax.ppermute(up_head, "tensor", up)
    far_tail = lax.ppermute(down_tail, "tensor", down)

    route_row, head = lax.optimization_barrier((route_row, head))
    packed = pack(route_row, tokens, out_grad, experts)
    got = lax.all_to_all(
        packed.reshape(experts, ROWS, -1), "expert", split_axis=0, concat_axis=0, tiled=True
    ).reshape(experts * ROWS, -1)

    far_up, far_down = far_parts(from_up, from_down, ((0, 0, HALF - HEAD), (1, HALF, PARTS - HEAD)))
    got, far_up, far_down = lax.optimization_barrier((got, far_up, far_down))
    far_up = lax.ppermute(far_up, "tensor", up)
    far_down = lax.ppermute(far_down, "tensor", down)
    x, dy, far_head, far_tail = lax.optimization_barrier((*unpack(got), far_head, far_tail))
    x_other, dy_other = (lax.ppermute(rows, "dp", swap) for rows in (x, dy))

    part = width // UP_PARTS
    squares = lambda piece: piece.reshape(-1, part, 2 * part)
    blocks = [list(map(squares, b)) for b in ((head, up_rest), (up_head, from_up), (from_down, down_tail))]
    ranges = ((ENDS[0], RESTS[0]),) * 2 + ((RESTS[1], ENDS[1]),)
    far = (far_head, far_up, far_down, far_tail)
    far_ranges = (ENDS[0], (HEAD, HALF), (HALF, PARTS - HEAD), ENDS[1])
    own_sums, other_sums, own_terms, other_terms = first_blocks((x, x_other, dy, dy_other), blocks, ranges)
    far = list(map(squares, far))
    other_sums = last_block(x_other, dy_other, far, far_ranges, other_sums, other_terms)
    other_sums = lax.ppermute(other_sums, "dp", swap)
    own_sums = last_block(x, dy, far, far_ranges, own_sums, own_terms)
    back = add_pack(own_sums, other_sums).reshape(experts, ROWS, -1)
    ret = lax.all_to_all(back, "expert", split_axis=0, concat_axis=0, tiled=True)
    own_term = jnp.sum(out_grad.astype(F32) * tokens.astype(F32), axis=1)
    token_grad, gate_grad = combine(
        route_row, gate.reshape(1, n), own_term.reshape(1, n), out_grad, ret.reshape(experts * ROWS, -1)
    )
    return token_grad, gate_grad.reshape(n)


def solution(mesh):
    rows = P(("dp", "expert", "tensor"), None)
    return jax.shard_map(
        per_device,
        mesh=mesh,
        in_specs=(
            rows,
            rows,
            P(("dp", "expert", "tensor")),
            rows,
            P("expert", None, "tensor"),
            P("expert", None, "tensor"),
            P("expert", "tensor", None),
        ),
        out_specs=(rows, P(("dp", "expert", "tensor"))),
        check_vma=False,
    )
```

```python
import functools

import jax
import jax.numpy as jnp
from jax import lax
from jax.experimental import pallas as pl
from jax.experimental.pallas import tpu as pltpu
from jax.sharding import PartitionSpec as P

BF = jnp.bfloat16
F32 = jnp.float32
CAP = 6
ROWS = 8
TERM_LANES = 128
PARTS = 60
UP_PARTS = 40
HALF = 30
HEAD = 18
ENDS = ((0, HEAD), (PARTS - HEAD, PARTS))
RESTS = ((HEAD, PARTS), (0, PARTS - HEAD))
MIDDLE = (PARTS - 2 * HEAD) // 3
WEIGHT_CUTS = (0, HEAD, HEAD + MIDDLE, HEAD + 2 * MIDDLE, PARTS - HEAD, PARTS)
FAR_FLOPS = 62000000000
FIRST_FLOPS = 1000
LAST_FLOPS = 1000
VMEM_ALL = 56 * 1024 * 1024
SMALL_VMEM = 20 * 1024 * 1024
FIRST_VMEM = 38 * 1024 * 1024
LAST_VMEM = 24 * 1024 * 1024


def dot(a, b):
    return jnp.dot(a, b, preferred_element_type=F32)


def dot_t(a, b):
    return lax.dot_general(a, b, (((1,), (1,)), ((), ())), preferred_element_type=F32)


def in_turn(steps):
    def body(i, carry):
        for k, step in enumerate(steps):
            pl.when(i == k)(step)
        return carry

    lax.fori_loop(0, len(steps), body, 0)


def eye(n):
    return lax.broadcasted_iota(jnp.int32, (n, n), 0) == lax.broadcasted_iota(jnp.int32, (n, n), 1)


def to_column(row):
    n = row.shape[1]
    return jnp.sum(jnp.where(eye(n), jnp.broadcast_to(row, (n, n)), 0), axis=1, keepdims=True)


def to_row(column):
    n = column.shape[0]
    return jnp.sum(jnp.where(eye(n), jnp.broadcast_to(column, (n, n)), 0), axis=0, keepdims=True)


def places(route_row):
    n = route_row.shape[1]
    across = jnp.broadcast_to(route_row, (n, n))
    down = jnp.broadcast_to(to_column(route_row), (n, n))
    earlier = lax.broadcasted_iota(jnp.int32, (n, n), 0) < lax.broadcasted_iota(jnp.int32, (n, n), 1)
    slot = jnp.sum(jnp.where((across == down) & earlier, 1, 0), axis=0, keepdims=True)
    second = jnp.where(slot >= 3, 1, 0)
    base = route_row * ROWS
    return base + slot, base + CAP + second, slot - 3 * second


def pack_kernel(route_ref, x_hbm, dy_hbm, out_hbm, rows, out, in_sems, out_sems):
    n, total = route_ref.shape[1], out.shape[0]
    part = rows.shape[2]
    reads = []
    for i, src in enumerate((x_hbm, dy_hbm)):
        for j in range(3):
            k = 3 * i + j
            reads.append(
                [
                    pltpu.make_async_copy(
                        src.at[:, pl.ds(quarter * part, part)], rows.at[k, pl.ds(low, n)], in_sems.at[2 * k + low // n]
                    )
                    for quarter, low in ((j, 0), (3, n))
                ]
            )
            for copy in reads[-1]:
                copy.start()
    main, tail, block = places(route_ref[...])
    row = lax.broadcasted_iota(jnp.int32, (total, n), 0)
    select = jnp.where(row == main, 1.0, 0.0).astype(BF)
    selects = [
        jnp.concatenate([select, jnp.where((row == tail) & (block == j), 1.0, 0.0).astype(BF)], axis=1)
        for j in range(3)
    ]
    writes = []
    for k in range(6):
        for copy in reads[k]:
            copy.wait()
        cols = pl.ds(k * part, part)
        out[:, cols] = dot(selects[k % 3], rows[k]).astype(BF)
        writes.append(pltpu.make_async_copy(out.at[:, cols], out_hbm.at[:, cols], out_sems.at[k]))
        writes[-1].start()
    for write in writes:
        write.wait()


def pack(route_row, x, dy, experts):
    n, width = x.shape
    shape = (experts * ROWS, width // 4 * 6)
    any_spec = pl.BlockSpec(memory_space=pl.ANY)
    return pl.pallas_call(
        pack_kernel,
        out_shape=jax.ShapeDtypeStruct(shape, BF),
        in_specs=[pl.BlockSpec(memory_space=pltpu.VMEM), any_spec, any_spec],
        out_specs=any_spec,
        scratch_shapes=[
            pltpu.VMEM((6, 2 * n, width // 4), BF),
            pltpu.VMEM(shape, BF),
            pltpu.SemaphoreType.DMA((12,)),
            pltpu.SemaphoreType.DMA((6,)),
        ],
        compiler_params=pltpu.CompilerParams(vmem_limit_bytes=VMEM_ALL),
        cost_estimate=pl.CostEstimate(
            flops=2 * experts * ROWS * n * width * 3,
            bytes_accessed=4 * width * (n + experts * CAP),
            transcendentals=0,
        ),
        name="pack",
    )(route_row, x, dy)


def part_copies(weights, core, low, high, out, sem):
    gate, up, down = weights
    hidden, span = out.shape[0] // (high - low), out.shape[1]
    columns = pl.ds(pl.multiple_of(core * hidden, hidden), hidden)
    last_up = min(high, UP_PARTS)
    copies = []
    if low < last_up:
        rows = slice(low * hidden, last_up * hidden)
        for i, ref in enumerate((gate, up)):
            dst = out.at[0 : (last_up - low) * hidden, i * hidden : (i + 1) * hidden]
            copies.append(pltpu.make_async_copy(ref.at[rows, columns], dst, sem))
    for k in range(max(low, UP_PARTS), high):
        src = down.at[columns, (k - UP_PARTS) * span : (k - UP_PARTS + 1) * span]
        dst = out.at[(k - low) * hidden : (k - low + 1) * hidden, :]
        copies.append(pltpu.make_async_copy(src, dst, sem))
    return copies


def weights_kernel(core_ref, gate, up, down, head, up_rest, down_rest, tail, held, read_sems, write_sems):
    hidden = held.shape[1] // 2
    reads, waits, writes = [], [], []
    outs = ((head, ENDS[0]), (tail, ENDS[1]), (up_rest, RESTS[0]), (down_rest, RESTS[1]))
    count = 0
    for i, (low, high) in enumerate(zip(WEIGHT_CUTS, WEIGHT_CUTS[1:])):
        rows = held.at[pl.ds(low * hidden, (high - low) * hidden)]
        reads += part_copies((gate, up, down), core_ref[0], low, high, rows, read_sems.at[i])
        waits.append(pltpu.make_async_copy(rows, rows, read_sems.at[i]))
        writes.append([])
        for out, (first, last) in outs:
            if first <= low and high <= last:
                dst = out.at[pl.ds((low - first) * hidden, (high - low) * hidden)]
                writes[-1].append(pltpu.make_async_copy(rows, dst, write_sems.at[count]))
                count += 1
    for copy in reads:
        copy.start()

    def step(i):
        waits[i].wait()
        for copy in writes[i]:
            copy.start()

    in_turn([functools.partial(step, i) for i in range(len(waits))])
    for copies in writes:
        for copy in copies:
            copy.wait()


def weight_parts(core, weights):
    width, span = weights[0].shape
    hidden = span // 2
    any_spec = pl.BlockSpec(memory_space=pl.ANY)
    size = lambda parts: jax.ShapeDtypeStruct(((parts[1] - parts[0]) * hidden, span), BF)
    return pl.pallas_call(
        weights_kernel,
        out_shape=[size(parts) for parts in (ENDS[0],) + RESTS + (ENDS[1],)],
        in_specs=[pl.BlockSpec(memory_space=pltpu.SMEM)] + [any_spec] * 3,
        out_specs=[any_spec] * 4,
        scratch_shapes=[
            pltpu.VMEM((PARTS * hidden, span), BF),
            pltpu.SemaphoreType.DMA((len(WEIGHT_CUTS) - 1,)),
            pltpu.SemaphoreType.DMA((2 * len(WEIGHT_CUTS),)),
        ],
        compiler_params=pltpu.CompilerParams(vmem_limit_bytes=VMEM_ALL),
        cost_estimate=pl.CostEstimate(flops=0, bytes_accessed=6 * PARTS * hidden * span, transcendentals=0),
        name="weights",
    )(core, *weights)


def far_kernel(ranges, up_hbm, down_hbm, *refs):
    count = len(ranges)
    outs, held, sems = refs[:count], refs[count : 2 * count], refs[-1]
    reads, writes = [], []
    for i, (side, low, high) in enumerate(ranges):
        hidden = outs[i].shape[0] // (high - low)
        src = (up_hbm, down_hbm)[side].at[low * hidden : high * hidden, :]
        reads.append(pltpu.make_async_copy(src, held[i], sems.at[i]))
        writes.append(pltpu.make_async_copy(held[i], outs[i], sems.at[count + i]))
    for read in reads:
        read.start()
    for read, write in zip(reads, writes):
        read.wait()
        write.start()
    for write in writes:
        write.wait()


def far_parts(from_up, from_down, ranges):
    rows, span = from_up.shape
    hidden = span // 2
    any_spec = pl.BlockSpec(memory_space=pl.ANY)
    return pl.pallas_call(
        functools.partial(far_kernel, ranges),
        out_shape=[jax.ShapeDtypeStruct(((high - low) * hidden, span), BF) for _, low, high in ranges],
        in_specs=[any_spec] * 2,
        out_specs=[any_spec] * len(ranges),
        scratch_shapes=[pltpu.VMEM(((high - low) * hidden, span), BF) for _, low, high in ranges]
        + [pltpu.SemaphoreType.DMA((2 * len(ranges),))],
        compiler_params=pltpu.CompilerParams(vmem_limit_bytes=VMEM_ALL),
        cost_estimate=pl.CostEstimate(flops=FAR_FLOPS, bytes_accessed=0, transcendentals=0),
        name="far",
    )(from_up, from_down)


def block_copies(pieces, ranges, gu, down, place, sems):
    hidden, span = pieces[0].shape[1:]
    up_copies, down_copies = [], []
    for i, (piece, (low, high)) in enumerate(zip(pieces, ranges)):
        middle = min(max(low, UP_PARTS), high)
        if low < middle:
            up_copies.append(
                pltpu.make_async_copy(
                    piece.at[pl.ds(0, middle - low)],
                    gu.at[pl.ds(low, middle - low), :, pl.ds(place * span, span)],
                    sems.at[2 * i],
                )
            )
        if middle < high:
            down_copies.append(
                pltpu.make_async_copy(
                    piece.at[pl.ds(middle - low, high - middle)],
                    down.at[pl.ds(middle - UP_PARTS, high - middle), pl.ds(place * hidden, hidden)],
                    sems.at[2 * i + 1],
                )
            )
    return up_copies, down_copies


def slot_matrix(slots, packed, slot_dim, tail):
    shape = (slots, packed) if slot_dim == 0 else (packed, slots)
    slot = lax.broadcasted_iota(jnp.int32, shape, slot_dim)
    row = lax.broadcasted_iota(jnp.int32, shape, 1 - slot_dim)
    group, place = row >> 3, row & 7
    if tail is None:
        hit = (slot == group * CAP + place) & (place < CAP)
    else:
        hit = (slot == group * CAP + (place - CAP) * 3 + tail) & (place >= CAP)
    return jnp.where(hit, 1.0, 0.0).astype(BF)


def hidden_grads(x, dy, gu, down, pre, grads, x_copies, up_copies, dy_copies, down_copies):
    spans, total, span = down.shape
    blocks = len(up_copies)
    hidden = total // blocks
    width = x.shape[1]
    stages = [x_copies + up_copies[0]] + up_copies[1:] + [dy_copies + [c for copies in down_copies for c in copies]]

    def start(i):
        for copy in stages[i] if i < len(stages) else []:
            copy.start()

    def wait(i):
        for copy in stages[i]:
            copy.wait()

    def forward(b):
        wait(b)
        start(b + 2)
        cols = slice(b * span, (b + 1) * span)
        pre[:, cols] = dot(x[...], gu[:, :, cols].reshape(width, span))

    def finish():
        wait(blocks)
        back = dot_t(dy[:, :span], down[0])
        for k in range(1, spans):
            back += dot_t(dy[:, k * span : (k + 1) * span], down[k])
        terms = None
        for b in range(blocks):
            low = b * span
            pre_gate, pre_up = pre[:, low : low + hidden], pre[:, low + hidden : low + span]
            here = back[:, b * hidden : (b + 1) * hidden]
            s = jax.nn.sigmoid(pre_gate)
            activated = pre_gate * s
            slope = s * (1.0 + pre_gate * (1.0 - s))
            grads[:, low : low + hidden] = (here * pre_up * slope).astype(BF)
            grads[:, low + hidden : low + span] = (here * activated).astype(BF)
            term = activated * pre_up * here
            terms = term if terms is None else terms + term
        pre[:, :hidden] = terms

    start(0)
    start(1)
    return [functools.partial(forward, b) for b in range(blocks)] + [finish]


def row_grads(grads, gu, j):
    parts, hidden, columns = gu.shape
    rows = slice(j * parts // 4, (j + 1) * parts // 4)
    return dot_t(grads[...], gu[rows].reshape(parts // 4 * hidden, columns))


def unpack_kernel(rows_hbm, x_ref, dy_ref, rows, sems):
    packed = rows.shape[0]
    slots, width = x_ref.shape
    part = width // 4
    cols = [slice(j * part, (j + 1) * part) for j in range(6)]
    copies = [pltpu.make_async_copy(rows_hbm.at[:, c], rows.at[:, c], sems.at[j]) for j, c in enumerate(cols)]
    for copy in copies:
        copy.start()
    spread = slot_matrix(slots, packed, 0, None)
    spread_tail = [slot_matrix(slots, packed, 0, j) for j in range(3)]
    for k, out_ref in enumerate((x_ref, dy_ref)):
        last = None
        for j in range(3):
            copies[3 * k + j].wait()
            piece = rows[:, cols[3 * k + j]]
            out_ref[:, cols[j]] = dot(spread, piece).astype(BF)
            more = dot(spread_tail[j], piece)
            last = more if last is None else last + more
        out_ref[:, cols[3]] = last.astype(BF)


def unpack(rows):
    packed = rows.shape[0]
    slots, width = packed // ROWS * CAP, rows.shape[1] // 6 * 4
    return pl.pallas_call(
        unpack_kernel,
        out_shape=[jax.ShapeDtypeStruct((slots, width), BF)] * 2,
        in_specs=[pl.BlockSpec(memory_space=pl.ANY)],
        scratch_shapes=[pltpu.VMEM(rows.shape, BF), pltpu.SemaphoreType.DMA((6,))],
        compiler_params=pltpu.CompilerParams(vmem_limit_bytes=SMALL_VMEM),
        cost_estimate=pl.CostEstimate(flops=FIRST_FLOPS, bytes_accessed=FIRST_FLOPS, transcendentals=0),
        name="unpack",
    )(rows)


def first_kernel(ranges, *refs):
    row_refs, refs = refs[:4], refs[4:]
    pieces, refs = refs[: sum(map(len, ranges))], refs[sum(map(len, ranges)) :]
    own_hbm, other_hbm, own_term, other_term, x, dy, gu, down, pre, grads, total, sems = refs
    slots, part = x.shape[0] // 2, x.shape[1] // 4
    row_copies = [
        pltpu.make_async_copy(src, full.at[pl.ds(i * slots, slots)], sems.at[2 * k + i])
        for k, full in enumerate((x, dy))
        for i, src in enumerate(row_refs[2 * k : 2 * k + 2])
    ]
    up_copies, down_copies, used = [], [], 0
    for b, block in enumerate(ranges):
        here = pieces[used : used + len(block)]
        ups, downs = block_copies(here, block, gu, down, b, sems.at[pl.ds(12 + 2 * used, 2 * len(block))])
        used += len(block)
        up_copies.append(ups)
        down_copies.append(downs)
    steps = hidden_grads(x, dy, gu, down, pre, grads, row_copies[:2], up_copies, row_copies[2:], down_copies)
    columns = [pl.ds(j * part, part) for j in range(4)]
    outs = [
        [
            pltpu.make_async_copy(total.at[pl.ds(i * slots, slots), cols], out.at[:, cols], sems.at[4 + 2 * j + i])
            for i, out in enumerate((own_hbm, other_hbm))
        ]
        for j, cols in enumerate(columns)
    ]

    def backward(j):
        total[:, columns[j]] = row_grads(grads, gu, j).astype(BF)
        for copy in outs[j]:
            copy.start()

    in_turn(steps + [functools.partial(backward, j) for j in range(4)])
    hidden = own_term.shape[1]
    own_term[...] = pre[:slots, :hidden]
    other_term[...] = pre[slots:, :hidden]
    for copies in outs:
        for copy in copies:
            copy.wait()


def first_blocks(rows, blocks, ranges):
    slots, width = rows[0].shape
    hidden, span = blocks[0][0].shape[1:]
    count = len(blocks)
    pieces = [piece for block in blocks for piece in block]
    any_spec = pl.BlockSpec(memory_space=pl.ANY)
    vmem_spec = pl.BlockSpec(memory_space=pltpu.VMEM)
    return pl.pallas_call(
        functools.partial(first_kernel, ranges),
        out_shape=[jax.ShapeDtypeStruct((slots, width), BF)] * 2 + [jax.ShapeDtypeStruct((slots, hidden), F32)] * 2,
        in_specs=[any_spec] * (4 + len(pieces)),
        out_specs=[any_spec] * 2 + [vmem_spec] * 2,
        scratch_shapes=[
            pltpu.VMEM((2 * slots, width), BF),
            pltpu.VMEM((2 * slots, width), BF),
            pltpu.VMEM((UP_PARTS, hidden, count * span), BF),
            pltpu.VMEM((PARTS - UP_PARTS, count * hidden, span), BF),
            pltpu.VMEM((2 * slots, count * span), F32),
            pltpu.VMEM((2 * slots, count * span), BF),
            pltpu.VMEM((2 * slots, width), BF),
            pltpu.SemaphoreType.DMA((12 + 2 * len(pieces),)),
        ],
        compiler_params=pltpu.CompilerParams(vmem_limit_bytes=FIRST_VMEM),
        cost_estimate=pl.CostEstimate(flops=FIRST_FLOPS, bytes_accessed=FIRST_FLOPS, transcendentals=0),
        name="first",
    )(*rows, *pieces)


def last_kernel(ranges, *refs):
    x_hbm, dy_hbm, refs = refs[0], refs[1], refs[2:]
    pieces, refs = refs[: len(ranges)], refs[len(ranges) :]
    sum_hbm, term_ref, out_ref, x, dy, gu, down, total, pre, grads, sems = refs
    slots, part = x.shape[0], x.shape[1] // 4
    x_copy = pltpu.make_async_copy(x_hbm, x, sems.at[0])
    dy_copy = pltpu.make_async_copy(dy_hbm, dy, sems.at[1])
    sum_copy = pltpu.make_async_copy(sum_hbm, total, sems.at[2])
    up_copies, down_copies = block_copies(pieces, ranges, gu, down, 0, sems.at[pl.ds(3, 2 * len(ranges))])
    steps = hidden_grads(
        x, dy, gu, down, pre, grads, [x_copy], [up_copies], [dy_copy], [down_copies + [sum_copy]]
    )

    def backward():
        for j in range(4):
            cols = slice(j * part, (j + 1) * part)
            out_ref[:, cols] = (total[:, cols].astype(F32) + row_grads(grads, gu, j)).astype(BF)
        terms = jnp.sum(pre[:, : term_ref.shape[1]] + term_ref[...], axis=1, keepdims=True)
        out_ref[:, 4 * part :] = jnp.broadcast_to(terms, (slots, TERM_LANES)).astype(BF)

    in_turn(steps + [backward])


def last_block(x, dy, pieces, ranges, total, term):
    rows, width = total.shape
    hidden, span = pieces[0].shape[1:]
    any_spec = pl.BlockSpec(memory_space=pl.ANY)
    vmem_spec = pl.BlockSpec(memory_space=pltpu.VMEM)
    return pl.pallas_call(
        functools.partial(last_kernel, ranges),
        out_shape=jax.ShapeDtypeStruct((rows, width + TERM_LANES), BF),
        in_specs=[any_spec] * (len(pieces) + 3) + [vmem_spec],
        out_specs=vmem_spec,
        scratch_shapes=[
            pltpu.VMEM((rows, width), BF),
            pltpu.VMEM((rows, width), BF),
            pltpu.VMEM((UP_PARTS, hidden, span), BF),
            pltpu.VMEM((PARTS - UP_PARTS, hidden, span), BF),
            pltpu.VMEM((rows, width), BF),
            pltpu.VMEM((rows, span), F32),
            pltpu.VMEM((rows, span), BF),
            pltpu.SemaphoreType.DMA((3 + 2 * len(pieces),)),
        ],
        compiler_params=pltpu.CompilerParams(vmem_limit_bytes=LAST_VMEM),
        cost_estimate=pl.CostEstimate(flops=LAST_FLOPS, bytes_accessed=LAST_FLOPS, transcendentals=0),
        name="last",
    )(x, dy, *pieces, total, term)


def add_pack_kernel(a_ref, b_ref, out_ref):
    slots, packed = a_ref.shape[0], out_ref.shape[0]
    part = (a_ref.shape[1] - TERM_LANES) // 4
    gather = slot_matrix(slots, packed, 1, None)
    gather_tail = [slot_matrix(slots, packed, 1, j) for j in range(3)]

    def total(low, size):
        cols = pl.ds(low, size)
        return (a_ref[:, cols].astype(F32) + b_ref[:, cols].astype(F32)).astype(BF)

    out_ref[:, 3 * part :] = dot(gather, total(4 * part, TERM_LANES)).astype(BF)
    last = total(3 * part, part)
    for j in range(3):
        out_ref[:, j * part : (j + 1) * part] = (
            dot(gather, total(j * part, part)) + dot(gather_tail[j], last)
        ).astype(BF)


def add_pack(a, b):
    slots, columns = a.shape
    packed, part = slots // CAP * ROWS, (columns - TERM_LANES) // 4
    return pl.pallas_call(
        add_pack_kernel,
        out_shape=jax.ShapeDtypeStruct((packed, 3 * part + TERM_LANES), BF),
        compiler_params=pltpu.CompilerParams(vmem_limit_bytes=SMALL_VMEM),
        cost_estimate=pl.CostEstimate(
            flops=2 * packed * slots * part * 6, bytes_accessed=6 * slots * columns, transcendentals=0
        ),
        name="add_pack",
    )(a, b)


def combine_kernel(route_ref, gate_ref, own_term_ref, out_grad_ref, ret_ref, token_grad_ref, gate_grad_ref):
    n, width = out_grad_ref.shape
    packed = ret_ref.shape[0]
    part = width // 4
    experts = packed // ROWS
    route_row = route_ref[...]
    main, tail, block = (to_column(v) for v in places(route_row))
    routed = to_column(route_row) < experts
    gate = to_column(gate_ref[...])
    row = lax.broadcasted_iota(jnp.int32, (n, packed), 1)
    select = jnp.where(row == main, 1.0, 0.0).astype(BF)
    last = jnp.zeros((n, part), F32)
    for j in range(4):
        cols = pl.ds(j * part, part)
        if j < 3:
            tail_select = jnp.where((row == tail) & (block == j), 1.0, 0.0).astype(BF)
            piece = ret_ref[:, cols]
            rows = dot(select, piece)
            last += dot(tail_select, piece)
        else:
            rows = last
        rows = jnp.where(routed, rows, out_grad_ref[:, cols].astype(F32))
        token_grad_ref[:, cols] = (gate * rows).astype(BF)
    terms = dot(select, ret_ref[:, 3 * part :])[:, :1]
    gate_grad_ref[...] = jnp.where(route_row < experts, to_row(terms), own_term_ref[...]).astype(BF)


def combine(route_row, gate_row, own_term, out_grad, ret):
    n, width = out_grad.shape
    return pl.pallas_call(
        combine_kernel,
        out_shape=(jax.ShapeDtypeStruct((n, width), BF), jax.ShapeDtypeStruct((1, n), BF)),
        compiler_params=pltpu.CompilerParams(vmem_limit_bytes=SMALL_VMEM),
        cost_estimate=pl.CostEstimate(
            flops=2 * ret.shape[0] * n * width * 3 // 2,
            bytes_accessed=2 * (2 * out_grad.size + ret.size),
            transcendentals=0,
        ),
        name="combine",
    )(route_row, gate_row, own_term, out_grad, ret)


def per_device(tokens, out_grad, gate, route, gate_weight, up_weight, down_weight):
    experts = lax.axis_size("expert")
    groups = lax.axis_size("tensor")
    n, width = tokens.shape
    swap = [(0, 1), (1, 0)]
    up = [(i, (i + 1) % groups) for i in range(groups)]
    down = [(i, (i - 1) % groups) for i in range(groups)]
    route_row = route.reshape(1, n)

    core = lax.axis_index("dp").reshape(1)
    weights = (gate_weight[0], up_weight[0], down_weight[0])
    head, up_rest, down_rest, tail = weight_parts(core, weights)
    up_head = lax.ppermute(head, "tensor", up)
    down_tail = lax.ppermute(tail, "tensor", down)
    from_up = lax.ppermute(up_rest, "tensor", up)
    from_down = lax.ppermute(down_rest, "tensor", down)
    far_head = lax.ppermute(up_head, "tensor", up)
    far_tail = lax.ppermute(down_tail, "tensor", down)

    route_row, head = lax.optimization_barrier((route_row, head))
    packed = pack(route_row, tokens, out_grad, experts)
    got = lax.all_to_all(
        packed.reshape(experts, ROWS, -1), "expert", split_axis=0, concat_axis=0, tiled=True
    ).reshape(experts * ROWS, -1)

    far_up, far_down = far_parts(from_up, from_down, ((0, 0, HALF - HEAD), (1, HALF, PARTS - HEAD)))
    got, far_up, far_down = lax.optimization_barrier((got, far_up, far_down))
    far_up = lax.ppermute(far_up, "tensor", up)
    far_down = lax.ppermute(far_down, "tensor", down)
    x, dy, far_head, far_tail = lax.optimization_barrier((*unpack(got), far_head, far_tail))
    x_other, dy_other = (lax.ppermute(rows, "dp", swap) for rows in (x, dy))

    part = width // UP_PARTS
    squares = lambda piece: piece.reshape(-1, part, 2 * part)
    blocks = [list(map(squares, b)) for b in ((head, up_rest), (up_head, from_up), (from_down, down_tail))]
    ranges = ((ENDS[0], RESTS[0]),) * 2 + ((RESTS[1], ENDS[1]),)
    far = (far_head, far_up, far_down, far_tail)
    far_ranges = (ENDS[0], (HEAD, HALF), (HALF, PARTS - HEAD), ENDS[1])
    own_sums, other_sums, own_terms, other_terms = first_blocks((x, x_other, dy, dy_other), blocks, ranges)
    far = list(map(squares, far))
    other_sums = last_block(x_other, dy_other, far, far_ranges, other_sums, other_terms)
    other_sums = lax.ppermute(other_sums, "dp", swap)
    own_sums = last_block(x, dy, far, far_ranges, own_sums, own_terms)
    back = add_pack(own_sums, other_sums).reshape(experts, ROWS, -1)
    ret = lax.all_to_all(back, "expert", split_axis=0, concat_axis=0, tiled=True)
    own_term = jnp.sum(out_grad.astype(F32) * tokens.astype(F32), axis=1)
    token_grad, gate_grad = combine(
        route_row, gate.reshape(1, n), own_term.reshape(1, n), out_grad, ret.reshape(experts * ROWS, -1)
    )
    return token_grad, gate_grad.reshape(n)


def solution(mesh):
    rows = P(("dp", "expert", "tensor"), None)
    return jax.shard_map(
        per_device,
        mesh=mesh,
        in_specs=(
            rows,
            rows,
            P(("dp", "expert", "tensor")),
            rows,
            P("expert", None, "tensor"),
            P("expert", None, "tensor"),
            P("expert", "tensor", None),
        ),
        out_specs=(rows, P(("dp", "expert", "tensor"))),
        check_vma=False,
    )
```

```python
import functools

import jax
import jax.numpy as jnp
from jax import lax
from jax.experimental import pallas as pl
from jax.experimental.pallas import tpu as pltpu
from jax.sharding import PartitionSpec as P

BF = jnp.bfloat16
F32 = jnp.float32
CAP = 6
ROWS = 8
TERM_LANES = 128
PARTS = 60
UP_PARTS = 40
HALF = 30
FAR = 17
HALVES = ((0, HALF), (HALF, PARTS))
WEIGHT_CUTS = (0, 15, 30, 45, 60)
FAR_FLOPS = (50000000000, 75000000000)
FIRST_FLOPS = 1000
LAST_FLOPS = 1000
VMEM_ALL = 56 * 1024 * 1024
SMALL_VMEM = 20 * 1024 * 1024
FIRST_VMEM = 38 * 1024 * 1024
LAST_VMEM = 24 * 1024 * 1024


def dot(a, b):
    return jnp.dot(a, b, preferred_element_type=F32)


def dot_t(a, b):
    return lax.dot_general(a, b, (((1,), (1,)), ((), ())), preferred_element_type=F32)


def in_turn(steps):
    def body(i, carry):
        for k, step in enumerate(steps):
            pl.when(i == k)(step)
        return carry

    lax.fori_loop(0, len(steps), body, 0)


def eye(n):
    return lax.broadcasted_iota(jnp.int32, (n, n), 0) == lax.broadcasted_iota(jnp.int32, (n, n), 1)


def to_column(row):
    n = row.shape[1]
    return jnp.sum(jnp.where(eye(n), jnp.broadcast_to(row, (n, n)), 0), axis=1, keepdims=True)


def to_row(column):
    n = column.shape[0]
    return jnp.sum(jnp.where(eye(n), jnp.broadcast_to(column, (n, n)), 0), axis=0, keepdims=True)


def places(route_row):
    n = route_row.shape[1]
    across = jnp.broadcast_to(route_row, (n, n))
    down = jnp.broadcast_to(to_column(route_row), (n, n))
    earlier = lax.broadcasted_iota(jnp.int32, (n, n), 0) < lax.broadcasted_iota(jnp.int32, (n, n), 1)
    slot = jnp.sum(jnp.where((across == down) & earlier, 1, 0), axis=0, keepdims=True)
    second = jnp.where(slot >= 3, 1, 0)
    base = route_row * ROWS
    return base + slot, base + CAP + second, slot - 3 * second


def pack_kernel(route_ref, x_hbm, dy_hbm, out_hbm, rows, out, in_sems, out_sems):
    n, total = route_ref.shape[1], out.shape[0]
    part = rows.shape[2]
    reads = []
    for i, src in enumerate((x_hbm, dy_hbm)):
        for j in range(3):
            k = 3 * i + j
            reads.append(
                [
                    pltpu.make_async_copy(
                        src.at[:, pl.ds(quarter * part, part)], rows.at[k, pl.ds(low, n)], in_sems.at[2 * k + low // n]
                    )
                    for quarter, low in ((j, 0), (3, n))
                ]
            )
            for copy in reads[-1]:
                copy.start()
    main, tail, block = places(route_ref[...])
    row = lax.broadcasted_iota(jnp.int32, (total, n), 0)
    select = jnp.where(row == main, 1.0, 0.0).astype(BF)
    selects = [
        jnp.concatenate([select, jnp.where((row == tail) & (block == j), 1.0, 0.0).astype(BF)], axis=1)
        for j in range(3)
    ]
    writes = []
    for k in range(6):
        for copy in reads[k]:
            copy.wait()
        cols = pl.ds(k * part, part)
        out[:, cols] = dot(selects[k % 3], rows[k]).astype(BF)
        writes.append(pltpu.make_async_copy(out.at[:, cols], out_hbm.at[:, cols], out_sems.at[k]))
        writes[-1].start()
    for write in writes:
        write.wait()


def pack(route_row, x, dy, experts):
    n, width = x.shape
    shape = (experts * ROWS, width // 4 * 6)
    any_spec = pl.BlockSpec(memory_space=pl.ANY)
    return pl.pallas_call(
        pack_kernel,
        out_shape=jax.ShapeDtypeStruct(shape, BF),
        in_specs=[pl.BlockSpec(memory_space=pltpu.VMEM), any_spec, any_spec],
        out_specs=any_spec,
        scratch_shapes=[
            pltpu.VMEM((6, 2 * n, width // 4), BF),
            pltpu.VMEM(shape, BF),
            pltpu.SemaphoreType.DMA((12,)),
            pltpu.SemaphoreType.DMA((6,)),
        ],
        compiler_params=pltpu.CompilerParams(vmem_limit_bytes=VMEM_ALL),
        cost_estimate=pl.CostEstimate(
            flops=2 * experts * ROWS * n * width * 3,
            bytes_accessed=4 * width * (n + experts * CAP),
            transcendentals=0,
        ),
        name="pack",
    )(route_row, x, dy)


def part_copies(weights, core, low, high, out, sem):
    gate, up, down = weights
    hidden, span = out.shape[0] // (high - low), out.shape[1]
    columns = pl.ds(pl.multiple_of(core * hidden, hidden), hidden)
    last_up = min(high, UP_PARTS)
    copies = []
    if low < last_up:
        rows = slice(low * hidden, last_up * hidden)
        for i, ref in enumerate((gate, up)):
            dst = out.at[0 : (last_up - low) * hidden, i * hidden : (i + 1) * hidden]
            copies.append(pltpu.make_async_copy(ref.at[rows, columns], dst, sem))
    for k in range(max(low, UP_PARTS), high):
        src = down.at[columns, (k - UP_PARTS) * span : (k - UP_PARTS + 1) * span]
        dst = out.at[(k - low) * hidden : (k - low + 1) * hidden, :]
        copies.append(pltpu.make_async_copy(src, dst, sem))
    return copies


def weights_kernel(core_ref, gate, up, down, low_half, high_half, held, read_sems, write_sems):
    hidden = held.shape[1] // 2
    reads, waits, writes = [], [], []
    outs = tuple(zip((low_half, high_half), HALVES))
    count = 0
    for i, (low, high) in enumerate(zip(WEIGHT_CUTS, WEIGHT_CUTS[1:])):
        rows = held.at[pl.ds(low * hidden, (high - low) * hidden)]
        reads += part_copies((gate, up, down), core_ref[0], low, high, rows, read_sems.at[i])
        waits.append(pltpu.make_async_copy(rows, rows, read_sems.at[i]))
        writes.append([])
        for out, (first, last) in outs:
            if first <= low and high <= last:
                dst = out.at[pl.ds((low - first) * hidden, (high - low) * hidden)]
                writes[-1].append(pltpu.make_async_copy(rows, dst, write_sems.at[count]))
                count += 1
    for copy in reads:
        copy.start()

    def step(i):
        waits[i].wait()
        for copy in writes[i]:
            copy.start()

    in_turn([functools.partial(step, i) for i in range(len(waits))])
    for copies in writes:
        for copy in copies:
            copy.wait()


def weight_parts(core, weights):
    width, span = weights[0].shape
    hidden = span // 2
    any_spec = pl.BlockSpec(memory_space=pl.ANY)
    size = lambda parts: jax.ShapeDtypeStruct(((parts[1] - parts[0]) * hidden, span), BF)
    return pl.pallas_call(
        weights_kernel,
        out_shape=[size(parts) for parts in HALVES],
        in_specs=[pl.BlockSpec(memory_space=pltpu.SMEM)] + [any_spec] * 3,
        out_specs=[any_spec] * 2,
        scratch_shapes=[
            pltpu.VMEM((PARTS * hidden, span), BF),
            pltpu.SemaphoreType.DMA((len(WEIGHT_CUTS) - 1,)),
            pltpu.SemaphoreType.DMA((2 * len(WEIGHT_CUTS),)),
        ],
        compiler_params=pltpu.CompilerParams(vmem_limit_bytes=VMEM_ALL),
        cost_estimate=pl.CostEstimate(flops=0, bytes_accessed=6 * PARTS * hidden * span, transcendentals=0),
        name="weights",
    )(core, *weights)


def far_kernel(ranges, up_hbm, down_hbm, *refs):
    count = len(ranges)
    outs, held, sems = refs[:count], refs[count : 2 * count], refs[-1]
    reads, writes = [], []
    for i, (side, low, high) in enumerate(ranges):
        hidden = outs[i].shape[0] // (high - low)
        src = (up_hbm, down_hbm)[side].at[low * hidden : high * hidden, :]
        reads.append(pltpu.make_async_copy(src, held[i], sems.at[i]))
        writes.append(pltpu.make_async_copy(held[i], outs[i], sems.at[count + i]))
    for read in reads:
        read.start()
    for read, write in zip(reads, writes):
        read.wait()
        write.start()
    for write in writes:
        write.wait()


def far_parts(from_up, from_down, ranges, flops):
    rows, span = from_up.shape
    hidden = span // 2
    any_spec = pl.BlockSpec(memory_space=pl.ANY)
    return pl.pallas_call(
        functools.partial(far_kernel, ranges),
        out_shape=[jax.ShapeDtypeStruct(((high - low) * hidden, span), BF) for _, low, high in ranges],
        in_specs=[any_spec] * 2,
        out_specs=[any_spec] * len(ranges),
        scratch_shapes=[pltpu.VMEM(((high - low) * hidden, span), BF) for _, low, high in ranges]
        + [pltpu.SemaphoreType.DMA((2 * len(ranges),))],
        compiler_params=pltpu.CompilerParams(vmem_limit_bytes=VMEM_ALL),
        cost_estimate=pl.CostEstimate(flops=flops, bytes_accessed=0, transcendentals=0),
        name="far",
    )(from_up, from_down)


def block_copies(pieces, ranges, gu, down, place, sems):
    hidden, span = pieces[0].shape[1:]
    up_copies, down_copies = [], []
    for i, (piece, (low, high)) in enumerate(zip(pieces, ranges)):
        middle = min(max(low, UP_PARTS), high)
        if low < middle:
            up_copies.append(
                pltpu.make_async_copy(
                    piece.at[pl.ds(0, middle - low)],
                    gu.at[pl.ds(low, middle - low), :, pl.ds(place * span, span)],
                    sems.at[2 * i],
                )
            )
        if middle < high:
            down_copies.append(
                pltpu.make_async_copy(
                    piece.at[pl.ds(middle - low, high - middle)],
                    down.at[pl.ds(middle - UP_PARTS, high - middle), pl.ds(place * hidden, hidden)],
                    sems.at[2 * i + 1],
                )
            )
    return up_copies, down_copies


def slot_matrix(slots, packed, slot_dim, tail):
    shape = (slots, packed) if slot_dim == 0 else (packed, slots)
    slot = lax.broadcasted_iota(jnp.int32, shape, slot_dim)
    row = lax.broadcasted_iota(jnp.int32, shape, 1 - slot_dim)
    group, place = row >> 3, row & 7
    if tail is None:
        hit = (slot == group * CAP + place) & (place < CAP)
    else:
        hit = (slot == group * CAP + (place - CAP) * 3 + tail) & (place >= CAP)
    return jnp.where(hit, 1.0, 0.0).astype(BF)


def hidden_grads(x, dy, gu, down, pre, grads, x_copies, up_copies, dy_copies, down_copies):
    spans, total, span = down.shape
    blocks = len(up_copies)
    hidden = total // blocks
    width = x.shape[1]
    stages = [x_copies + up_copies[0]] + up_copies[1:] + [dy_copies + [c for copies in down_copies for c in copies]]

    def start(i):
        for copy in stages[i] if i < len(stages) else []:
            copy.start()

    def wait(i):
        for copy in stages[i]:
            copy.wait()

    def forward(b):
        wait(b)
        start(b + 2)
        cols = slice(b * span, (b + 1) * span)
        pre[:, cols] = dot(x[...], gu[:, :, cols].reshape(width, span))

    def finish():
        wait(blocks)
        back = dot_t(dy[:, :span], down[0])
        for k in range(1, spans):
            back += dot_t(dy[:, k * span : (k + 1) * span], down[k])
        terms = None
        for b in range(blocks):
            low = b * span
            pre_gate, pre_up = pre[:, low : low + hidden], pre[:, low + hidden : low + span]
            here = back[:, b * hidden : (b + 1) * hidden]
            s = jax.nn.sigmoid(pre_gate)
            activated = pre_gate * s
            slope = s * (1.0 + pre_gate * (1.0 - s))
            grads[:, low : low + hidden] = (here * pre_up * slope).astype(BF)
            grads[:, low + hidden : low + span] = (here * activated).astype(BF)
            term = activated * pre_up * here
            terms = term if terms is None else terms + term
        pre[:, :hidden] = terms

    start(0)
    start(1)
    return [functools.partial(forward, b) for b in range(blocks)] + [finish]


def row_grads(grads, gu, j):
    parts, hidden, columns = gu.shape
    rows = slice(j * parts // 4, (j + 1) * parts // 4)
    return dot_t(grads[...], gu[rows].reshape(parts // 4 * hidden, columns))


def unpack_kernel(rows_hbm, x_ref, dy_ref, rows, sems):
    packed = rows.shape[0]
    slots, width = x_ref.shape
    part = width // 4
    cols = [slice(j * part, (j + 1) * part) for j in range(6)]
    copies = [pltpu.make_async_copy(rows_hbm.at[:, c], rows.at[:, c], sems.at[j]) for j, c in enumerate(cols)]
    for copy in copies:
        copy.start()
    spread = slot_matrix(slots, packed, 0, None)
    spread_tail = [slot_matrix(slots, packed, 0, j) for j in range(3)]
    for k, out_ref in enumerate((x_ref, dy_ref)):
        last = None
        for j in range(3):
            copies[3 * k + j].wait()
            piece = rows[:, cols[3 * k + j]]
            out_ref[:, cols[j]] = dot(spread, piece).astype(BF)
            more = dot(spread_tail[j], piece)
            last = more if last is None else last + more
        out_ref[:, cols[3]] = last.astype(BF)


def unpack(rows):
    packed = rows.shape[0]
    slots, width = packed // ROWS * CAP, rows.shape[1] // 6 * 4
    return pl.pallas_call(
        unpack_kernel,
        out_shape=[jax.ShapeDtypeStruct((slots, width), BF)] * 2,
        in_specs=[pl.BlockSpec(memory_space=pl.ANY)],
        scratch_shapes=[pltpu.VMEM(rows.shape, BF), pltpu.SemaphoreType.DMA((6,))],
        compiler_params=pltpu.CompilerParams(vmem_limit_bytes=SMALL_VMEM),
        cost_estimate=pl.CostEstimate(flops=FIRST_FLOPS, bytes_accessed=FIRST_FLOPS, transcendentals=0),
        name="unpack",
    )(rows)


def first_kernel(ranges, *refs):
    row_refs, refs = refs[:4], refs[4:]
    pieces, refs = refs[: sum(map(len, ranges))], refs[sum(map(len, ranges)) :]
    own_hbm, other_hbm, own_term, other_term, x, dy, gu, down, pre, grads, total, sems = refs
    slots, part = x.shape[0] // 2, x.shape[1] // 4
    row_copies = [
        pltpu.make_async_copy(src, full.at[pl.ds(i * slots, slots)], sems.at[2 * k + i])
        for k, full in enumerate((x, dy))
        for i, src in enumerate(row_refs[2 * k : 2 * k + 2])
    ]
    up_copies, down_copies, used = [], [], 0
    for b, block in enumerate(ranges):
        here = pieces[used : used + len(block)]
        ups, downs = block_copies(here, block, gu, down, b, sems.at[pl.ds(12 + 2 * used, 2 * len(block))])
        used += len(block)
        up_copies.append(ups)
        down_copies.append(downs)
    steps = hidden_grads(x, dy, gu, down, pre, grads, row_copies[:2], up_copies, row_copies[2:], down_copies)
    columns = [pl.ds(j * part, part) for j in range(4)]
    outs = [
        [
            pltpu.make_async_copy(total.at[pl.ds(i * slots, slots), cols], out.at[:, cols], sems.at[4 + 2 * j + i])
            for i, out in enumerate((own_hbm, other_hbm))
        ]
        for j, cols in enumerate(columns)
    ]

    def backward(j):
        total[:, columns[j]] = row_grads(grads, gu, j).astype(BF)
        for copy in outs[j]:
            copy.start()

    in_turn(steps + [functools.partial(backward, j) for j in range(4)])
    hidden = own_term.shape[1]
    own_term[...] = pre[:slots, :hidden]
    other_term[...] = pre[slots:, :hidden]
    for copies in outs:
        for copy in copies:
            copy.wait()


def first_blocks(rows, blocks, ranges):
    slots, width = rows[0].shape
    hidden, span = blocks[0][0].shape[1:]
    count = len(blocks)
    pieces = [piece for block in blocks for piece in block]
    any_spec = pl.BlockSpec(memory_space=pl.ANY)
    vmem_spec = pl.BlockSpec(memory_space=pltpu.VMEM)
    return pl.pallas_call(
        functools.partial(first_kernel, ranges),
        out_shape=[jax.ShapeDtypeStruct((slots, width), BF)] * 2 + [jax.ShapeDtypeStruct((slots, hidden), F32)] * 2,
        in_specs=[any_spec] * (4 + len(pieces)),
        out_specs=[any_spec] * 2 + [vmem_spec] * 2,
        scratch_shapes=[
            pltpu.VMEM((2 * slots, width), BF),
            pltpu.VMEM((2 * slots, width), BF),
            pltpu.VMEM((UP_PARTS, hidden, count * span), BF),
            pltpu.VMEM((PARTS - UP_PARTS, count * hidden, span), BF),
            pltpu.VMEM((2 * slots, count * span), F32),
            pltpu.VMEM((2 * slots, count * span), BF),
            pltpu.VMEM((2 * slots, width), BF),
            pltpu.SemaphoreType.DMA((12 + 2 * len(pieces),)),
        ],
        compiler_params=pltpu.CompilerParams(vmem_limit_bytes=FIRST_VMEM),
        cost_estimate=pl.CostEstimate(flops=FIRST_FLOPS, bytes_accessed=FIRST_FLOPS, transcendentals=0),
        name="first",
    )(*rows, *pieces)


def last_kernel(ranges, *refs):
    x_hbm, dy_hbm, refs = refs[0], refs[1], refs[2:]
    pieces, refs = refs[: len(ranges)], refs[len(ranges) :]
    sum_hbm, term_ref, out_ref, x, dy, gu, down, total, pre, grads, sems = refs
    slots, part = x.shape[0], x.shape[1] // 4
    x_copy = pltpu.make_async_copy(x_hbm, x, sems.at[0])
    dy_copy = pltpu.make_async_copy(dy_hbm, dy, sems.at[1])
    sum_copy = pltpu.make_async_copy(sum_hbm, total, sems.at[2])
    up_copies, down_copies = block_copies(pieces, ranges, gu, down, 0, sems.at[pl.ds(3, 2 * len(ranges))])
    steps = hidden_grads(
        x, dy, gu, down, pre, grads, [x_copy], [up_copies], [dy_copy], [down_copies + [sum_copy]]
    )

    def backward():
        for j in range(4):
            cols = slice(j * part, (j + 1) * part)
            out_ref[:, cols] = (total[:, cols].astype(F32) + row_grads(grads, gu, j)).astype(BF)
        terms = jnp.sum(pre[:, : term_ref.shape[1]] + term_ref[...], axis=1, keepdims=True)
        out_ref[:, 4 * part :] = jnp.broadcast_to(terms, (slots, TERM_LANES)).astype(BF)

    in_turn(steps + [backward])


def last_block(x, dy, pieces, ranges, total, term):
    rows, width = total.shape
    hidden, span = pieces[0].shape[1:]
    any_spec = pl.BlockSpec(memory_space=pl.ANY)
    vmem_spec = pl.BlockSpec(memory_space=pltpu.VMEM)
    return pl.pallas_call(
        functools.partial(last_kernel, ranges),
        out_shape=jax.ShapeDtypeStruct((rows, width + TERM_LANES), BF),
        in_specs=[any_spec] * (len(pieces) + 3) + [vmem_spec],
        out_specs=vmem_spec,
        scratch_shapes=[
            pltpu.VMEM((rows, width), BF),
            pltpu.VMEM((rows, width), BF),
            pltpu.VMEM((UP_PARTS, hidden, span), BF),
            pltpu.VMEM((PARTS - UP_PARTS, hidden, span), BF),
            pltpu.VMEM((rows, width), BF),
            pltpu.VMEM((rows, span), F32),
            pltpu.VMEM((rows, span), BF),
            pltpu.SemaphoreType.DMA((3 + 2 * len(pieces),)),
        ],
        compiler_params=pltpu.CompilerParams(vmem_limit_bytes=LAST_VMEM),
        cost_estimate=pl.CostEstimate(flops=LAST_FLOPS, bytes_accessed=LAST_FLOPS, transcendentals=0),
        name="last",
    )(x, dy, *pieces, total, term)


def add_pack_kernel(a_ref, b_ref, out_ref):
    slots, packed = a_ref.shape[0], out_ref.shape[0]
    part = (a_ref.shape[1] - TERM_LANES) // 4
    gather = slot_matrix(slots, packed, 1, None)
    gather_tail = [slot_matrix(slots, packed, 1, j) for j in range(3)]

    def total(low, size):
        cols = pl.ds(low, size)
        return (a_ref[:, cols].astype(F32) + b_ref[:, cols].astype(F32)).astype(BF)

    out_ref[:, 3 * part :] = dot(gather, total(4 * part, TERM_LANES)).astype(BF)
    last = total(3 * part, part)
    for j in range(3):
        out_ref[:, j * part : (j + 1) * part] = (
            dot(gather, total(j * part, part)) + dot(gather_tail[j], last)
        ).astype(BF)


def add_pack(a, b):
    slots, columns = a.shape
    packed, part = slots // CAP * ROWS, (columns - TERM_LANES) // 4
    return pl.pallas_call(
        add_pack_kernel,
        out_shape=jax.ShapeDtypeStruct((packed, 3 * part + TERM_LANES), BF),
        compiler_params=pltpu.CompilerParams(vmem_limit_bytes=SMALL_VMEM),
        cost_estimate=pl.CostEstimate(
            flops=2 * packed * slots * part * 6, bytes_accessed=6 * slots * columns, transcendentals=0
        ),
        name="add_pack",
    )(a, b)


def combine_kernel(route_ref, gate_ref, own_term_ref, out_grad_ref, ret_ref, token_grad_ref, gate_grad_ref):
    n, width = out_grad_ref.shape
    packed = ret_ref.shape[0]
    part = width // 4
    experts = packed // ROWS
    route_row = route_ref[...]
    main, tail, block = (to_column(v) for v in places(route_row))
    routed = to_column(route_row) < experts
    gate = to_column(gate_ref[...])
    row = lax.broadcasted_iota(jnp.int32, (n, packed), 1)
    select = jnp.where(row == main, 1.0, 0.0).astype(BF)
    last = jnp.zeros((n, part), F32)
    for j in range(4):
        cols = pl.ds(j * part, part)
        if j < 3:
            tail_select = jnp.where((row == tail) & (block == j), 1.0, 0.0).astype(BF)
            piece = ret_ref[:, cols]
            rows = dot(select, piece)
            last += dot(tail_select, piece)
        else:
            rows = last
        rows = jnp.where(routed, rows, out_grad_ref[:, cols].astype(F32))
        token_grad_ref[:, cols] = (gate * rows).astype(BF)
    terms = dot(select, ret_ref[:, 3 * part :])[:, :1]
    gate_grad_ref[...] = jnp.where(route_row < experts, to_row(terms), own_term_ref[...]).astype(BF)


def combine(route_row, gate_row, own_term, out_grad, ret):
    n, width = out_grad.shape
    return pl.pallas_call(
        combine_kernel,
        out_shape=(jax.ShapeDtypeStruct((n, width), BF), jax.ShapeDtypeStruct((1, n), BF)),
        compiler_params=pltpu.CompilerParams(vmem_limit_bytes=SMALL_VMEM),
        cost_estimate=pl.CostEstimate(
            flops=2 * ret.shape[0] * n * width * 3 // 2,
            bytes_accessed=2 * (2 * out_grad.size + ret.size),
            transcendentals=0,
        ),
        name="combine",
    )(route_row, gate_row, own_term, out_grad, ret)


def per_device(tokens, out_grad, gate, route, gate_weight, up_weight, down_weight):
    experts = lax.axis_size("expert")
    groups = lax.axis_size("tensor")
    n, width = tokens.shape
    swap = [(0, 1), (1, 0)]
    up = [(i, (i + 1) % groups) for i in range(groups)]
    down = [(i, (i - 1) % groups) for i in range(groups)]
    route_row = route.reshape(1, n)

    core = lax.axis_index("dp").reshape(1)
    weights = (gate_weight[0], up_weight[0], down_weight[0])
    low_half, high_half = weight_parts(core, weights)
    up_low = lax.ppermute(low_half, "tensor", up)
    down_high = lax.ppermute(high_half, "tensor", down)
    up_high = lax.ppermute(high_half, "tensor", up)
    down_low = lax.ppermute(low_half, "tensor", down)

    route_row, low_half = lax.optimization_barrier((route_row, low_half))
    packed = pack(route_row, tokens, out_grad, experts)
    got = lax.all_to_all(
        packed.reshape(experts, ROWS, -1), "expert", split_axis=0, concat_axis=0, tiled=True
    ).reshape(experts * ROWS, -1)

    far_head, far_tail = far_parts(up_low, down_high, ((0, 0, FAR), (1, HALF - FAR, HALF)), FAR_FLOPS[0])
    far_head = lax.ppermute(far_head, "tensor", up)
    far_tail = lax.ppermute(far_tail, "tensor", down)
    up_low, down_high, up_high, down_low = lax.optimization_barrier((up_low, down_high, up_high, down_low))
    far_up, far_down = far_parts(up_low, down_high, ((0, FAR, HALF), (1, 0, HALF - FAR)), FAR_FLOPS[1])
    got, far_up, far_down = lax.optimization_barrier((got, far_up, far_down))
    far_up = lax.ppermute(far_up, "tensor", up)
    far_down = lax.ppermute(far_down, "tensor", down)
    x, dy, far_head, far_tail = lax.optimization_barrier((*unpack(got), far_head, far_tail))
    x_other, dy_other = (lax.ppermute(rows, "dp", swap) for rows in (x, dy))

    part = width // UP_PARTS
    squares = lambda piece: piece.reshape(-1, part, 2 * part)
    blocks = [list(map(squares, b)) for b in ((low_half, high_half), (up_low, up_high), (down_low, down_high))]
    ranges = (HALVES,) * 3
    far = (far_head, far_up, far_down, far_tail)
    far_ranges = ((0, FAR), (FAR, HALF), (HALF, PARTS - FAR), (PARTS - FAR, PARTS))
    own_sums, other_sums, own_terms, other_terms = first_blocks((x, x_other, dy, dy_other), blocks, ranges)
    far = list(map(squares, far))
    other_sums = last_block(x_other, dy_other, far, far_ranges, other_sums, other_terms)
    other_sums = lax.ppermute(other_sums, "dp", swap)
    own_sums = last_block(x, dy, far, far_ranges, own_sums, own_terms)
    back = add_pack(own_sums, other_sums).reshape(experts, ROWS, -1)
    ret = lax.all_to_all(back, "expert", split_axis=0, concat_axis=0, tiled=True)
    own_term = jnp.sum(out_grad.astype(F32) * tokens.astype(F32), axis=1)
    token_grad, gate_grad = combine(
        route_row, gate.reshape(1, n), own_term.reshape(1, n), out_grad, ret.reshape(experts * ROWS, -1)
    )
    return token_grad, gate_grad.reshape(n)


def solution(mesh):
    rows = P(("dp", "expert", "tensor"), None)
    return jax.shard_map(
        per_device,
        mesh=mesh,
        in_specs=(
            rows,
            rows,
            P(("dp", "expert", "tensor")),
            rows,
            P("expert", None, "tensor"),
            P("expert", None, "tensor"),
            P("expert", "tensor", None),
        ),
        out_specs=(rows, P(("dp", "expert", "tensor"))),
        check_vma=False,
    )
```

```python
import functools

import jax
import jax.numpy as jnp
from jax import lax
from jax.experimental import pallas as pl
from jax.experimental.pallas import tpu as pltpu
from jax.sharding import PartitionSpec as P

BF = jnp.bfloat16
F32 = jnp.float32
CAP = 6
ROWS = 8
TERM_LANES = 128
PARTS = 60
UP_PARTS = 40
HALF = 30
FAR = 18
HALVES = ((0, HALF), (HALF, PARTS))
WEIGHT_CUTS = (0, 15, 30, 45, 60)
FAR_FLOPS = (62000000000, 1000)
FIRST_FLOPS = 1000
LAST_FLOPS = 1000
VMEM_ALL = 56 * 1024 * 1024
SMALL_VMEM = 20 * 1024 * 1024
FIRST_VMEM = 38 * 1024 * 1024
LAST_VMEM = 24 * 1024 * 1024


def dot(a, b):
    return jnp.dot(a, b, preferred_element_type=F32)


def dot_t(a, b):
    return lax.dot_general(a, b, (((1,), (1,)), ((), ())), preferred_element_type=F32)


def in_turn(steps):
    def body(i, carry):
        for k, step in enumerate(steps):
            pl.when(i == k)(step)
        return carry

    lax.fori_loop(0, len(steps), body, 0)


def eye(n):
    return lax.broadcasted_iota(jnp.int32, (n, n), 0) == lax.broadcasted_iota(jnp.int32, (n, n), 1)


def to_column(row):
    n = row.shape[1]
    return jnp.sum(jnp.where(eye(n), jnp.broadcast_to(row, (n, n)), 0), axis=1, keepdims=True)


def to_row(column):
    n = column.shape[0]
    return jnp.sum(jnp.where(eye(n), jnp.broadcast_to(column, (n, n)), 0), axis=0, keepdims=True)


def places(route_row):
    n = route_row.shape[1]
    across = jnp.broadcast_to(route_row, (n, n))
    down = jnp.broadcast_to(to_column(route_row), (n, n))
    earlier = lax.broadcasted_iota(jnp.int32, (n, n), 0) < lax.broadcasted_iota(jnp.int32, (n, n), 1)
    slot = jnp.sum(jnp.where((across == down) & earlier, 1, 0), axis=0, keepdims=True)
    second = jnp.where(slot >= 3, 1, 0)
    base = route_row * ROWS
    return base + slot, base + CAP + second, slot - 3 * second


def pack_kernel(route_ref, x_hbm, dy_hbm, out_hbm, rows, out, in_sems, out_sems):
    n, total = route_ref.shape[1], out.shape[0]
    part = rows.shape[2]
    reads = []
    for i, src in enumerate((x_hbm, dy_hbm)):
        for j in range(3):
            k = 3 * i + j
            reads.append(
                [
                    pltpu.make_async_copy(
                        src.at[:, pl.ds(quarter * part, part)], rows.at[k, pl.ds(low, n)], in_sems.at[2 * k + low // n]
                    )
                    for quarter, low in ((j, 0), (3, n))
                ]
            )
            for copy in reads[-1]:
                copy.start()
    main, tail, block = places(route_ref[...])
    row = lax.broadcasted_iota(jnp.int32, (total, n), 0)
    select = jnp.where(row == main, 1.0, 0.0).astype(BF)
    selects = [
        jnp.concatenate([select, jnp.where((row == tail) & (block == j), 1.0, 0.0).astype(BF)], axis=1)
        for j in range(3)
    ]
    writes = []
    for k in range(6):
        for copy in reads[k]:
            copy.wait()
        cols = pl.ds(k * part, part)
        out[:, cols] = dot(selects[k % 3], rows[k]).astype(BF)
        writes.append(pltpu.make_async_copy(out.at[:, cols], out_hbm.at[:, cols], out_sems.at[k]))
        writes[-1].start()
    for write in writes:
        write.wait()


def pack(route_row, x, dy, experts):
    n, width = x.shape
    shape = (experts * ROWS, width // 4 * 6)
    any_spec = pl.BlockSpec(memory_space=pl.ANY)
    return pl.pallas_call(
        pack_kernel,
        out_shape=jax.ShapeDtypeStruct(shape, BF),
        in_specs=[pl.BlockSpec(memory_space=pltpu.VMEM), any_spec, any_spec],
        out_specs=any_spec,
        scratch_shapes=[
            pltpu.VMEM((6, 2 * n, width // 4), BF),
            pltpu.VMEM(shape, BF),
            pltpu.SemaphoreType.DMA((12,)),
            pltpu.SemaphoreType.DMA((6,)),
        ],
        compiler_params=pltpu.CompilerParams(vmem_limit_bytes=VMEM_ALL),
        cost_estimate=pl.CostEstimate(
            flops=2 * experts * ROWS * n * width * 3,
            bytes_accessed=4 * width * (n + experts * CAP),
            transcendentals=0,
        ),
        name="pack",
    )(route_row, x, dy)


def part_copies(weights, core, low, high, out, sem):
    gate, up, down = weights
    hidden, span = out.shape[0] // (high - low), out.shape[1]
    columns = pl.ds(pl.multiple_of(core * hidden, hidden), hidden)
    last_up = min(high, UP_PARTS)
    copies = []
    if low < last_up:
        rows = slice(low * hidden, last_up * hidden)
        for i, ref in enumerate((gate, up)):
            dst = out.at[0 : (last_up - low) * hidden, i * hidden : (i + 1) * hidden]
            copies.append(pltpu.make_async_copy(ref.at[rows, columns], dst, sem))
    for k in range(max(low, UP_PARTS), high):
        src = down.at[columns, (k - UP_PARTS) * span : (k - UP_PARTS + 1) * span]
        dst = out.at[(k - low) * hidden : (k - low + 1) * hidden, :]
        copies.append(pltpu.make_async_copy(src, dst, sem))
    return copies


def weights_kernel(core_ref, gate, up, down, low_half, high_half, held, read_sems, write_sems):
    hidden = held.shape[1] // 2
    reads, waits, writes = [], [], []
    outs = tuple(zip((low_half, high_half), HALVES))
    count = 0
    for i, (low, high) in enumerate(zip(WEIGHT_CUTS, WEIGHT_CUTS[1:])):
        rows = held.at[pl.ds(low * hidden, (high - low) * hidden)]
        reads += part_copies((gate, up, down), core_ref[0], low, high, rows, read_sems.at[i])
        waits.append(pltpu.make_async_copy(rows, rows, read_sems.at[i]))
        writes.append([])
        for out, (first, last) in outs:
            if first <= low and high <= last:
                dst = out.at[pl.ds((low - first) * hidden, (high - low) * hidden)]
                writes[-1].append(pltpu.make_async_copy(rows, dst, write_sems.at[count]))
                count += 1
    for copy in reads:
        copy.start()

    def step(i):
        waits[i].wait()
        for copy in writes[i]:
            copy.start()

    in_turn([functools.partial(step, i) for i in range(len(waits))])
    for copies in writes:
        for copy in copies:
            copy.wait()


def weight_parts(core, weights):
    width, span = weights[0].shape
    hidden = span // 2
    any_spec = pl.BlockSpec(memory_space=pl.ANY)
    size = lambda parts: jax.ShapeDtypeStruct(((parts[1] - parts[0]) * hidden, span), BF)
    return pl.pallas_call(
        weights_kernel,
        out_shape=[size(parts) for parts in HALVES],
        in_specs=[pl.BlockSpec(memory_space=pltpu.SMEM)] + [any_spec] * 3,
        out_specs=[any_spec] * 2,
        scratch_shapes=[
            pltpu.VMEM((PARTS * hidden, span), BF),
            pltpu.SemaphoreType.DMA((len(WEIGHT_CUTS) - 1,)),
            pltpu.SemaphoreType.DMA((2 * len(WEIGHT_CUTS),)),
        ],
        compiler_params=pltpu.CompilerParams(vmem_limit_bytes=VMEM_ALL),
        cost_estimate=pl.CostEstimate(flops=0, bytes_accessed=6 * PARTS * hidden * span, transcendentals=0),
        name="weights",
    )(core, *weights)


def far_kernel(ranges, up_hbm, down_hbm, *refs):
    count = len(ranges)
    outs, held, sems = refs[:count], refs[count : 2 * count], refs[-1]
    reads, writes = [], []
    for i, (side, low, high) in enumerate(ranges):
        hidden = outs[i].shape[0] // (high - low)
        src = (up_hbm, down_hbm)[side].at[low * hidden : high * hidden, :]
        reads.append(pltpu.make_async_copy(src, held[i], sems.at[i]))
        writes.append(pltpu.make_async_copy(held[i], outs[i], sems.at[count + i]))
    for read in reads:
        read.start()
    for read, write in zip(reads, writes):
        read.wait()
        write.start()
    for write in writes:
        write.wait()


def far_parts(from_up, from_down, ranges, flops):
    rows, span = from_up.shape
    hidden = span // 2
    any_spec = pl.BlockSpec(memory_space=pl.ANY)
    return pl.pallas_call(
        functools.partial(far_kernel, ranges),
        out_shape=[jax.ShapeDtypeStruct(((high - low) * hidden, span), BF) for _, low, high in ranges],
        in_specs=[any_spec] * 2,
        out_specs=[any_spec] * len(ranges),
        scratch_shapes=[pltpu.VMEM(((high - low) * hidden, span), BF) for _, low, high in ranges]
        + [pltpu.SemaphoreType.DMA((2 * len(ranges),))],
        compiler_params=pltpu.CompilerParams(vmem_limit_bytes=VMEM_ALL),
        cost_estimate=pl.CostEstimate(flops=flops, bytes_accessed=0, transcendentals=0),
        name="far",
    )(from_up, from_down)


def block_copies(pieces, ranges, gu, down, place, sems):
    hidden, span = pieces[0].shape[1:]
    up_copies, down_copies = [], []
    for i, (piece, (low, high)) in enumerate(zip(pieces, ranges)):
        middle = min(max(low, UP_PARTS), high)
        if low < middle:
            up_copies.append(
                pltpu.make_async_copy(
                    piece.at[pl.ds(0, middle - low)],
                    gu.at[pl.ds(low, middle - low), :, pl.ds(place * span, span)],
                    sems.at[2 * i],
                )
            )
        if middle < high:
            down_copies.append(
                pltpu.make_async_copy(
                    piece.at[pl.ds(middle - low, high - middle)],
                    down.at[pl.ds(middle - UP_PARTS, high - middle), pl.ds(place * hidden, hidden)],
                    sems.at[2 * i + 1],
                )
            )
    return up_copies, down_copies


def slot_matrix(slots, packed, slot_dim, tail):
    shape = (slots, packed) if slot_dim == 0 else (packed, slots)
    slot = lax.broadcasted_iota(jnp.int32, shape, slot_dim)
    row = lax.broadcasted_iota(jnp.int32, shape, 1 - slot_dim)
    group, place = row >> 3, row & 7
    if tail is None:
        hit = (slot == group * CAP + place) & (place < CAP)
    else:
        hit = (slot == group * CAP + (place - CAP) * 3 + tail) & (place >= CAP)
    return jnp.where(hit, 1.0, 0.0).astype(BF)


def hidden_grads(x, dy, gu, down, pre, grads, x_copies, up_copies, dy_copies, down_copies):
    spans, total, span = down.shape
    blocks = len(up_copies)
    hidden = total // blocks
    width = x.shape[1]
    stages = [x_copies + up_copies[0]] + up_copies[1:] + [dy_copies + [c for copies in down_copies for c in copies]]

    def start(i):
        for copy in stages[i] if i < len(stages) else []:
            copy.start()

    def wait(i):
        for copy in stages[i]:
            copy.wait()

    def forward(b):
        wait(b)
        start(b + 2)
        cols = slice(b * span, (b + 1) * span)
        pre[:, cols] = dot(x[...], gu[:, :, cols].reshape(width, span))

    def finish():
        wait(blocks)
        back = dot_t(dy[:, :span], down[0])
        for k in range(1, spans):
            back += dot_t(dy[:, k * span : (k + 1) * span], down[k])
        terms = None
        for b in range(blocks):
            low = b * span
            pre_gate, pre_up = pre[:, low : low + hidden], pre[:, low + hidden : low + span]
            here = back[:, b * hidden : (b + 1) * hidden]
            s = jax.nn.sigmoid(pre_gate)
            activated = pre_gate * s
            slope = s * (1.0 + pre_gate * (1.0 - s))
            grads[:, low : low + hidden] = (here * pre_up * slope).astype(BF)
            grads[:, low + hidden : low + span] = (here * activated).astype(BF)
            term = activated * pre_up * here
            terms = term if terms is None else terms + term
        pre[:, :hidden] = terms

    start(0)
    start(1)
    return [functools.partial(forward, b) for b in range(blocks)] + [finish]


def row_grads(grads, gu, j):
    parts, hidden, columns = gu.shape
    rows = slice(j * parts // 4, (j + 1) * parts // 4)
    return dot_t(grads[...], gu[rows].reshape(parts // 4 * hidden, columns))


def unpack_kernel(rows_hbm, x_ref, dy_ref, rows, sems):
    packed = rows.shape[0]
    slots, width = x_ref.shape
    part = width // 4
    cols = [slice(j * part, (j + 1) * part) for j in range(6)]
    copies = [pltpu.make_async_copy(rows_hbm.at[:, c], rows.at[:, c], sems.at[j]) for j, c in enumerate(cols)]
    for copy in copies:
        copy.start()
    spread = slot_matrix(slots, packed, 0, None)
    spread_tail = [slot_matrix(slots, packed, 0, j) for j in range(3)]
    for k, out_ref in enumerate((x_ref, dy_ref)):
        last = None
        for j in range(3):
            copies[3 * k + j].wait()
            piece = rows[:, cols[3 * k + j]]
            out_ref[:, cols[j]] = dot(spread, piece).astype(BF)
            more = dot(spread_tail[j], piece)
            last = more if last is None else last + more
        out_ref[:, cols[3]] = last.astype(BF)


def unpack(rows):
    packed = rows.shape[0]
    slots, width = packed // ROWS * CAP, rows.shape[1] // 6 * 4
    return pl.pallas_call(
        unpack_kernel,
        out_shape=[jax.ShapeDtypeStruct((slots, width), BF)] * 2,
        in_specs=[pl.BlockSpec(memory_space=pl.ANY)],
        scratch_shapes=[pltpu.VMEM(rows.shape, BF), pltpu.SemaphoreType.DMA((6,))],
        compiler_params=pltpu.CompilerParams(vmem_limit_bytes=SMALL_VMEM),
        cost_estimate=pl.CostEstimate(flops=FIRST_FLOPS, bytes_accessed=FIRST_FLOPS, transcendentals=0),
        name="unpack",
    )(rows)


def first_kernel(ranges, *refs):
    row_refs, refs = refs[:4], refs[4:]
    pieces, refs = refs[: sum(map(len, ranges))], refs[sum(map(len, ranges)) :]
    own_hbm, other_hbm, own_term, other_term, x, dy, gu, down, pre, grads, total, sems = refs
    slots, part = x.shape[0] // 2, x.shape[1] // 4
    row_copies = [
        pltpu.make_async_copy(src, full.at[pl.ds(i * slots, slots)], sems.at[2 * k + i])
        for k, full in enumerate((x, dy))
        for i, src in enumerate(row_refs[2 * k : 2 * k + 2])
    ]
    up_copies, down_copies, used = [], [], 0
    for b, block in enumerate(ranges):
        here = pieces[used : used + len(block)]
        ups, downs = block_copies(here, block, gu, down, b, sems.at[pl.ds(12 + 2 * used, 2 * len(block))])
        used += len(block)
        up_copies.append(ups)
        down_copies.append(downs)
    steps = hidden_grads(x, dy, gu, down, pre, grads, row_copies[:2], up_copies, row_copies[2:], down_copies)
    columns = [pl.ds(j * part, part) for j in range(4)]
    outs = [
        [
            pltpu.make_async_copy(total.at[pl.ds(i * slots, slots), cols], out.at[:, cols], sems.at[4 + 2 * j + i])
            for i, out in enumerate((own_hbm, other_hbm))
        ]
        for j, cols in enumerate(columns)
    ]

    def backward(j):
        total[:, columns[j]] = row_grads(grads, gu, j).astype(BF)
        for copy in outs[j]:
            copy.start()

    in_turn(steps + [functools.partial(backward, j) for j in range(4)])
    hidden = own_term.shape[1]
    own_term[...] = pre[:slots, :hidden]
    other_term[...] = pre[slots:, :hidden]
    for copies in outs:
        for copy in copies:
            copy.wait()


def first_blocks(rows, blocks, ranges):
    slots, width = rows[0].shape
    hidden, span = blocks[0][0].shape[1:]
    count = len(blocks)
    pieces = [piece for block in blocks for piece in block]
    any_spec = pl.BlockSpec(memory_space=pl.ANY)
    vmem_spec = pl.BlockSpec(memory_space=pltpu.VMEM)
    return pl.pallas_call(
        functools.partial(first_kernel, ranges),
        out_shape=[jax.ShapeDtypeStruct((slots, width), BF)] * 2 + [jax.ShapeDtypeStruct((slots, hidden), F32)] * 2,
        in_specs=[any_spec] * (4 + len(pieces)),
        out_specs=[any_spec] * 2 + [vmem_spec] * 2,
        scratch_shapes=[
            pltpu.VMEM((2 * slots, width), BF),
            pltpu.VMEM((2 * slots, width), BF),
            pltpu.VMEM((UP_PARTS, hidden, count * span), BF),
            pltpu.VMEM((PARTS - UP_PARTS, count * hidden, span), BF),
            pltpu.VMEM((2 * slots, count * span), F32),
            pltpu.VMEM((2 * slots, count * span), BF),
            pltpu.VMEM((2 * slots, width), BF),
            pltpu.SemaphoreType.DMA((12 + 2 * len(pieces),)),
        ],
        compiler_params=pltpu.CompilerParams(vmem_limit_bytes=FIRST_VMEM),
        cost_estimate=pl.CostEstimate(flops=FIRST_FLOPS, bytes_accessed=FIRST_FLOPS, transcendentals=0),
        name="first",
    )(*rows, *pieces)


def last_kernel(ranges, *refs):
    x_hbm, dy_hbm, refs = refs[0], refs[1], refs[2:]
    pieces, refs = refs[: len(ranges)], refs[len(ranges) :]
    sum_hbm, term_ref, out_ref, x, dy, gu, down, total, pre, grads, sems = refs
    slots, part = x.shape[0], x.shape[1] // 4
    x_copy = pltpu.make_async_copy(x_hbm, x, sems.at[0])
    dy_copy = pltpu.make_async_copy(dy_hbm, dy, sems.at[1])
    sum_copy = pltpu.make_async_copy(sum_hbm, total, sems.at[2])
    up_copies, down_copies = block_copies(pieces, ranges, gu, down, 0, sems.at[pl.ds(3, 2 * len(ranges))])
    steps = hidden_grads(
        x, dy, gu, down, pre, grads, [x_copy], [up_copies], [dy_copy], [down_copies + [sum_copy]]
    )

    def backward():
        for j in range(4):
            cols = slice(j * part, (j + 1) * part)
            out_ref[:, cols] = (total[:, cols].astype(F32) + row_grads(grads, gu, j)).astype(BF)
        terms = jnp.sum(pre[:, : term_ref.shape[1]] + term_ref[...], axis=1, keepdims=True)
        out_ref[:, 4 * part :] = jnp.broadcast_to(terms, (slots, TERM_LANES)).astype(BF)

    in_turn(steps + [backward])


def last_block(x, dy, pieces, ranges, total, term):
    rows, width = total.shape
    hidden, span = pieces[0].shape[1:]
    any_spec = pl.BlockSpec(memory_space=pl.ANY)
    vmem_spec = pl.BlockSpec(memory_space=pltpu.VMEM)
    return pl.pallas_call(
        functools.partial(last_kernel, ranges),
        out_shape=jax.ShapeDtypeStruct((rows, width + TERM_LANES), BF),
        in_specs=[any_spec] * (len(pieces) + 3) + [vmem_spec],
        out_specs=vmem_spec,
        scratch_shapes=[
            pltpu.VMEM((rows, width), BF),
            pltpu.VMEM((rows, width), BF),
            pltpu.VMEM((UP_PARTS, hidden, span), BF),
            pltpu.VMEM((PARTS - UP_PARTS, hidden, span), BF),
            pltpu.VMEM((rows, width), BF),
            pltpu.VMEM((rows, span), F32),
            pltpu.VMEM((rows, span), BF),
            pltpu.SemaphoreType.DMA((3 + 2 * len(pieces),)),
        ],
        compiler_params=pltpu.CompilerParams(vmem_limit_bytes=LAST_VMEM),
        cost_estimate=pl.CostEstimate(flops=LAST_FLOPS, bytes_accessed=LAST_FLOPS, transcendentals=0),
        name="last",
    )(x, dy, *pieces, total, term)


def add_pack_kernel(a_ref, b_ref, out_ref):
    slots, packed = a_ref.shape[0], out_ref.shape[0]
    part = (a_ref.shape[1] - TERM_LANES) // 4
    gather = slot_matrix(slots, packed, 1, None)
    gather_tail = [slot_matrix(slots, packed, 1, j) for j in range(3)]

    def total(low, size):
        cols = pl.ds(low, size)
        return (a_ref[:, cols].astype(F32) + b_ref[:, cols].astype(F32)).astype(BF)

    out_ref[:, 3 * part :] = dot(gather, total(4 * part, TERM_LANES)).astype(BF)
    last = total(3 * part, part)
    for j in range(3):
        out_ref[:, j * part : (j + 1) * part] = (
            dot(gather, total(j * part, part)) + dot(gather_tail[j], last)
        ).astype(BF)


def add_pack(a, b):
    slots, columns = a.shape
    packed, part = slots // CAP * ROWS, (columns - TERM_LANES) // 4
    return pl.pallas_call(
        add_pack_kernel,
        out_shape=jax.ShapeDtypeStruct((packed, 3 * part + TERM_LANES), BF),
        compiler_params=pltpu.CompilerParams(vmem_limit_bytes=SMALL_VMEM),
        cost_estimate=pl.CostEstimate(
            flops=2 * packed * slots * part * 6, bytes_accessed=6 * slots * columns, transcendentals=0
        ),
        name="add_pack",
    )(a, b)


def combine_kernel(route_ref, gate_ref, own_term_ref, out_grad_ref, ret_ref, token_grad_ref, gate_grad_ref):
    n, width = out_grad_ref.shape
    packed = ret_ref.shape[0]
    part = width // 4
    experts = packed // ROWS
    route_row = route_ref[...]
    main, tail, block = (to_column(v) for v in places(route_row))
    routed = to_column(route_row) < experts
    gate = to_column(gate_ref[...])
    row = lax.broadcasted_iota(jnp.int32, (n, packed), 1)
    select = jnp.where(row == main, 1.0, 0.0).astype(BF)
    last = jnp.zeros((n, part), F32)
    for j in range(4):
        cols = pl.ds(j * part, part)
        if j < 3:
            tail_select = jnp.where((row == tail) & (block == j), 1.0, 0.0).astype(BF)
            piece = ret_ref[:, cols]
            rows = dot(select, piece)
            last += dot(tail_select, piece)
        else:
            rows = last
        rows = jnp.where(routed, rows, out_grad_ref[:, cols].astype(F32))
        token_grad_ref[:, cols] = (gate * rows).astype(BF)
    terms = dot(select, ret_ref[:, 3 * part :])[:, :1]
    gate_grad_ref[...] = jnp.where(route_row < experts, to_row(terms), own_term_ref[...]).astype(BF)


def combine(route_row, gate_row, own_term, out_grad, ret):
    n, width = out_grad.shape
    return pl.pallas_call(
        combine_kernel,
        out_shape=(jax.ShapeDtypeStruct((n, width), BF), jax.ShapeDtypeStruct((1, n), BF)),
        compiler_params=pltpu.CompilerParams(vmem_limit_bytes=SMALL_VMEM),
        cost_estimate=pl.CostEstimate(
            flops=2 * ret.shape[0] * n * width * 3 // 2,
            bytes_accessed=2 * (2 * out_grad.size + ret.size),
            transcendentals=0,
        ),
        name="combine",
    )(route_row, gate_row, own_term, out_grad, ret)


def per_device(tokens, out_grad, gate, route, gate_weight, up_weight, down_weight):
    experts = lax.axis_size("expert")
    groups = lax.axis_size("tensor")
    n, width = tokens.shape
    swap = [(0, 1), (1, 0)]
    up = [(i, (i + 1) % groups) for i in range(groups)]
    down = [(i, (i - 1) % groups) for i in range(groups)]
    route_row = route.reshape(1, n)

    core = lax.axis_index("dp").reshape(1)
    weights = (gate_weight[0], up_weight[0], down_weight[0])
    low_half, high_half = weight_parts(core, weights)
    up_low = lax.ppermute(low_half, "tensor", up)
    down_high = lax.ppermute(high_half, "tensor", down)
    up_high = lax.ppermute(high_half, "tensor", up)
    down_low = lax.ppermute(low_half, "tensor", down)

    route_row, low_half = lax.optimization_barrier((route_row, low_half))
    packed = pack(route_row, tokens, out_grad, experts)
    got = lax.all_to_all(
        packed.reshape(experts, ROWS, -1), "expert", split_axis=0, concat_axis=0, tiled=True
    ).reshape(experts * ROWS, -1)

    far_head, far_tail = far_parts(up_low, down_high, ((0, 0, FAR), (1, HALF - FAR, HALF)), FAR_FLOPS[0])
    far_head = lax.ppermute(far_head, "tensor", up)
    far_tail = lax.ppermute(far_tail, "tensor", down)
    up_low, down_high, up_high, down_low = lax.optimization_barrier((up_low, down_high, up_high, down_low))
    far_up, far_down = far_parts(up_low, down_high, ((0, FAR, HALF), (1, 0, HALF - FAR)), FAR_FLOPS[1])
    got, far_up, far_down = lax.optimization_barrier((got, far_up, far_down))
    far_up = lax.ppermute(far_up, "tensor", up)
    far_down = lax.ppermute(far_down, "tensor", down)
    x, dy, far_head, far_tail = lax.optimization_barrier((*unpack(got), far_head, far_tail))
    x_other, dy_other = (lax.ppermute(rows, "dp", swap) for rows in (x, dy))

    part = width // UP_PARTS
    squares = lambda piece: piece.reshape(-1, part, 2 * part)
    blocks = [list(map(squares, b)) for b in ((low_half, high_half), (up_low, up_high), (down_low, down_high))]
    ranges = (HALVES,) * 3
    far = (far_head, far_up, far_down, far_tail)
    far_ranges = ((0, FAR), (FAR, HALF), (HALF, PARTS - FAR), (PARTS - FAR, PARTS))
    own_sums, other_sums, own_terms, other_terms = first_blocks((x, x_other, dy, dy_other), blocks, ranges)
    far = list(map(squares, far))
    other_sums = last_block(x_other, dy_other, far, far_ranges, other_sums, other_terms)
    other_sums = lax.ppermute(other_sums, "dp", swap)
    own_sums = last_block(x, dy, far, far_ranges, own_sums, own_terms)
    back = add_pack(own_sums, other_sums).reshape(experts, ROWS, -1)
    ret = lax.all_to_all(back, "expert", split_axis=0, concat_axis=0, tiled=True)
    own_term = jnp.sum(out_grad.astype(F32) * tokens.astype(F32), axis=1)
    token_grad, gate_grad = combine(
        route_row, gate.reshape(1, n), own_term.reshape(1, n), out_grad, ret.reshape(experts * ROWS, -1)
    )
    return token_grad, gate_grad.reshape(n)


def solution(mesh):
    rows = P(("dp", "expert", "tensor"), None)
    return jax.shard_map(
        per_device,
        mesh=mesh,
        in_specs=(
            rows,
            rows,
            P(("dp", "expert", "tensor")),
            rows,
            P("expert", None, "tensor"),
            P("expert", None, "tensor"),
            P("expert", "tensor", None),
        ),
        out_specs=(rows, P(("dp", "expert", "tensor"))),
        check_vma=False,
    )
```
